32 devices in a mesh: dp: 16 (over z, x, core), seq: 2 (over y).
Axes of the slice: x: 2, y: 2, z: 4, core: 2. Of those that a mesh axis runs over, the one named last changes fastest.
Arguments:
- row_gene: bfloat16 [16, 1024, 768], P('dp', 'seq'), may hold values from -4 to 4
- row_value: bfloat16 [16, 1024, 768], P('dp', 'seq'), may hold values from -4 to 4
- row_promoter: bfloat16 [16, 1024, 768], P('dp', 'seq'), may hold values from -4 to 4
- row_grn: bfloat16 [16, 1024, 768], P('dp', 'seq'), may hold values from -4 to 4
- row_coexp: bfloat16 [16, 1024, 768], P('dp', 'seq'), may hold values from -4 to 4
- row_family: bfloat16 [16, 1024, 768], P('dp', 'seq'), may hold values from -4 to 4
- lengths: int32 [16], P('dp'), may hold values from 513 to 1024, as said below
- gene_ids: int32 [16, 1024], P('dp', 'seq'), may hold values from 0 to 35999
- norm1_gain: float32 [768], replicated, may hold values from 0.5 to 1.5
- norm1_bias: float32 [768], replicated, may hold values from -1 to 1
- qkv_weight: bfloat16 [768, 2304], replicated, may hold values from -0.3125 to 0.3125
- query_bias: float32 [768], replicated, may hold values from -1 to 1
- value_bias: float32 [768], replicated, may hold values from -1 to 1
- out_weight: bfloat16 [768, 768], replicated, may hold values from -0.4375 to 0.4375
- out_bias: float32 [768], replicated, may hold values from -1 to 1
- norm2_gain: float32 [768], replicated, may hold values from 0.5 to 1.5
- norm2_bias: float32 [768], replicated, may hold values from -1 to 1
- up_weight: bfloat16 [768, 3072], replicated, may hold values from -0.21875 to 0.21875
- up_bias: float32 [3072], replicated, may hold values from -1 to 1
- down_weight: bfloat16 [3072, 768], replicated, may hold values from -0.109375 to 0.109375
- down_bias: float32 [768], replicated, may hold values from -1 to 1
- cotangent: bfloat16 [16, 1024, 768], P('dp', 'seq'), may hold values from -6 to 6
Outputs:
- output: bfloat16 [16, 1024, 768], P('dp', 'seq')
- grad_rows: bfloat16 [16, 1024, 768], P('dp', 'seq')
- attn_grads: float32 [2363392], P(('dp', 'seq'))
- ffn_grads: float32 [4726784], P(('dp', 'seq'))
- gene_counts: int32 [36000], replicated
The draws below stay inside these ranges and needn't reach their ends.
Inputs may be any that keep to these rules, and one draw needn't show every extreme that they name: `lengths`: every cell has more than half of its 1024 slots live, and one cell in every draw is full.
All inputs are finite; a program needn't handle non-finite values.
Results may differ from the reference program's by a relative error of at most 0.013.
Values may be sent and summed in bfloat16 or wider, within the bound.
A program may use at most 256 MiB of HBM per device.

```python
import math
import jax
import jax.numpy as jnp
import numpy as np
from jax import lax

D = 768
HDIM = 64
FF = 3072
VOCAB = 36000
CELL = 1024
CELLS = 16
ATT_PAD = 2363392
FFN_PAD = 4726784


def draw_lengths(key, part):
    key = jax.random.fold_in(key, 7)
    first_key, second_key = jax.random.split(key)
    drawn = jax.random.randint(first_key, (CELLS,), CELL // 2 + 1, CELL + 1)
    chosen = jax.random.randint(second_key, (), 0, CELLS)
    return jnp.where(jnp.arange(CELLS) == chosen, CELL, drawn).astype(jnp.int32)


def set_ends(values, own_key, smallest, largest):
    dims = values.shape
    index_at = [jax.random.randint(jax.random.fold_in(own_key, axis), (), 0, dims[axis]) for axis in range(len(dims))]
    values = values.at[tuple(index_at)].set(smallest)
    longest = dims.index(max(dims))
    index_at[longest] = (index_at[longest] + 1) % dims[longest]
    return values.at[tuple(index_at)].set(largest)


def shard_levels(rng, extent, shards, smallest, largest):
    factor_of, own = 1.0, jax.random.fold_in(rng, 6)
    for position, blocks in shards:
        heights = jnp.exp(jax.random.uniform(jax.random.fold_in(own, position), (blocks,), jnp.float32, smallest / len(shards), largest / len(shards)))
        factor_of = factor_of * jnp.repeat(heights, extent[position] // blocks).reshape([-1 if axis == position else 1 for axis in range(len(extent))])
    return factor_of


def rank_table(number_of, skew):
    portions = [(1 << 20) // math.isqrt(grade ** skew) + 1 for grade in range(1, number_of + 1)]
    deviation = 1 + sum(portions) // (1 << 30)
    return np.cumsum(np.array([max(1, weight // deviation) for weight in portions]))


def ranked(stream_key, dims, amount, skew):
    table = rank_table(amount, skew)
    ticket = jax.random.randint(jax.random.fold_in(stream_key, 1), dims, 0, int(table[amount - 1]))
    grade = jnp.searchsorted(jnp.asarray(table, jnp.int32), ticket, side="right")
    return jax.random.permutation(jax.random.fold_in(stream_key, 2), amount)[grade].astype(jnp.int32)


def scatter_about(own_key, shape, deviation, most, pieces=(), kind=jnp.bfloat16):
    values = jax.random.normal(own_key, shape, jnp.float32) * deviation
    if len(pieces) > 0:
        values = shard_levels(own_key, shape, pieces, -0.22, 0.18) * values
    return jnp.clip(values, min=-most, max=most).astype(kind)


def setup_inputs(seed: int = 0) -> dict:
    key_of = jax.random.split(jax.random.key(seed), 23)
    row_gene = scatter_about(key_of[0], (CELLS, CELL, D), 0.5, 4.0, ((0, 16), (1, 2)))
    row_value = scatter_about(key_of[1], (CELLS, CELL, D), 0.5, 4.0, ((0, 16), (1, 2)))
    row_promoter = scatter_about(key_of[2], (CELLS, CELL, D), 0.5, 4.0, ((0, 16), (1, 2)))
    row_grn = scatter_about(key_of[3], (CELLS, CELL, D), 0.5, 4.0, ((0, 16), (1, 2)))
    row_coexp = scatter_about(key_of[4], (CELLS, CELL, D), 0.5, 4.0, ((0, 16), (1, 2)))
    row_family = scatter_about(key_of[5], (CELLS, CELL, D), 0.5, 4.0, ((0, 16), (1, 2)))
    lengths = draw_lengths(jax.random.fold_in(key_of[22], 71), 0)
    gene_ids = set_ends(ranked(key_of[7], (CELLS, CELL), VOCAB, 2), jax.random.fold_in(key_of[7], 3), 0, VOCAB - 1).astype(jnp.int32)
    norm1_gain = jnp.clip(1.0 + 0.1 * jax.random.normal(key_of[8], (D,), jnp.float32), 0.5, 1.5)
    norm1_bias = scatter_about(key_of[9], (D,), 0.2, 1.0, (), jnp.float32)
    qkv_weight = scatter_about(key_of[10], (D, 3 * D), (D // 2) ** -0.5, 0.3125)
    query_bias = scatter_about(key_of[11], (D,), 0.2, 1.0, (), jnp.float32)
    value_bias = scatter_about(key_of[12], (D,), 0.2, 1.0, (), jnp.float32)
    out_weight = scatter_about(key_of[13], (D, D), (D // 4) ** -0.5, 0.4375)
    out_bias = scatter_about(key_of[14], (D,), 0.2, 1.0, (), jnp.float32)
    norm2_gain = jnp.clip(1.0 + 0.1 * jax.random.normal(key_of[15], (D,), jnp.float32), 0.5, 1.5)
    norm2_bias = scatter_about(key_of[16], (D,), 0.2, 1.0, (), jnp.float32)
    up_weight = scatter_about(key_of[17], (D, FF), D ** -0.5, 0.21875)
    up_bias = scatter_about(key_of[18], (FF,), 0.2, 1.0, (), jnp.float32)
    down_weight = scatter_about(key_of[19], (FF, D), FF ** -0.5, 0.109375)
    down_bias = scatter_about(key_of[20], (D,), 0.2, 1.0, (), jnp.float32)
    cotangent = scatter_about(key_of[21], (CELLS, CELL, D), 1.0, 6.0, ((0, 16), (1, 2)))
    return dict(row_gene=row_gene, row_value=row_value, row_promoter=row_promoter, row_grn=row_grn, row_coexp=row_coexp, row_family=row_family, lengths=lengths, gene_ids=gene_ids, norm1_gain=norm1_gain, norm1_bias=norm1_bias, qkv_weight=qkv_weight, query_bias=query_bias, value_bias=value_bias, out_weight=out_weight, out_bias=out_bias, norm2_gain=norm2_gain, norm2_bias=norm2_bias, up_weight=up_weight, up_bias=up_bias, down_weight=down_weight, down_bias=down_bias, cotangent=cotangent)


EPSILON = 1e-05
NEGATIVE = -1e+30
HIGHEST = lax.Precision.HIGHEST

@jax.custom_vjp
def low(v):
    return lax.optimization_barrier(v.astype(jnp.bfloat16)).astype(jnp.float32)

@jax.custom_vjp
def low_back(v):
    return v

def low_keep(v):
    return (low(v), None)

def low_pass(kept, grad):
    return (grad,)

def back_keep(v):
    return (v, None)

def back_low(kept, grad):
    return (low(grad),)
low.defvjp(low_keep, low_pass)
low_back.defvjp(back_keep, back_low)

def layer_norm(values_in, gain_vec, bias_vec):
    center = values_in - lax.optimization_barrier(jnp.mean(values_in, axis=-1, keepdims=True))
    variance = lax.optimization_barrier(jnp.mean(center * center, axis=-1, keepdims=True))
    return center * lax.rsqrt(variance + EPSILON) * gain_vec + bias_vec

def cell_forward(summed, key_keep, weights):
    norm1_gain, norm1_bias, qkv_weight, query_bias, value_bias, out_weight, out_bias, norm2_gain, norm2_bias, up_weight, up_bias, down_weight, down_bias = weights
    model_width = summed.shape[-1]
    head_count = model_width // HDIM
    length_rows = summed.shape[0]
    normed_in = low(layer_norm(summed, norm1_gain, norm1_bias))
    projected = jnp.dot(normed_in, qkv_weight, precision=HIGHEST)
    queries = low(low_back(projected[:, :model_width] + query_bias))
    key_rows = low(low_back(projected[:, model_width:2 * model_width]))
    value_rows = low(low_back(projected[:, 2 * model_width:] + value_bias))
    scores = jnp.einsum('qhd,khd->hqk', queries.reshape(length_rows, head_count, HDIM), key_rows.reshape(length_rows, head_count, HDIM), precision=HIGHEST) * HDIM ** (-0.5)
    scores = low_back(jnp.where(key_keep[None, None, :], scores, NEGATIVE))
    attn_probs = jax.nn.softmax(scores, axis=-1)
    context = jnp.einsum('hqk,khd->qhd', low(attn_probs), value_rows.reshape(length_rows, head_count, HDIM), precision=HIGHEST).reshape(length_rows, model_width)
    context = low(low_back(context))
    hidden = summed + low_back(jnp.dot(context, out_weight, precision=HIGHEST) + out_bias)
    normed_mid = low(layer_norm(hidden, norm2_gain, norm2_bias))
    inner = low_back(jnp.dot(normed_mid, up_weight, precision=HIGHEST) + up_bias)
    activated = low(jax.nn.gelu(inner, approximate=False))
    return hidden + jnp.dot(activated, down_weight, precision=HIGHEST) + down_bias

def flatten_padded(members, total):
    flat = jnp.concatenate([member.reshape(-1) for member in members])
    return jnp.pad(flat, (0, total - flat.shape[0]))

def reference(row_gene, row_value, row_promoter, row_grn, row_coexp, row_family, lengths, gene_ids, norm1_gain, norm1_bias, qkv_weight, query_bias, value_bias, out_weight, out_bias, norm2_gain, norm2_bias, up_weight, up_bias, down_weight, down_bias, cotangent):
    summed = row_gene.astype(jnp.float32) + row_value.astype(jnp.float32) + row_promoter.astype(jnp.float32) + row_grn.astype(jnp.float32) + row_coexp.astype(jnp.float32) + row_family.astype(jnp.float32)
    weights = tuple((member.astype(jnp.float32) for member in (norm1_gain, norm1_bias, qkv_weight, query_bias, value_bias, out_weight, out_bias, norm2_gain, norm2_bias, up_weight, up_bias, down_weight, down_bias)))
    positions = jnp.arange(CELL, dtype=jnp.int32)
    key_keep = positions[None, :] < lengths[:, None]

    def forward(summed_in, weights_in):

        def per_cell(scan_state, cell_pair):
            return (scan_state, jax.checkpoint(cell_forward)(cell_pair[0], cell_pair[1], weights_in))
        _, result = lax.scan(per_cell, None, (summed_in, key_keep))
        return result
    output, pullback = jax.vjp(forward, summed, weights)
    grad_in, grad_weights = pullback(cotangent.astype(jnp.float32))
    attn_flat = flatten_padded(grad_weights[:7], ATT_PAD)
    ffn_flat = flatten_padded(grad_weights[7:], FFN_PAD)
    counts = jax.ops.segment_sum(key_keep.astype(jnp.int32).reshape(-1), gene_ids.reshape(-1), num_segments=VOCAB)
    return (output.astype(jnp.bfloat16), grad_in.astype(jnp.bfloat16), attn_flat, ffn_flat, counts)
```

```python
import functools
import typing

import jax
import jax.numpy as jnp
from jax import lax
from jax.experimental import pallas as pl
from jax.experimental.pallas import tpu as pltpu
from jax.sharding import PartitionSpec as P

HDIM = 64
VOCAB = 36000
EPSILON = 1e-05
NEGATIVE = -1e30

F32, BF16, I32 = jnp.float32, jnp.bfloat16, jnp.int32
MESH = pl.DeviceIdType.MESH
LOG2E = 1.4426950408889634
LN2 = 0.6931471805599453
HALF = 512
WIDE = 768
NT = (((1,), (1,)), ((), ()))
NN = (((1,), (0,)), ((), ()))


def mm(lhs, rhs, dims=NN):
    return lax.dot_general(lhs, rhs, dims, preferred_element_type=F32)


def when(pred, body):
    if pred is None:
        body()
    else:
        pl.when(pred)(body)


def both(one, other):
    if one is None:
        return other
    if other is None:
        return one
    return jnp.logical_and(one, other)


CORE, X, Y, Z0, Z1, DIAG, NEXT, PREV = range(8)


class Place:
    def __init__(self):
        self.dp = lax.axis_index("dp")
        self.y = lax.axis_index("seq")
        self.core = self.dp % 2
        self.bit = [
            self.core,
            (self.dp // 2) % 2,
            self.y,
            (self.dp // 4) % 2,
            (self.dp // 8) % 2,
        ]
        flip = lambda name, step: self.dp + step - 2 * step * self.bit[name]
        self.index = self.dp * 2 + self.y
        count = 32
        after, before = (self.index + 1) % count, (self.index + count - 1) % count
        self.partner = [
            (flip(CORE, 1), self.y),
            (flip(X, 2), self.y),
            (self.dp, 1 - self.y),
            (flip(Z0, 4), self.y),
            (flip(Z1, 8), self.y),
            (flip(CORE, 1), 1 - self.y),
            (after // 2, after % 2),
            (before // 2, before % 2),
        ]
        self.moves = self.core != self.y
        self.stays = self.core == self.y


def greet(place, names):
    barrier = pltpu.get_barrier_semaphore()
    for name in names:
        pl.semaphore_signal(barrier, inc=1, device_id=place.partner[name], device_id_type=MESH)
    return lambda: pl.semaphore_wait(barrier, len(names))


def remote(src, dst, send_sem, recv_sem, partner):
    return pltpu.make_async_remote_copy(
        src_ref=src,
        dst_ref=dst,
        send_sem=send_sem,
        recv_sem=recv_sem,
        device_id=partner,
        device_id_type=MESH,
    )


def column(length, start, rows):
    return lax.broadcasted_iota(I32, (rows, 1), 0) + start < length


def hat_of(values):
    center = values - jnp.mean(values, axis=-1, keepdims=True)
    inv_std = lax.rsqrt(jnp.mean(center * center, axis=-1, keepdims=True) + EPSILON)
    return center * inv_std, inv_std


def norm_pull(grad, normed, inv_std, gain):
    grad_hat = grad * gain
    return inv_std * (
        grad_hat
        - jnp.mean(grad_hat, axis=-1, keepdims=True)
        - normed * jnp.mean(grad_hat * normed, axis=-1, keepdims=True)
    )


def padded_head(block, odd):
    zero = jnp.zeros((HDIM, block.shape[1]), block.dtype)
    if odd:
        return jnp.concatenate([zero, block], axis=0)
    return jnp.concatenate([block, zero], axis=0)


ROW_CHUNKS = 4
CHUNK = HALF // ROW_CHUNKS


def attend_kernel(
    *refs,
):
    rows_in = refs[:6]
    (cot_in, lens, qkv_in, gain, bias, query_bias, value_bias) = refs[6:13]
    (x_out, a1t_out, q_out, k_out, v_out, ot_out, lse_out, cot_out, len_out) = refs[13:22]
    (
        rows,
        weight,
        x_full,
        x_send,
        x_recv,
        a1,
        a1t,
        q,
        qt,
        k,
        v,
        vt,
        ot,
        len_tile,
        row_sem,
        in_sem,
        out_sem,
        x_sem,
        kv_sem,
        len_sem,
        cot_sem,
    ) = refs[22:]
    place = Place()
    core = place.core
    greeted = greet(place, (CORE, DIAG))

    def rows_at(chunk):
        return pl.ds(chunk * CHUNK, CHUNK)

    loads = [
        [
            pltpu.make_async_copy(
                rows_in[i].at[rows_at(r)], rows.at[i, rows_at(r)], row_sem.at[r, i]
            )
            for i in range(6)
        ]
        for r in range(ROW_CHUNKS)
    ]
    for group in loads:
        for copy in group:
            copy.start()
    load_weight = pltpu.make_async_copy(qkv_in, weight, in_sem)
    load_weight.start()

    len_tile[0] = jnp.full((8, 128), lens[0], I32)
    greeted()
    send_len = remote(
        len_tile.at[0], len_tile.at[1], len_sem.at[0], len_sem.at[1], place.partner[CORE]
    )
    send_len.start()

    swaps = [
        remote(
            x_send.at[rows_at(r)],
            x_recv.at[rows_at(r)],
            x_sem.at[0, r],
            x_sem.at[1, r],
            place.partner[DIAG],
        )
        for r in range(ROW_CHUNKS)
    ]
    for r in range(ROW_CHUNKS):
        for copy in loads[r]:
            copy.wait()
        total = rows[0, rows_at(r)].astype(F32)
        for i in range(1, 6):
            total = total + rows[i, rows_at(r)].astype(F32)
        x_full[rows_at(r)] = total

        @pl.when(place.moves)
        def _():
            x_send[rows_at(r)] = x_full[rows_at(r)].astype(BF16)
            swaps[r].start()

    load_weight.wait()
    send_len.wait()
    length = jnp.where(place.stays, len_tile[0], len_tile[1])
    len_out[...] = length
    length = length[0:1, 0:1]
    start = pl.multiple_of(core * HALF, HALF)

    key_first = None
    sends = []
    for r in range(ROW_CHUNKS):

        @pl.when(place.moves)
        def _():
            swaps[r].wait_recv()
            x_full[rows_at(r)] = x_recv[rows_at(r)].astype(F32)

        normed, _ = hat_of(x_full[rows_at(r)])
        low = (normed * gain[...].reshape(1, WIDE) + bias[...].reshape(1, WIDE)).astype(BF16)
        a1[rows_at(r)] = low
        projected = mm(low, weight[...])
        scaled = (projected[:, :WIDE] + query_bias[...].reshape(1, WIDE)) * (LOG2E * HDIM**-0.5)
        q[rows_at(r)] = scaled.astype(BF16)
        keys = projected[:, WIDE : 2 * WIDE]
        values = projected[:, 2 * WIDE :] + value_bias[...].reshape(1, WIDE)
        if r == 0:
            key_first = keys[0:1]
        live = column(length, start + r * CHUNK, CHUNK)
        own = pl.ds(pl.multiple_of(start + r * CHUNK, CHUNK), CHUNK)
        k[own] = jnp.where(live, keys, key_first).astype(BF16)
        v[own] = jnp.where(live, values, 0.0).astype(BF16)
        for which, ref in enumerate((k, v)):
            copy = remote(
                ref.at[own],
                ref.at[own],
                kv_sem.at[0, which, r],
                kv_sem.at[1, which, r],
                place.partner[CORE],
            )
            copy.start()
            sends.append(copy)

    swap_cot = remote(cot_in, cot_out, cot_sem.at[0], cot_sem.at[1], place.partner[DIAG])

    @pl.when(place.moves)
    def _():
        swap_cot.start()

    qt[...] = q[...].T
    flipped = a1[...].T
    for c in range(2):
        for m in range(6):
            a1t[c, 64 * m : 64 * m + 64] = flipped[128 * m + 64 * c : 128 * m + 64 * c + 64]
    stores = [
        pltpu.make_async_copy(x_full, x_out, out_sem.at[0]),
        pltpu.make_async_copy(a1t, a1t_out, out_sem.at[1]),
        pltpu.make_async_copy(q, q_out, out_sem.at[2]),
    ]
    for copy in stores:
        copy.start()
    for copy in sends:
        copy.wait_recv()
    more = [
        pltpu.make_async_copy(k, k_out, out_sem.at[3]),
        pltpu.make_async_copy(v, v_out, out_sem.at[4]),
    ]
    for copy in more:
        copy.start()

    values_t = v[...].T
    live_row = (lax.broadcasted_iota(I32, (16, 2 * HALF), 1) < length).astype(BF16)
    heads = WIDE // HDIM
    for h in range(heads):
        vt[h, 0:HDIM] = values_t[HDIM * h : HDIM * h + HDIM]
        vt[h, HDIM : HDIM + 16] = live_row

    def score(h):
        return mm(
            k[:, 128 * (h // 2) : 128 * (h // 2) + 128],
            padded_head(qt[HDIM * h : HDIM * h + HDIM], h % 2),
        )

    lse_out[...] = jnp.zeros_like(lse_out)
    scores = score(0)
    for h in range(heads):
        later = score(h + 1) if h + 1 < heads else None
        top = jnp.max(scores, axis=0, keepdims=True)
        probs = jnp.exp2(scores - top).astype(BF16)
        context = mm(vt[h], probs)
        mass = context[HDIM : HDIM + 1]
        ot[HDIM * h : HDIM * h + HDIM] = (context[:HDIM] / mass).astype(BF16)
        lse_out[h : h + 1] = top + jnp.log2(mass)
        scores = later

    last = pltpu.make_async_copy(ot, ot_out, out_sem.at[5])
    last.start()
    for copy in stores + more + [last]:
        copy.wait()
    for copy in sends:
        copy.wait_send()

    @pl.when(place.moves)
    def _():
        for swap in swaps:
            swap.wait_send()
        swap_cot.wait()


def attend_call(rows, cotangent, lengths, qkv_weight, gain, bias, query_bias, value_bias):
    any_spec = pl.BlockSpec(memory_space=pl.ANY)
    vmem = pl.BlockSpec(memory_space=pltpu.VMEM)
    shape = jax.ShapeDtypeStruct
    dma = pltpu.SemaphoreType.DMA
    return pl.pallas_call(
        attend_kernel,
        out_shape=(
            shape((HALF, WIDE), F32),
            shape((2, WIDE // 2, HALF), BF16),
            shape((HALF, WIDE), BF16),
            shape((2 * HALF, WIDE), BF16),
            shape((2 * HALF, WIDE), BF16),
            shape((WIDE, HALF), BF16),
            shape((16, HALF), F32),
            shape((HALF, WIDE), BF16),
            shape((8, 128), I32),
        ),
        in_specs=[any_spec] * 7
        + [pl.BlockSpec(memory_space=pltpu.SMEM), any_spec]
        + [vmem] * 4,
        out_specs=(any_spec,) * 6 + (vmem, any_spec, vmem),
        scratch_shapes=[
            pltpu.VMEM((6, HALF, WIDE), BF16),
            pltpu.VMEM((WIDE, 3 * WIDE), BF16),
            pltpu.VMEM((HALF, WIDE), F32),
            pltpu.VMEM((HALF, WIDE), BF16),
            pltpu.VMEM((HALF, WIDE), BF16),
            pltpu.VMEM((HALF, WIDE), BF16),
            pltpu.VMEM((2, WIDE // 2, HALF), BF16),
            pltpu.VMEM((HALF, WIDE), BF16),
            pltpu.VMEM((WIDE, HALF), BF16),
            pltpu.VMEM((2 * HALF, WIDE), BF16),
            pltpu.VMEM((2 * HALF, WIDE), BF16),
            pltpu.VMEM((WIDE // HDIM, HDIM + 16, 2 * HALF), BF16),
            pltpu.VMEM((WIDE, HALF), BF16),
            pltpu.VMEM((2, 8, 128), I32),
            dma((ROW_CHUNKS, 6)),
            dma,
            dma((6,)),
            dma((2, ROW_CHUNKS)),
            dma((2, 2, ROW_CHUNKS)),
            dma((2,)),
            dma((2,)),
        ],
        compiler_params=pltpu.CompilerParams(
            collective_id=0, has_side_effects=True, vmem_limit_bytes=60 * 2**20
        ),
        name="attend",
    )(*rows, cotangent, lengths, qkv_weight, gain, bias, query_bias, value_bias)


SLOTS = 72
V_GAIN1, V_BIAS1, V_QUERY, V_VALUE, V_OUT, V_GAIN2, V_BIAS2, V_DOWN, V_UP = (
    0, 6, 12, 18, 24, 30, 36, 42, 48,
)
F_BASE, F_ROWS = 64, 1152
A_BASE, A_ROWS = 32, 576


class Part:
    def __init__(self, place, order, fixed, rows, local, landing, sems, finish):
        self.place, self.order, self.fixed, self.rows = place, order, fixed, rows
        self.local, self.landing, self.sems, self.finish = local, landing, sems, finish
        self.first, self.count = 0, 2 ** sum(name not in fixed for name in order)
        self.active, self.step, self.sent = None, 0, []

    @staticmethod
    def landing_blocks(order, fixed):
        count, sizes = 2 ** sum(name not in fixed for name in order), []
        for name in order:
            count = count if name in fixed else count // 2
            sizes.append(count)
        return sizes

    def copy(self, step, start, count):
        return remote(
            self.local.at[pl.ds(start, count)],
            self.landing[step],
            self.sems.at[0, step],
            self.sems.at[1, step],
            self.place.partner[self.order[step]],
        )

    def plan(self):
        name = self.order[self.step]
        mine = self.place.bit[name]
        if name in self.fixed:
            away = both(self.active, mine != self.fixed[name])
            home = both(self.active, mine == self.fixed[name])
            return self.copy(self.step, self.first, self.count), away, home
        half = self.count // 2
        return self.copy(self.step, self.first + (1 - mine) * half, half), self.active, self.active

    def launch(self):
        copy, sends, _ = self.plan()
        when(sends, copy.start)
        self.sent.append((copy, sends))

    def tick(self):
        copy, _, takes = self.plan()
        name = self.order[self.step]
        if name not in self.fixed:
            self.count //= 2
            self.first = self.first + self.place.bit[name] * self.count
        last = self.step == len(self.order) - 1
        kept = self.local.at[pl.ds(self.first, self.count)]
        landed = self.landing[self.step]
        self.active = takes
        self.step += 1
        following = None if last else self.plan()

        def body():
            copy.wait_recv()
            if last:
                self.finish(kept[0].astype(F32) + landed[0].astype(F32))
                return
            kept[...] = kept[...] + landed[...]
            when(
                None
                if following[1] is self.active
                else self.place.bit[self.order[self.step]] != self.fixed[self.order[self.step]],
                following[0].start,
            )

        when(takes, body)
        if not last:
            self.sent.append(following[:2])

    @property
    def done(self):
        return self.step == len(self.order)

    def drain(self):
        for copy, sends in self.sent:
            when(sends, copy.wait_send)


DOWN, UP, OUT, LOW, HIGH = range(5)

ORDERS = {
    (DOWN, 0): (Z0, X, Z1, Y),
    (DOWN, 1): (Y, X, Z0, Z1),
    (DOWN, 2): (Z0, Y, X, Z1),
    (DOWN, 3): (Y, X, Z0, Z1),
    (UP, 0): (Y, X, Z1, Z0),
    (UP, 1): (X, Z0, Z1, Y),
    (UP, 2): (Z0, X, Y, Z1),
    (UP, 3): (X, Y, Z0, Z1),
    (OUT, 0): (Y, Z0, X, Z1),
    (LOW, 0): (X, Z0, Z1, Y),
    (LOW, 1): (Y, X, Z1, Z0),
    (LOW, 2): (X, Z0, Y, Z1),
    (HIGH, 0): (Y, X, Z0, Z1),
    (HIGH, 1): (Z0, X, Y, Z1),
    (HIGH, 2): (X, Z0, Y, Z1),
}


def part_plans():
    plans = {}
    for j in range(4):
        plans[DOWN, j] = (ORDERS[DOWN, j], {Z1: 1, Z0: j // 2, X: j % 2}, 192)
        plans[UP, j] = (ORDERS[UP, j], {Z1: 0}, 48)
    plans[OUT, 0] = (ORDERS[OUT, 0], {Z1: 1, Z0: 1}, 96)
    for p in range(3):
        plans[LOW, p] = (ORDERS[LOW, p], {Z1: 0}, 32)
        plans[HIGH, p] = (ORDERS[HIGH, p], {Z1: 1, Z0: 0}, 32)
    return plans


NORM2, PROJECT, HEADS, QKV, GRADS, NORM1, END = 16, 17, 18, 30, 31, 34, 35
IDS, VEC, COUNT, EDGE = range(4)

SCHEDULE = {
    4: (IDS,),
    6: (IDS,),
    8: (IDS,),
    10: (IDS,),
    11: ((UP, 0),),
    12: (IDS,),
    15: ((UP, 1),),
    17: ((DOWN, 0), (DOWN, 1), (UP, 0),),
    21: ((DOWN, 3),),
    22: ((UP, 3), (DOWN, 2),),
    24: ((UP, 2),),
    25: ((UP, 0),),
    26: ((UP, 1), (DOWN, 1),),
    30: ((UP, 2), (DOWN, 0),),
    32: ((OUT, 0), (UP, 0),),
    33: ((UP, 1), (DOWN, 3),),
    34: ((DOWN, 1), (UP, 3),),
    35: (COUNT, (LOW, 0), (DOWN, 2), (HIGH, 1), (UP, 2), (HIGH, 0), (DOWN, 3), VEC, (LOW, 2), (HIGH, 2), (OUT, 0), (LOW, 1), (UP, 1), (UP, 3), (DOWN, 0), VEC, (UP, 3), (HIGH, 1), (UP, 2), (LOW, 0), (DOWN, 2), (HIGH, 0), (DOWN, 1), VEC, (HIGH, 2), (LOW, 1), (OUT, 0), (LOW, 2), (LOW, 0), (DOWN, 3), (HIGH, 0), VEC, (DOWN, 2), (HIGH, 1), (LOW, 2), (LOW, 0), (HIGH, 2), (LOW, 1), (LOW, 2), VEC, (OUT, 0), (DOWN, 0), EDGE, (HIGH, 0), (HIGH, 1), (HIGH, 2), (LOW, 1),),
}


class Scratch(typing.NamedTuple):
    qkv: typing.Any
    out: typing.Any
    up: typing.Any
    down: typing.Any
    e: typing.Any
    a2: typing.Any
    q: typing.Any
    k: typing.Any
    v: typing.Any
    ot: typing.Any
    ft: typing.Any
    a1t: typing.Any
    a2t: typing.Any
    h: typing.Any
    y: typing.Any
    mid: typing.Any
    dh: typing.Any
    lse: typing.Any
    pair_send: typing.Any
    pair_recv: typing.Any
    flat_f: typing.Any
    flat_a: typing.Any
    vec: typing.Any
    vec_recv: typing.Any
    ids: typing.Any
    down_send: typing.Any
    up_send: typing.Any
    out_send: typing.Any
    qkv_send: typing.Any
    local: typing.Any
    landing: typing.Any
    sems: typing.Any
    load_sem: typing.Any
    core_sem: typing.Any
    pair_sem: typing.Any
    vec_sem: typing.Any
    ids_sem: typing.Any
    edge_sem: typing.Any
    result_sem: typing.Any


def backward_scratch():
    vmem, dma = pltpu.VMEM, pltpu.SemaphoreType.DMA
    low, low_t, full = vmem((HALF, WIDE), BF16), vmem((WIDE, HALF), BF16), vmem((HALF, WIDE), F32)
    plans = part_plans()
    return Scratch(
        qkv=vmem((WIDE, 3 * WIDE), BF16),
        out=vmem((WIDE, WIDE), BF16),
        up=vmem((WIDE, 4 * WIDE), BF16),
        down=vmem((4 * WIDE, WIDE), BF16),
        e=low,
        a2=low,
        q=low,
        k=vmem((2 * HALF, WIDE), BF16),
        v=vmem((2 * HALF, WIDE), BF16),
        ot=low_t,
        ft=low_t,
        a1t=vmem((2, WIDE // 2, HALF), BF16),
        a2t=vmem((2, WIDE // 2, HALF), BF16),
        h=full,
        y=full,
        mid=full,
        dh=full,
        lse=vmem((16, HALF), F32),
        pair_send=vmem((2, 6, HALF, 128), BF16),
        pair_recv=vmem((2, 6, HALF, 128), BF16),
        flat_f=vmem((F_BASE + F_ROWS + 64, 128), F32),
        flat_a=vmem((A_BASE + A_ROWS + 32, 128), F32),
        vec=vmem((6, SLOTS, 128), F32),
        vec_recv=vmem((5, SLOTS, 128), F32),
        ids=vmem((32, 8, 128), I32),
        down_send=vmem((2, 2, 192, WIDE), BF16),
        up_send=vmem((2, 8, 48, WIDE), BF16),
        out_send=vmem((4, 96, WIDE), BF16),
        qkv_send=vmem((2, 12, 32, WIDE), BF16),
        local=[
            [vmem((2, 192, WIDE), BF16)] * 4,
            [vmem((8, 48, WIDE), BF16)] * 4,
            [vmem((4, 96, WIDE), BF16)],
            [vmem((12, 32, WIDE), BF16)] * 3,
        ],
        landing={
            key: [vmem((count, rows, WIDE), BF16) for count in Part.landing_blocks(order, fixed)]
            for key, (order, fixed, rows) in plans.items()
        },
        sems={key: dma((2, 4)) for key in plans},
        load_sem=dma((21,)),
        core_sem=dma((2, 12)),
        pair_sem=dma((2, 2, 6)),
        vec_sem=dma((2, 5)),
        ids_sem=dma((2, 5)),
        edge_sem=dma((2, 4)),
        result_sem=dma((2, 3)),
    )


STAGES = (CORE, X, Y, Z0, Z1)


def backward_kernel(*refs):
    (
        x_in, a1t_in, q_in, k_in, v_in, ot_in, lse_in, e_in, cot_in, qkv_in, out_in, up_in, down_in,
        len_tile, gain1, out_bias, gain2, bias2, up_bias, down_bias, gene_ids, lens,
    ) = refs[:22]
    output_o, rows_o, attn_o, ffn_o, counts_o = refs[22:27]
    s = jax.tree.unflatten(jax.tree.structure(backward_scratch()), refs[27:])
    place = Place()
    core, y_bit = place.core, place.y
    mate = place.partner[CORE]
    greeted = greet(place, range(8))

    own_half = pl.ds(pl.multiple_of(core * HALF, HALF), HALF)
    far_half = pl.ds(pl.multiple_of((1 - core) * HALF, HALF), HALF)
    load_sem = s.load_sem

    def load(n, src, dst):
        copy = pltpu.make_async_copy(src, dst, load_sem.at[n])
        copy.start()
        return copy

    load_out = [load(0, ot_in, s.ot), load(1, out_in, s.out), load(2, x_in, s.h)]
    load_e = [pltpu.make_async_copy(ref, s.e, load_sem.at[3]) for ref in (cot_in, e_in)]
    pl.when(place.stays)(load_e[0].start)
    pl.when(place.moves)(load_e[1].start)
    load_up, load_down = [], []
    for j in range(4):
        cols = pl.ds(WIDE * j, WIDE)
        load_up.append(load(4 + 2 * j, up_in.at[:, cols], s.up.at[:, cols]))
        load_down.append(load(5 + 2 * j, down_in.at[cols], s.down.at[cols]))

    vec = s.vec

    def put_vec(slot, row):
        for t in range(row.shape[1] // 128):
            vec[0, slot + t : slot + t + 1] = row[:, 128 * t : 128 * t + 128]

    def flat_store(ref, base, stride, value):
        for t in range(WIDE // 128):
            ref[pl.ds(base + t, value.shape[0], stride=stride), :] = value[:, 128 * t : 128 * t + 128]

    parts = {}
    for key, (order, fixed, rows) in part_plans().items():
        kind, n = key
        if kind == DOWN:
            local = s.local[DOWN][n]
            finish = functools.partial(flat_store, s.flat_f, F_BASE, 6)
        elif kind == UP:
            local = s.local[UP][n]
            finish = functools.partial(flat_store, s.flat_f, F_BASE + 6 * n, 24)
        elif kind == OUT:
            local = s.local[OUT][0]
            finish = functools.partial(flat_store, s.flat_a, A_BASE, 6)
        else:
            whole = s.local[LOW][n]
            local = whole.at[pl.ds(0, 8)] if kind == LOW else whole.at[pl.ds(8, 4)]
            finish = functools.partial(flat_store, s.flat_a, A_BASE + 6 * n, 18)
        landing = s.landing[key]
        parts[key] = Part(place, order, fixed, rows, local, landing, s.sems[key], finish)

    vec_copies = []

    def vec_launch(stage):
        copy = remote(
            vec.at[stage], s.vec_recv.at[stage], s.vec_sem.at[0, stage], s.vec_sem.at[1, stage],
            place.partner[STAGES[stage]],
        )
        copy.start()
        vec_copies.append(copy)

    def vec_tick():
        n = len(vec_copies) - 1
        vec_copies[-1].wait_recv()
        vec[n + 1] = vec[n] + s.vec_recv[n]
        if n < 4:
            vec_launch(n + 1)

    edges = []

    def edge_launch(ref, base, rows):
        end = base + rows
        for src, dst, size, to in ((end - 24, base - 24, 24, NEXT), (base, end, 32, PREV)):
            n = len(edges)
            copy = remote(
                ref.at[pl.ds(src, size)], ref.at[pl.ds(dst, size)],
                s.edge_sem.at[0, n], s.edge_sem.at[1, n], place.partner[to],
            )
            copy.start()
            edges.append(copy)

    def count(n, total):
        high_row = lax.broadcasted_iota(I32, (288, 128), 0)
        low_row = lax.broadcasted_iota(I32, (128, 128), 0)
        tile = s.ids[n]
        for r in range(0, 4, 2):
            high = [(high_row == (tile[r + i : r + i + 1] >> 7)).astype(F32).astype(BF16) for i in range(2)]
            low = [(low_row == (tile[r + i : r + i + 1] & 127)).astype(F32).astype(BF16) for i in range(2)]
            total = total + mm(jnp.concatenate(high, axis=1), jnp.concatenate(low, axis=1), NT)
        return total

    def count_all():
        counts_o[...] = lax.fori_loop(0, 32, count, jnp.zeros((288, 128), F32)).astype(I32)

    special = {
        IDS: lambda: ids_tick(),
        VEC: vec_tick,
        COUNT: count_all,
        EDGE: lambda: edge_launch(s.flat_f, F_BASE, F_ROWS),
    }

    def pause(hook):
        for entry in SCHEDULE.get(hook, ()):
            if isinstance(entry, tuple):
                parts[entry].tick()
            else:
                special[entry]()

    core_copies = []

    def core_send(src, dst):
        n = len(core_copies)
        copy = remote(src, dst, s.core_sem.at[0, n], s.core_sem.at[1, n], mate)
        copy.start()
        core_copies.append(copy)
        return copy

    def put_blocks(ref, key, value):
        order, fixed, rows = part_plans()[key]
        free = [name for name in order if name not in fixed]
        natural = [name for name in (Z1, Z0, X, Y) if name not in fixed]
        for m in range(2 ** len(free)):
            bits = {name: (m >> (len(natural) - 1 - i)) & 1 for i, name in enumerate(natural)}
            at = sum(bits[name] << (len(free) - 1 - i) for i, name in enumerate(free))
            ref[at] = value[m * rows : m * rows + rows]

    for copy in load_out:
        copy.wait()
    gain2_row, bias2_row = gain2[...].reshape(1, WIDE), bias2[...].reshape(1, WIDE)
    h, y, mid, dh, e = s.h, s.y, s.mid, s.dh, s.e
    h[...] = h[...] + mm(s.ot[...].T, s.out[...]) + out_bias[...].reshape(1, WIDE)
    for r in range(4):
        at = pl.ds(128 * r, 128)
        normed, _ = hat_of(h[at])
        s.a2[at] = (normed * gain2_row + bias2_row).astype(BF16)
        y[at] = h[at] + down_bias[...].reshape(1, WIDE)
    flipped = s.a2[...].T
    for c in range(2):
        for m in range(4):
            s.a2t[c, 96 * m : 96 * m + 96] = flipped[192 * m + 96 * c : 192 * m + 96 * c + 96]

    own_len = jnp.full((1, 128), lens[0], I32)
    slots = lax.broadcasted_iota(I32, (1, 128), 1) + y_bit * HALF
    ids = s.ids
    here = sum(place.bit[name] * 2**stage for stage, name in enumerate(STAGES))
    tile = [
        jnp.where(slots + 128 * r < own_len, gene_ids[0:1, 128 * r : 128 * r + 128], -1) for r in range(4)
    ]
    ids[pl.ds(here, 1)] = jnp.concatenate(tile + [jnp.full((4, 128), -1, I32)], axis=0)[None]
    ids_copies = []

    def ids_launch(stage):
        size = 2**stage
        at = pl.ds((here // size) * size, size)
        copy = remote(
            ids.at[at], ids.at[at], s.ids_sem.at[0, stage], s.ids_sem.at[1, stage],
            place.partner[STAGES[stage]],
        )
        copy.start()
        ids_copies.append(copy)

    def ids_tick():
        ids_copies[-1].wait_recv()
        if len(ids_copies) < 5:
            ids_launch(len(ids_copies))

    greeted()
    ids_launch(0)

    load_e[0].wait()
    put_vec(V_DOWN, jnp.sum(e[...].astype(F32), axis=0, keepdims=True))
    half_rows = WIDE // 2
    theirs = pl.ds(pl.multiple_of((1 - core) * half_rows, half_rows), half_rows)
    ours = pl.ds(pl.multiple_of(core * half_rows, half_rows), half_rows)
    for j in range(4):
        cols = pl.ds(WIDE * j, WIDE)
        load_up[j].wait()
        load_down[j].wait()
        if j == 0:
            load_att = [
                load(12, q_in, s.q),
                load(13, k_in.at[own_half], s.k.at[pl.ds(0, HALF)]),
                load(14, k_in.at[far_half], s.k.at[pl.ds(HALF, HALF)]),
                load(15, v_in.at[own_half], s.v.at[pl.ds(0, HALF)]),
                load(16, v_in.at[far_half], s.v.at[pl.ds(HALF, HALF)]),
                load(17, lse_in, s.lse),
            ]
            load_qkv = [load(18, a1t_in, s.a1t), load(19, qkv_in, s.qkv)]
        inner = mm(s.a2[...], s.up[:, cols]) + up_bias[WIDE * j : WIDE * j + WIDE].reshape(1, WIDE)
        phi = 0.5 * (1.0 + lax.erf(inner * 0.7071067811865476))
        slope = phi + inner * jnp.exp2(inner * inner * (-0.5 * LOG2E)) * 0.3989422804014327
        active = (inner * phi).astype(BF16)
        s.ft[...] = active.T
        if j >= 2:
            core_copies[2 * j - 4].wait_send()
            core_copies[2 * j - 3].wait_send()
        sent = s.down_send.at[j % 2]
        sent[...] = mm(s.ft[theirs], e[...]).astype(BF16).reshape(2, 192, WIDE)
        down_copy = core_send(sent, s.local[DOWN][j])
        pause(4 * j)
        grad = (mm(e[...], s.down[cols], NT) * slope).astype(BF16)
        sent = s.up_send.at[j % 2]
        put_blocks(sent, (UP, j), mm(s.a2t[1 - core], grad).astype(BF16))
        up_copy = core_send(sent, s.local[UP][j])
        pause(4 * j + 1)
        put_vec(V_UP + 6 * j, jnp.sum(grad.astype(F32), axis=0, keepdims=True))
        back = mm(grad, s.up[:, cols], NT)
        mid[...] = back if j == 0 else mid[...] + back
        y[...] = y[...] + mm(active, s.down[cols])
        pause(4 * j + 2)

        own = mm(s.ft[ours], e[...]).reshape(2, 192, WIDE)
        down_copy.wait_recv()
        local = s.local[DOWN][j]
        local[...] = (own + local[...].astype(F32)).astype(BF16)
        parts[DOWN, j].launch()
        own = mm(s.a2t[core], grad)
        up_copy.wait_recv()
        add_blocks(s.local[UP][j], (UP, j), own)
        parts[UP, j].launch()
        pause(4 * j + 3)
    down = s.down
    grad_h, grad_o, grad_q, grad_k, grad_v, grad_rows = [
        down.at[pl.ds(HALF * n, HALF)] for n in range(6)
    ]
    output = s.a2
    sums = [jnp.zeros((1, WIDE), F32) for _ in range(3)]
    for r in range(4):
        at = pl.ds(128 * r, 128)
        output[at] = y[at].astype(BF16)
        normed, inv_std = hat_of(h[at])
        grad = mid[at]
        sums[0] += jnp.sum(grad * normed, axis=0, keepdims=True)
        sums[1] += jnp.sum(grad, axis=0, keepdims=True)
        total = e[at].astype(F32) + norm_pull(grad, normed, inv_std, gain2_row)
        dh[at] = total
        low = total.astype(BF16)
        grad_h[at] = low
        sums[2] += jnp.sum(low.astype(F32), axis=0, keepdims=True)
    put_vec(V_GAIN2, sums[0])
    put_vec(V_BIAS2, sums[1])
    put_vec(V_OUT, sums[2])

    result_copies = []

    def give_back(n, src, dst):
        keep = pltpu.make_async_copy(src, dst, s.result_sem.at[n, 2])
        swap = remote(
            src, dst, s.result_sem.at[n, 0], s.result_sem.at[n, 1], place.partner[DIAG]
        )
        pl.when(place.stays)(keep.start)
        pl.when(place.moves)(swap.start)
        result_copies.append((keep, swap))

    give_back(0, output, output_o)
    pause(NORM2)

    def out_rows(c):
        return jnp.concatenate(
            [s.ot[pl.ds(pl.multiple_of(384 * x + 192 * c, 192), 192)] for x in range(2)], axis=0
        )

    put_blocks(s.out_send, (OUT, 0), mm(out_rows(1 - core), grad_h[...]).astype(BF16))
    out_copy = core_send(s.out_send, s.local[OUT][0])
    grad_o[...] = mm(grad_h[...], s.out[...], NT).astype(BF16)
    own = mm(out_rows(core), grad_h[...])
    out_copy.wait_recv()
    add_blocks(s.local[OUT][0], (OUT, 0), own)
    parts[OUT, 0].launch()
    pause(PROJECT)

    up = s.up
    grad_ot, grad_qt, qt = [up.at[:, pl.ds(HALF * n, HALF)] for n in range(3)]
    grad_ot[...] = grad_o[...].T
    for copy in load_att:
        copy.wait()
    load_x = pltpu.make_async_copy(x_in, y, load_sem.at[20])
    load_x.start()
    qt[...] = s.q[...].T
    length = len_tile[0:1, 0:1]
    live_own = column(length, core * HALF, HALF)
    live_far = column(length, (1 - core) * HALF, HALF)
    live = jnp.concatenate([live_own, live_far], axis=0)
    lane = lax.broadcasted_iota(I32, (1, 128), 1)
    dk, dv = h, mid
    pair_copies = []
    for j in range(WIDE // 128):
        at = slice(128 * j, 128 * j + 128)
        keys, values = s.k[:, at], s.v[:, at]
        keys_t = jnp.where(live, keys, jnp.zeros_like(keys)).T
        grad_keys = grad_values = None
        for i in range(2):
            head = 2 * j + i
            rows = slice(HDIM * head, HDIM * head + HDIM)
            mine = lane // HDIM == i
            scores = mm(keys, padded_head(qt[rows], i))
            probs = jnp.exp2(scores - s.lse[head : head + 1])
            grad_ot_head = grad_ot[rows]
            grad_probs = mm(values, padded_head(grad_ot_head, i))
            delta = jnp.sum(
                grad_ot_head.astype(F32) * s.ot[rows].astype(F32), axis=0, keepdims=True
            )
            grad_scores = (probs * (grad_probs - delta)).astype(BF16)
            queries = jnp.where(mine, s.q[:, at], jnp.zeros((), BF16))
            grad_out = jnp.where(mine, grad_o[:, at], jnp.zeros((), BF16))
            more = mm(probs.astype(BF16), grad_out)
            grad_values = more if i == 0 else grad_values + more
            more = mm(grad_scores, queries)
            grad_keys = more if i == 0 else grad_keys + more
            grad_qt[rows] = (mm(keys_t[HDIM * i : HDIM * i + HDIM], grad_scores) * HDIM**-0.5).astype(BF16)
            if i == 0:
                pause(HEADS + head)
        grad_keys = grad_keys * LN2
        dk[:, at] = grad_keys[:HALF]
        dv[:, at] = grad_values[:HALF]
        for n, value in enumerate((grad_keys, grad_values)):
            s.pair_send[n, j] = value[HALF:].astype(BF16)
            copy = remote(
                s.pair_send.at[n, j], s.pair_recv.at[n, j],
                s.pair_sem.at[0, n, j], s.pair_sem.at[1, n, j], mate,
            )
            copy.start()
            pair_copies.append(copy)
        pause(HEADS + 2 * j + 1)

    grad_q[...] = grad_qt[...].T
    for copy in load_qkv:
        copy.wait()
    for copy in pair_copies:
        copy.wait_recv()
    for j in range(WIDE // 128):
        at = slice(128 * j, 128 * j + 128)
        for n, (mine, out) in enumerate(((dk, grad_k), (dv, grad_v))):
            total = mine[:, at] + s.pair_recv[n, j].astype(F32)
            out[:, at] = jnp.where(live_own, total, 0.0).astype(BF16)
    put_vec(V_QUERY, jnp.sum(grad_q[...].astype(F32), axis=0, keepdims=True))
    put_vec(V_VALUE, jnp.sum(grad_v[...].astype(F32), axis=0, keepdims=True))
    grads = (grad_q, grad_k, grad_v)
    qkv_copies = []
    for p in range(3):
        sent = s.qkv_send.at[p % 2]
        if p == 2:
            qkv_copies[0].wait_send()
        value = mm(s.a1t[1 - core], grads[p][...]).astype(BF16)
        put_blocks(sent.at[pl.ds(0, 8)], (LOW, p), value[:256])
        put_blocks(sent.at[pl.ds(8, 4)], (HIGH, p), value[256:])
        qkv_copies.append(core_send(sent, s.local[LOW][p]))
    pause(QKV)
    for p in range(3):
        own = mm(s.a1t[core], grads[p][...])
        qkv_copies[p].wait_recv()
        local = s.local[LOW][p]
        add_blocks(local.at[pl.ds(0, 8)], (LOW, p), own[:256])
        add_blocks(local.at[pl.ds(8, 4)], (HIGH, p), own[256:])
        parts[LOW, p].launch()
        parts[HIGH, p].launch()
        pause(GRADS + p)

    grad = mm(grad_q[...], s.qkv[:, :WIDE], NT)
    grad = grad + mm(grad_k[...], s.qkv[:, WIDE : 2 * WIDE], NT)
    mid[...] = grad + mm(grad_v[...], s.qkv[:, 2 * WIDE :], NT)
    load_x.wait()
    gain1_row = gain1[...].reshape(1, WIDE)
    sums = [jnp.zeros((1, WIDE), F32) for _ in range(2)]
    for r in range(4):
        at = pl.ds(128 * r, 128)
        normed, inv_std = hat_of(y[at])
        grad = mid[at]
        sums[0] += jnp.sum(grad * normed, axis=0, keepdims=True)
        sums[1] += jnp.sum(grad, axis=0, keepdims=True)
        grad_rows[at] = (dh[at] + norm_pull(grad, normed, inv_std, gain1_row)).astype(BF16)
    put_vec(V_GAIN1, sums[0])
    put_vec(V_BIAS1, sums[1])
    give_back(1, grad_rows, rows_o)
    pause(NORM1)

    vec_launch(0)
    pause(END)
    while any(not part.done for part in parts.values()):
        for part in parts.values():
            if not part.done:
                part.tick()
    edge_launch(s.flat_a, A_BASE, A_ROWS)
    for copy in edges:
        copy.wait()
    total = vec[5]
    flat_f, flat_a = s.flat_f, s.flat_a
    me = place.index
    f_end, a_end = F_BASE + F_ROWS, A_BASE + A_ROWS

    @pl.when(me == 0)
    def _():
        flat_f[F_BASE - 12 : F_BASE] = total[V_GAIN2 : V_GAIN2 + 12]
        flat_a[A_BASE - 12 : A_BASE] = total[V_GAIN1 : V_GAIN1 + 12]

    @pl.when(me == 15)
    def _():
        flat_f[f_end : f_end + 24] = total[V_UP : V_UP + 24]

    @pl.when(me == 16)
    def _():
        flat_f[F_BASE - 24 : F_BASE] = total[V_UP : V_UP + 24]

    @pl.when(me == 23)
    def _():
        flat_a[a_end : a_end + 12] = total[V_QUERY : V_QUERY + 12]

    @pl.when(me == 31)
    def _():
        flat_f[f_end : f_end + 6] = total[V_DOWN : V_DOWN + 6]
        flat_f[f_end + 6 : f_end + 32] = jnp.zeros((26, 128), F32)
        flat_a[a_end : a_end + 6] = total[V_OUT : V_OUT + 6]
        flat_a[a_end + 6 : a_end + 32] = jnp.zeros((26, 128), F32)

    f_start = jnp.where(me < 16, F_BASE - 12 + 2 * me, F_BASE - 4 + 2 * (me - 16))
    a_start = jnp.where(me < 24, A_BASE - 12 + me, A_BASE + me - 24)
    ffn_o[...] = flat_f[pl.ds(f_start, ffn_o.shape[0]), :]
    attn_o[...] = flat_a[pl.ds(a_start, attn_o.shape[0]), :]

    for part in parts.values():
        part.drain()
    core_copies[4].wait_send()
    for n in (5, 6, 7, 8, 10, 11):
        core_copies[n].wait_send()
    for copy in pair_copies + ids_copies + vec_copies:
        copy.wait_send()
    for keep, swap in result_copies:
        pl.when(place.stays)(keep.wait)
        pl.when(place.moves)(swap.wait)


def add_blocks(ref, key, value):
    order, fixed, rows = part_plans()[key]
    free = [name for name in order if name not in fixed]
    natural = [name for name in (Z1, Z0, X, Y) if name not in fixed]
    for m in range(2 ** len(free)):
        bits = {name: (m >> (len(natural) - 1 - i)) & 1 for i, name in enumerate(natural)}
        at = sum(bits[name] << (len(free) - 1 - i) for i, name in enumerate(free))
        ref[at] = (ref[at].astype(F32) + value[m * rows : m * rows + rows]).astype(BF16)


def backward_call(arrays, weights, len_tile, vectors, gene_ids, lengths, attn_units, ffn_units):
    any_spec = pl.BlockSpec(memory_space=pl.ANY)
    vmem = pl.BlockSpec(memory_space=pltpu.VMEM)
    shape = jax.ShapeDtypeStruct
    return pl.pallas_call(
        backward_kernel,
        out_shape=(
            shape((HALF, WIDE), BF16),
            shape((HALF, WIDE), BF16),
            shape((attn_units, 128), F32),
            shape((ffn_units, 128), F32),
            shape((288, 128), I32),
        ),
        in_specs=[any_spec] * 13 + [vmem] * 8 + [pl.BlockSpec(memory_space=pltpu.SMEM)],
        out_specs=(any_spec, any_spec, vmem, vmem, vmem),
        scratch_shapes=jax.tree.leaves(backward_scratch()),
        compiler_params=pltpu.CompilerParams(
            collective_id=1, has_side_effects=True, vmem_limit_bytes=64 * 2**20
        ),
        name="backward",
    )(*arrays, *weights, len_tile, *vectors, gene_ids, lengths)


def on_device(
    row_gene,
    row_value,
    row_promoter,
    row_grn,
    row_coexp,
    row_family,
    lengths,
    gene_ids,
    norm1_gain,
    norm1_bias,
    qkv_weight,
    query_bias,
    value_bias,
    out_weight,
    out_bias,
    norm2_gain,
    norm2_bias,
    up_weight,
    up_bias,
    down_weight,
    down_bias,
    cotangent,
):
    rows = [
        member.reshape(HALF, WIDE)
        for member in (row_gene, row_value, row_promoter, row_grn, row_coexp, row_family)
    ]
    x, a1t, q, k, v, ot, lse, e, len_tile = attend_call(
        rows,
        cotangent.reshape(HALF, WIDE),
        lengths,
        qkv_weight,
        norm1_gain,
        norm1_bias,
        query_bias,
        value_bias,
    )
    devices = lax.axis_size("dp") * lax.axis_size("seq")
    attn_len, ffn_len = gradient_lengths(WIDE, 4 * WIDE, devices)
    output, grad_rows, attn, ffn, counts = backward_call(
        (x, a1t, q, k, v, ot, lse, e, cotangent.reshape(HALF, WIDE)),
        (qkv_weight, out_weight, up_weight, down_weight),
        len_tile,
        (norm1_gain, out_bias, norm2_gain, norm2_bias, up_bias, down_bias),
        gene_ids,
        lengths,
        attn_len // devices // 128,
        ffn_len // devices // 128,
    )
    return (
        output.reshape(row_gene.shape),
        grad_rows.reshape(row_gene.shape),
        attn.reshape(-1),
        ffn.reshape(-1),
        counts.reshape(-1)[:VOCAB],
    )


def gradient_lengths(width, hidden, devices):
    pad = lambda count: -(-count // (devices * 128)) * devices * 128
    return (
        pad(3 * width * width + width * width + 5 * width),
        pad(2 * width * hidden + 3 * width + hidden),
    )


def layer_norm(values_in, gain_vec, bias_vec):
    center = values_in - jnp.mean(values_in, axis=-1, keepdims=True)
    variance = jnp.mean(center * center, axis=-1, keepdims=True)
    inv_std = lax.rsqrt(variance + EPSILON)
    normed = center * inv_std
    return (normed * gain_vec + bias_vec, normed, inv_std)


def norm_back(grad_normed, normed, inv_std, gain_vec):
    grad_hat = grad_normed * gain_vec
    grad_gain = jnp.sum(grad_normed * normed, axis=0)
    grad_bias = jnp.sum(grad_normed, axis=0)
    grad_input = inv_std * (
        grad_hat
        - jnp.mean(grad_hat, axis=-1, keepdims=True)
        - normed * jnp.mean(grad_hat * normed, axis=-1, keepdims=True)
    )
    return (grad_input, grad_gain, grad_bias)


def gelu_exact(inner):
    return jax.nn.gelu(inner, approximate=False)


def padded_flat(members, multiple):
    flat = jnp.concatenate([member.reshape(-1) for member in members])
    total = -(-flat.shape[0] // multiple) * multiple
    return jnp.pad(flat, (0, total - flat.shape[0]))


def attend(queries, key_rows, value_rows, key_keep):
    cell_count, query_len, local_width = queries.shape
    head_count = local_width // HDIM
    block_rows = min(query_len, 512)
    block_count = query_len // block_rows
    scale = HDIM ** (-0.5)

    def one_cell(inputs):
        cell_query, cell_key, cell_value, cell_keep = inputs
        key_heads = cell_key.reshape(-1, head_count, HDIM)
        value_heads = cell_value.reshape(-1, head_count, HDIM)

        def one_block(query_block):
            scores = (
                jnp.einsum(
                    "qhd,khd->hqk", query_block, key_heads, preferred_element_type=jnp.float32
                )
                * scale
            )
            scores = jnp.where(cell_keep[None, None, :], scores, NEGATIVE)
            row_max = jnp.max(scores, axis=-1, keepdims=True)
            exp_scores = jnp.exp(scores - row_max)
            row_total = jnp.sum(exp_scores, axis=-1, keepdims=True)
            attn_probs = exp_scores / row_total
            context = jnp.einsum(
                "hqk,khd->qhd",
                attn_probs.astype(jnp.bfloat16),
                value_heads,
                preferred_element_type=jnp.float32,
            )
            return (
                context.reshape(block_rows, local_width),
                (row_max + jnp.log(row_total))[..., 0],
            )

        context, log_total = lax.map(
            one_block, cell_query.reshape(block_count, block_rows, head_count, HDIM)
        )
        return (context.reshape(query_len, local_width), log_total)

    return lax.map(one_cell, (queries, key_rows, value_rows, key_keep))


def attend_back(queries, key_rows, value_rows, key_keep, log_total, grad_context):
    cell_count, query_len, local_width = queries.shape
    head_count = local_width // HDIM
    block_rows = min(query_len, 512)
    block_count = query_len // block_rows
    scale = HDIM ** (-0.5)

    def one_cell(inputs):
        cell_query, cell_key, cell_value, cell_keep, cell_lse, cell_grad = inputs
        key_heads = cell_key.reshape(-1, head_count, HDIM)
        value_heads = cell_value.reshape(-1, head_count, HDIM)
        key_len = key_heads.shape[0]

        def one_block(running, block_in):
            query_block, lse_block, grad_block = block_in
            scores = (
                jnp.einsum(
                    "qhd,khd->hqk", query_block, key_heads, preferred_element_type=jnp.float32
                )
                * scale
            )
            scores = jnp.where(cell_keep[None, None, :], scores, NEGATIVE)
            attn_probs = jnp.exp(scores - lse_block[..., None])
            grad_probs = jnp.einsum(
                "qhd,khd->hqk", grad_block, value_heads, preferred_element_type=jnp.float32
            )
            grad_scores = (
                attn_probs * (grad_probs - jnp.sum(attn_probs * grad_probs, axis=-1, keepdims=True))
            ).astype(jnp.bfloat16)
            grad_query = (
                jnp.einsum(
                    "hqk,khd->qhd", grad_scores, key_heads, preferred_element_type=jnp.float32
                )
                * scale
            )
            grad_key = (
                running[0]
                + jnp.einsum(
                    "hqk,qhd->khd", grad_scores, query_block, preferred_element_type=jnp.float32
                )
                * scale
            )
            grad_value = running[1] + jnp.einsum(
                "hqk,qhd->khd",
                attn_probs.astype(jnp.bfloat16),
                grad_block,
                preferred_element_type=jnp.float32,
            )
            return ((grad_key, grad_value), grad_query.reshape(block_rows, local_width))

        zeros_start = jnp.zeros((key_len, head_count, HDIM), jnp.float32)
        (grad_key, grad_value), grad_query = lax.scan(
            one_block,
            (zeros_start, zeros_start),
            (
                cell_query.reshape(block_count, block_rows, head_count, HDIM),
                cell_lse,
                cell_grad.reshape(block_count, block_rows, head_count, HDIM),
            ),
        )
        return (
            grad_query.reshape(query_len, local_width),
            grad_key.reshape(key_len, local_width),
            grad_value.reshape(key_len, local_width),
        )

    return lax.map(one_cell, (queries, key_rows, value_rows, key_keep, log_total, grad_context))


def plain_on_device(
    row_gene,
    row_value,
    row_promoter,
    row_grn,
    row_coexp,
    row_family,
    lengths,
    gene_ids,
    norm1_gain,
    norm1_bias,
    qkv_weight,
    query_bias,
    value_bias,
    out_weight,
    out_bias,
    norm2_gain,
    norm2_bias,
    up_weight,
    up_bias,
    down_weight,
    down_bias,
    cotangent,
):
    cell_count, local_len, model_width = row_gene.shape
    row_count = cell_count * local_len
    seq_size = lax.axis_size("seq")
    multiple = lax.axis_size("dp") * seq_size * 128
    place = lax.axis_index("seq")
    positions = place * local_len + jnp.arange(local_len, dtype=jnp.int32)
    live_local = (positions[None, :] < lengths[:, None]).astype(jnp.int32)
    local_counts = jax.ops.segment_sum(
        live_local.reshape(-1), gene_ids.reshape(-1), num_segments=VOCAB
    )
    gene_counts = lax.psum(local_counts, ("dp", "seq"))
    summed = (
        row_gene.astype(jnp.float32)
        + row_value.astype(jnp.float32)
        + row_promoter.astype(jnp.float32)
        + row_grn.astype(jnp.float32)
        + row_coexp.astype(jnp.float32)
        + row_family.astype(jnp.float32)
    )
    summed = summed.reshape(row_count, model_width)
    normed_one, hat_one, inv_one = layer_norm(summed, norm1_gain, norm1_bias)
    normed_in = normed_one.astype(jnp.bfloat16)
    projected = jnp.dot(normed_in, qkv_weight, preferred_element_type=jnp.float32)
    query_full = projected[:, :model_width] + query_bias
    key_full = projected[:, model_width : 2 * model_width]
    value_full = projected[:, 2 * model_width :] + value_bias
    stacked = jnp.stack([query_full, key_full, value_full], axis=1).astype(jnp.bfloat16)
    stacked = stacked.reshape(cell_count, local_len, 3, model_width)
    full_len = local_len * seq_size
    key_keep = jnp.arange(full_len, dtype=jnp.int32)[None, :] < lengths[:, None]
    heads_in = lax.all_to_all(stacked, "seq", split_axis=3, concat_axis=1, tiled=True)
    query_att = heads_in[:, :, 0]
    key_att = heads_in[:, :, 1]
    value_att = heads_in[:, :, 2]
    context, log_total = attend(query_att, key_att, value_att, key_keep)
    context_local = lax.all_to_all(
        context.astype(jnp.bfloat16), "seq", split_axis=1, concat_axis=2, tiled=True
    )
    context_flat = context_local.reshape(row_count, model_width)
    hidden = (
        summed + jnp.dot(context_flat, out_weight, preferred_element_type=jnp.float32) + out_bias
    )
    normed_two, hat_two, inv_two = layer_norm(hidden, norm2_gain, norm2_bias)
    normed_mid = normed_two.astype(jnp.bfloat16)
    inner = jnp.dot(normed_mid, up_weight, preferred_element_type=jnp.float32) + up_bias
    activated, gelu_pull = jax.vjp(gelu_exact, inner)
    activated_low = activated.astype(jnp.bfloat16)
    result = (
        hidden + jnp.dot(activated_low, down_weight, preferred_element_type=jnp.float32) + down_bias
    )
    output = result.astype(jnp.bfloat16).reshape(cell_count, local_len, model_width)
    grad_out_low = cotangent.reshape(row_count, model_width)
    grad_out = grad_out_low.astype(jnp.float32)
    grad_down = jnp.einsum(
        "nf,nd->fd", activated_low, grad_out_low, preferred_element_type=jnp.float32
    )
    grad_down_bias = jnp.sum(grad_out, axis=0)
    grad_act = jnp.einsum(
        "nd,fd->nf", grad_out_low, down_weight, preferred_element_type=jnp.float32
    )
    grad_inner = gelu_pull(grad_act)[0].astype(jnp.bfloat16)
    grad_up = jnp.einsum("nd,nf->df", normed_mid, grad_inner, preferred_element_type=jnp.float32)
    grad_up_bias = jnp.sum(grad_inner.astype(jnp.float32), axis=0)
    grad_mid = jnp.einsum("nf,df->nd", grad_inner, up_weight, preferred_element_type=jnp.float32)
    grad_hid_norm, grad_gain_two, grad_bias_two = norm_back(grad_mid, hat_two, inv_two, norm2_gain)
    grad_hidden = grad_out + grad_hid_norm
    ffn_flat = padded_flat(
        (grad_gain_two, grad_bias_two, grad_up, grad_up_bias, grad_down, grad_down_bias), multiple
    )
    grad_hidden_low = grad_hidden.astype(jnp.bfloat16)
    grad_out_weight = jnp.einsum(
        "nc,nd->cd", context_flat, grad_hidden_low, preferred_element_type=jnp.float32
    )
    grad_out_bias = jnp.sum(grad_hidden_low.astype(jnp.float32), axis=0)
    grad_context = jnp.einsum(
        "nd,cd->nc", grad_hidden_low, out_weight, preferred_element_type=jnp.float32
    )
    grad_context = grad_context.astype(jnp.bfloat16).reshape(cell_count, local_len, model_width)
    grad_heads = lax.all_to_all(grad_context, "seq", split_axis=2, concat_axis=1, tiled=True)
    grad_query, grad_key, grad_value = attend_back(
        query_att, key_att, value_att, key_keep, log_total, grad_heads
    )
    grad_stack = jnp.stack([grad_query, grad_key, grad_value], axis=2).astype(jnp.bfloat16)
    grad_local = lax.all_to_all(grad_stack, "seq", split_axis=1, concat_axis=3, tiled=True)
    grad_qkv = grad_local.reshape(row_count, 3 * model_width)
    grad_qkv_weight = jnp.einsum(
        "nd,ne->de", normed_in, grad_qkv, preferred_element_type=jnp.float32
    )
    grad_query_bias = jnp.sum(grad_qkv[:, :model_width].astype(jnp.float32), axis=0)
    grad_value_bias = jnp.sum(grad_qkv[:, 2 * model_width :].astype(jnp.float32), axis=0)
    grad_normed_in = jnp.einsum(
        "ne,de->nd", grad_qkv, qkv_weight, preferred_element_type=jnp.float32
    )
    grad_sum_norm, grad_gain_one, grad_bias_one = norm_back(
        grad_normed_in, hat_one, inv_one, norm1_gain
    )
    grad_rows = (
        (grad_hidden + grad_sum_norm)
        .astype(jnp.bfloat16)
        .reshape(cell_count, local_len, model_width)
    )
    attn_flat = padded_flat(
        (
            grad_gain_one,
            grad_bias_one,
            grad_qkv_weight,
            grad_query_bias,
            grad_value_bias,
            grad_out_weight,
            grad_out_bias,
        ),
        multiple,
    )
    attn_share, ffn_share = (
        lax.psum_scatter(attn_flat, ("dp", "seq"), scatter_dimension=0, tiled=True),
        lax.psum_scatter(ffn_flat, ("dp", "seq"), scatter_dimension=0, tiled=True),
    )
    return (output, grad_rows, attn_share, ffn_share, gene_counts)


def fits(mesh):
    return dict(mesh.shape) == {"dp": 16, "seq": 2}


def solution(mesh):
    return jax.shard_map(
        on_device if fits(mesh) else plain_on_device,
        mesh=mesh,
        in_specs=(
            P("dp", "seq", None),
            P("dp", "seq", None),
            P("dp", "seq", None),
            P("dp", "seq", None),
            P("dp", "seq", None),
            P("dp", "seq", None),
            P("dp"),
            P("dp", "seq"),
            P(),
            P(),
            P(),
            P(),
            P(),
            P(),
            P(),
            P(),
            P(),
            P(),
            P(),
            P(),
            P(),
            P("dp", "seq", None),
        ),
        out_specs=(
            P("dp", "seq", None),
            P("dp", "seq", None),
            P(("dp", "seq")),
            P(("dp", "seq")),
            P(),
        ),
        check_vma=False,
    )
```

```python
import functools
import typing

import jax
import jax.numpy as jnp
from jax import lax
from jax.experimental import pallas as pl
from jax.experimental.pallas import tpu as pltpu
from jax.sharding import PartitionSpec as P

HDIM = 64
VOCAB = 36000
EPSILON = 1e-05
NEGATIVE = -1e30

F32, BF16, I32 = jnp.float32, jnp.bfloat16, jnp.int32
MESH = pl.DeviceIdType.MESH
LOG2E = 1.4426950408889634
LN2 = 0.6931471805599453
HALF = 512
WIDE = 768
NT = (((1,), (1,)), ((), ()))
NN = (((1,), (0,)), ((), ()))


def mm(lhs, rhs, dims=NN):
    return lax.dot_general(lhs, rhs, dims, preferred_element_type=F32)


def when(pred, body):
    if pred is None:
        body()
    else:
        pl.when(pred)(body)


def both(one, other):
    if one is None:
        return other
    if other is None:
        return one
    return jnp.logical_and(one, other)


CORE, X, Y, Z0, Z1, DIAG, NEXT, PREV = range(8)


class Place:
    def __init__(self):
        self.dp = lax.axis_index("dp")
        self.y = lax.axis_index("seq")
        self.core = self.dp % 2
        self.bit = [
            self.core,
            (self.dp // 2) % 2,
            self.y,
            (self.dp // 4) % 2,
            (self.dp // 8) % 2,
        ]
        flip = lambda name, step: self.dp + step - 2 * step * self.bit[name]
        self.index = self.dp * 2 + self.y
        count = 32
        after, before = (self.index + 1) % count, (self.index + count - 1) % count
        self.partner = [
            (flip(CORE, 1), self.y),
            (flip(X, 2), self.y),
            (self.dp, 1 - self.y),
            (flip(Z0, 4), self.y),
            (flip(Z1, 8), self.y),
            (flip(CORE, 1), 1 - self.y),
            (after // 2, after % 2),
            (before // 2, before % 2),
        ]
        self.moves = self.core != self.y
        self.stays = self.core == self.y


def greet(place, names):
    barrier = pltpu.get_barrier_semaphore()
    for name in names:
        pl.semaphore_signal(barrier, inc=1, device_id=place.partner[name], device_id_type=MESH)
    return lambda: pl.semaphore_wait(barrier, len(names))


def remote(src, dst, send_sem, recv_sem, partner):
    return pltpu.make_async_remote_copy(
        src_ref=src,
        dst_ref=dst,
        send_sem=send_sem,
        recv_sem=recv_sem,
        device_id=partner,
        device_id_type=MESH,
    )


def column(length, start, rows):
    return lax.broadcasted_iota(I32, (rows, 1), 0) + start < length


def hat_of(values):
    center = values - jnp.mean(values, axis=-1, keepdims=True)
    inv_std = lax.rsqrt(jnp.mean(center * center, axis=-1, keepdims=True) + EPSILON)
    return center * inv_std, inv_std


def norm_pull(grad, normed, inv_std, gain):
    grad_hat = grad * gain
    return inv_std * (
        grad_hat
        - jnp.mean(grad_hat, axis=-1, keepdims=True)
        - normed * jnp.mean(grad_hat * normed, axis=-1, keepdims=True)
    )


def padded_head(block, odd):
    zero = jnp.zeros((HDIM, block.shape[1]), block.dtype)
    if odd:
        return jnp.concatenate([zero, block], axis=0)
    return jnp.concatenate([block, zero], axis=0)


ROW_CHUNKS = 4
CHUNK = HALF // ROW_CHUNKS


def attend_kernel(
    *refs,
):
    rows_in = refs[:6]
    (cot_in, lens, qkv_in, gain, bias, query_bias, value_bias) = refs[6:13]
    (x_out, a1t_out, q_out, k_out, v_out, ot_out, lse_out, cot_out, len_out) = refs[13:22]
    (
        rows,
        weight,
        x_full,
        x_send,
        x_recv,
        a1,
        a1t,
        q,
        qt,
        k,
        v,
        vt,
        ot,
        len_tile,
        row_sem,
        in_sem,
        out_sem,
        x_sem,
        kv_sem,
        len_sem,
        cot_sem,
    ) = refs[22:]
    place = Place()
    core = place.core
    greeted = greet(place, (CORE, DIAG))

    def rows_at(chunk):
        return pl.ds(chunk * CHUNK, CHUNK)

    loads = [
        [
            pltpu.make_async_copy(
                rows_in[i].at[rows_at(r)], rows.at[i, rows_at(r)], row_sem.at[r, i]
            )
            for i in range(6)
        ]
        for r in range(ROW_CHUNKS)
    ]
    for group in loads:
        for copy in group:
            copy.start()
    load_weight = pltpu.make_async_copy(qkv_in, weight, in_sem)
    load_weight.start()

    len_tile[0] = jnp.full((8, 128), lens[0], I32)
    greeted()
    send_len = remote(
        len_tile.at[0], len_tile.at[1], len_sem.at[0], len_sem.at[1], place.partner[CORE]
    )
    send_len.start()

    swaps = [
        remote(
            x_send.at[rows_at(r)],
            x_recv.at[rows_at(r)],
            x_sem.at[0, r],
            x_sem.at[1, r],
            place.partner[DIAG],
        )
        for r in range(ROW_CHUNKS)
    ]
    for r in range(ROW_CHUNKS):
        for copy in loads[r]:
            copy.wait()
        total = rows[0, rows_at(r)].astype(F32)
        for i in range(1, 6):
            total = total + rows[i, rows_at(r)].astype(F32)
        x_full[rows_at(r)] = total

        @pl.when(place.moves)
        def _():
            x_send[rows_at(r)] = x_full[rows_at(r)].astype(BF16)
            swaps[r].start()

    load_weight.wait()
    send_len.wait()
    length = jnp.where(place.stays, len_tile[0], len_tile[1])
    len_out[...] = length
    length = length[0:1, 0:1]
    start = pl.multiple_of(core * HALF, HALF)

    key_first = None
    sends = []
    for r in range(ROW_CHUNKS):

        @pl.when(place.moves)
        def _():
            swaps[r].wait_recv()
            x_full[rows_at(r)] = x_recv[rows_at(r)].astype(F32)

        normed, _ = hat_of(x_full[rows_at(r)])
        low = (normed * gain[...].reshape(1, WIDE) + bias[...].reshape(1, WIDE)).astype(BF16)
        a1[rows_at(r)] = low
        projected = mm(low, weight[...])
        scaled = (projected[:, :WIDE] + query_bias[...].reshape(1, WIDE)) * (LOG2E * HDIM**-0.5)
        q[rows_at(r)] = scaled.astype(BF16)
        keys = projected[:, WIDE : 2 * WIDE]
        values = projected[:, 2 * WIDE :] + value_bias[...].reshape(1, WIDE)
        if r == 0:
            key_first = keys[0:1]
        live = column(length, start + r * CHUNK, CHUNK)
        own = pl.ds(pl.multiple_of(start + r * CHUNK, CHUNK), CHUNK)
        k[own] = jnp.where(live, keys, key_first).astype(BF16)
        v[own] = jnp.where(live, values, 0.0).astype(BF16)
        for which, ref in enumerate((k, v)):
            copy = remote(
                ref.at[own],
                ref.at[own],
                kv_sem.at[0, which, r],
                kv_sem.at[1, which, r],
                place.partner[CORE],
            )
            copy.start()
            sends.append(copy)

    swap_cot = remote(cot_in, cot_out, cot_sem.at[0], cot_sem.at[1], place.partner[DIAG])

    @pl.when(place.moves)
    def _():
        swap_cot.start()

    qt[...] = q[...].T
    flipped = a1[...].T
    for c in range(2):
        for m in range(6):
            a1t[c, 64 * m : 64 * m + 64] = flipped[128 * m + 64 * c : 128 * m + 64 * c + 64]
    stores = [
        pltpu.make_async_copy(x_full, x_out, out_sem.at[0]),
        pltpu.make_async_copy(a1t, a1t_out, out_sem.at[1]),
        pltpu.make_async_copy(q, q_out, out_sem.at[2]),
    ]
    for copy in stores:
        copy.start()
    for copy in sends:
        copy.wait_recv()
    more = [
        pltpu.make_async_copy(k, k_out, out_sem.at[3]),
        pltpu.make_async_copy(v, v_out, out_sem.at[4]),
    ]
    for copy in more:
        copy.start()

    values_t = v[...].T
    live_row = (lax.broadcasted_iota(I32, (16, 2 * HALF), 1) < length).astype(BF16)
    heads = WIDE // HDIM
    for h in range(heads):
        vt[h, 0:HDIM] = values_t[HDIM * h : HDIM * h + HDIM]
        vt[h, HDIM : HDIM + 16] = live_row

    def score(h):
        return mm(
            k[:, 128 * (h // 2) : 128 * (h // 2) + 128],
            padded_head(qt[HDIM * h : HDIM * h + HDIM], h % 2),
        )

    lse_out[...] = jnp.zeros_like(lse_out)
    scores = score(0)
    for h in range(heads):
        later = score(h + 1) if h + 1 < heads else None
        top = jnp.max(scores, axis=0, keepdims=True)
        probs = jnp.exp2(scores - top).astype(BF16)
        context = mm(vt[h], probs)
        mass = context[HDIM : HDIM + 1]
        ot[HDIM * h : HDIM * h + HDIM] = (context[:HDIM] / mass).astype(BF16)
        lse_out[h : h + 1] = top + jnp.log2(mass)
        scores = later

    last = pltpu.make_async_copy(ot, ot_out, out_sem.at[5])
    last.start()
    for copy in stores + more + [last]:
        copy.wait()
    for copy in sends:
        copy.wait_send()

    @pl.when(place.moves)
    def _():
        for swap in swaps:
            swap.wait_send()
        swap_cot.wait()


def attend_call(rows, cotangent, lengths, qkv_weight, gain, bias, query_bias, value_bias):
    any_spec = pl.BlockSpec(memory_space=pl.ANY)
    vmem = pl.BlockSpec(memory_space=pltpu.VMEM)
    shape = jax.ShapeDtypeStruct
    dma = pltpu.SemaphoreType.DMA
    return pl.pallas_call(
        attend_kernel,
        out_shape=(
            shape((HALF, WIDE), F32),
            shape((2, WIDE // 2, HALF), BF16),
            shape((HALF, WIDE), BF16),
            shape((2 * HALF, WIDE), BF16),
            shape((2 * HALF, WIDE), BF16),
            shape((WIDE, HALF), BF16),
            shape((16, HALF), F32),
            shape((HALF, WIDE), BF16),
            shape((8, 128), I32),
        ),
        in_specs=[any_spec] * 7
        + [pl.BlockSpec(memory_space=pltpu.SMEM), any_spec]
        + [vmem] * 4,
        out_specs=(any_spec,) * 6 + (vmem, any_spec, vmem),
        scratch_shapes=[
            pltpu.VMEM((6, HALF, WIDE), BF16),
            pltpu.VMEM((WIDE, 3 * WIDE), BF16),
            pltpu.VMEM((HALF, WIDE), F32),
            pltpu.VMEM((HALF, WIDE), BF16),
            pltpu.VMEM((HALF, WIDE), BF16),
            pltpu.VMEM((HALF, WIDE), BF16),
            pltpu.VMEM((2, WIDE // 2, HALF), BF16),
            pltpu.VMEM((HALF, WIDE), BF16),
            pltpu.VMEM((WIDE, HALF), BF16),
            pltpu.VMEM((2 * HALF, WIDE), BF16),
            pltpu.VMEM((2 * HALF, WIDE), BF16),
            pltpu.VMEM((WIDE // HDIM, HDIM + 16, 2 * HALF), BF16),
            pltpu.VMEM((WIDE, HALF), BF16),
            pltpu.VMEM((2, 8, 128), I32),
            dma((ROW_CHUNKS, 6)),
            dma,
            dma((6,)),
            dma((2, ROW_CHUNKS)),
            dma((2, 2, ROW_CHUNKS)),
            dma((2,)),
            dma((2,)),
        ],
        compiler_params=pltpu.CompilerParams(
            collective_id=0, has_side_effects=True, vmem_limit_bytes=60 * 2**20
        ),
        name="attend",
    )(*rows, cotangent, lengths, qkv_weight, gain, bias, query_bias, value_bias)


SLOTS = 72
V_EARLY = 48
V_UP, V_DOWN, V_GAIN2, V_BIAS2, V_OUT, V_GAIN1, V_BIAS1, V_QUERY, V_VALUE = (
    0, 24, 30, 36, 42, 48, 54, 60, 66,
)
F_BASE, F_ROWS = 64, 1152
A_BASE, A_ROWS = 32, 576


class Part:
    def __init__(self, place, order, fixed, rows, local, landing, sems, finish):
        self.place, self.order, self.fixed, self.rows = place, order, fixed, rows
        self.local, self.landing, self.sems, self.finish = local, landing, sems, finish
        self.first, self.count = 0, 2 ** sum(name not in fixed for name in order)
        self.active, self.step, self.sent = None, 0, []

    @staticmethod
    def landing_blocks(order, fixed):
        count, sizes = 2 ** sum(name not in fixed for name in order), []
        for name in order:
            count = count if name in fixed else count // 2
            sizes.append(count)
        return sizes

    def copy(self, step, start, count):
        return remote(
            self.local.at[pl.ds(start, count)],
            self.landing[step],
            self.sems.at[0, step],
            self.sems.at[1, step],
            self.place.partner[self.order[step]],
        )

    def plan(self):
        name = self.order[self.step]
        mine = self.place.bit[name]
        if name in self.fixed:
            away = both(self.active, mine != self.fixed[name])
            home = both(self.active, mine == self.fixed[name])
            return self.copy(self.step, self.first, self.count), away, home
        half = self.count // 2
        return self.copy(self.step, self.first + (1 - mine) * half, half), self.active, self.active

    def launch(self):
        copy, sends, _ = self.plan()
        when(sends, copy.start)
        self.sent.append((copy, sends))

    def tick(self):
        copy, _, takes = self.plan()
        name = self.order[self.step]
        if name not in self.fixed:
            self.count //= 2
            self.first = self.first + self.place.bit[name] * self.count
        last = self.step == len(self.order) - 1
        kept = self.local.at[pl.ds(self.first, self.count)]
        landed = self.landing[self.step]
        self.active = takes
        self.step += 1
        following = None if last else self.plan()

        def body():
            copy.wait_recv()
            if last:
                self.finish(kept[0].astype(F32) + landed[0].astype(F32))
                return
            kept[...] = kept[...] + landed[...]
            when(
                None
                if following[1] is self.active
                else self.place.bit[self.order[self.step]] != self.fixed[self.order[self.step]],
                following[0].start,
            )

        when(takes, body)
        if not last:
            self.sent.append(following[:2])

    @property
    def done(self):
        return self.step == len(self.order)

    def drain(self):
        for copy, sends in self.sent:
            when(sends, copy.wait_send)


DOWN, UP, OUT, LOW, HIGH = range(5)

ORDERS = {
    (DOWN, 0): (Y, Z0, X, Z1),
    (DOWN, 1): (Z0, X, Y, Z1),
    (DOWN, 2): (Z0, X, Y, Z1),
    (DOWN, 3): (X, Y, Z0, Z1),
    (UP, 0): (X, Z0, Y, Z1),
    (UP, 1): (X, Z0, Z1, Y),
    (UP, 2): (Y, Z0, X, Z1),
    (UP, 3): (Z0, X, Y, Z1),
    (OUT, 0): (X, Y, Z1, Z0),
    (LOW, 0): (Y, Z1, Z0, X),
    (LOW, 1): (Y, X, Z0, Z1),
    (LOW, 2): (X, Z0, Y, Z1),
    (HIGH, 0): (X, Z1, Y, Z0),
    (HIGH, 1): (Z0, Y, X, Z1),
    (HIGH, 2): (X, Z1, Y, Z0),
}


def part_plans():
    plans = {}
    for j in range(4):
        plans[DOWN, j] = (ORDERS[DOWN, j], {Z1: 1, Z0: j // 2, X: j % 2}, 192)
        plans[UP, j] = (ORDERS[UP, j], {Z1: 0}, 48)
    plans[OUT, 0] = (ORDERS[OUT, 0], {Z1: 1, Z0: 1}, 96)
    for p in range(3):
        plans[LOW, p] = (ORDERS[LOW, p], {Z1: 0}, 32)
        plans[HIGH, p] = (ORDERS[HIGH, p], {Z1: 1, Z0: 0}, 32)
    return plans


NORM2, PROJECT, PAIRS, QKV, NORM1, END = 16, 17, 18, 24, 25, 26
IDS, VEC, LATE, COUNT, EDGE = range(5)

SCHEDULE = {
    0: (IDS,),
    4: (IDS,),
    13: (IDS,),
    14: ((DOWN, 0),),
    18: (IDS,),
    19: (VEC, (DOWN, 3), (DOWN, 1), (DOWN, 2),),
    20: ((DOWN, 0), (UP, 0), IDS, (OUT, 0), (UP, 2), VEC,),
    22: ((OUT, 0), (UP, 1), VEC,),
    25: (VEC,),
    26: ((HIGH, 0), (DOWN, 3), (LOW, 0), (DOWN, 2), COUNT, (UP, 2), (LOW, 1), (HIGH, 2), (DOWN, 2), (DOWN, 3), (DOWN, 1), LATE, (UP, 3), (HIGH, 0), (UP, 1), (HIGH, 1), (LOW, 0), (UP, 2), (UP, 3), (HIGH, 2), (LOW, 1), (HIGH, 1), (UP, 0), (LOW, 2), LATE, (UP, 3), (DOWN, 1), (UP, 1), (LOW, 0), (DOWN, 0), (HIGH, 1), (HIGH, 0), (UP, 2), (OUT, 0), (LOW, 2), (UP, 0), LATE, (DOWN, 2), (UP, 1), (UP, 0), (DOWN, 3), (HIGH, 0), (LOW, 2), (HIGH, 2), (DOWN, 1), (LOW, 1), LATE, (DOWN, 0), (LOW, 2), (OUT, 0), (UP, 3), (HIGH, 2), EDGE, VEC, (LOW, 0), (LOW, 1), LATE, (HIGH, 1),),
}


class Scratch(typing.NamedTuple):
    qkv: typing.Any
    out: typing.Any
    up: typing.Any
    down: typing.Any
    e: typing.Any
    a2: typing.Any
    q: typing.Any
    k: typing.Any
    v: typing.Any
    ot: typing.Any
    ft: typing.Any
    a1t: typing.Any
    a2t: typing.Any
    h: typing.Any
    y: typing.Any
    mid: typing.Any
    dh: typing.Any
    lse: typing.Any
    pair_send: typing.Any
    pair_recv: typing.Any
    flat_f: typing.Any
    flat_a: typing.Any
    vec: typing.Any
    vec_recv: typing.Any
    ids: typing.Any
    down_send: typing.Any
    up_send: typing.Any
    out_send: typing.Any
    qkv_send: typing.Any
    local: typing.Any
    landing: typing.Any
    sems: typing.Any
    load_sem: typing.Any
    core_sem: typing.Any
    pair_sem: typing.Any
    vec_sem: typing.Any
    ids_sem: typing.Any
    edge_sem: typing.Any
    result_sem: typing.Any


def backward_scratch():
    vmem, dma = pltpu.VMEM, pltpu.SemaphoreType.DMA
    low, low_t, full = vmem((HALF, WIDE), BF16), vmem((WIDE, HALF), BF16), vmem((HALF, WIDE), F32)
    plans = part_plans()
    return Scratch(
        qkv=vmem((WIDE, 3 * WIDE), BF16),
        out=vmem((WIDE, WIDE), BF16),
        up=vmem((WIDE, 4 * WIDE), BF16),
        down=vmem((4 * WIDE, WIDE), BF16),
        e=low,
        a2=low,
        q=low,
        k=vmem((2 * HALF, WIDE), BF16),
        v=vmem((2 * HALF, WIDE), BF16),
        ot=low_t,
        ft=vmem((2, WIDE, HALF), BF16),
        a1t=vmem((2, WIDE // 2, HALF), BF16),
        a2t=vmem((2, WIDE // 2, HALF), BF16),
        h=full,
        y=full,
        mid=full,
        dh=full,
        lse=vmem((16, HALF), F32),
        pair_send=vmem((2, 6, HALF, 128), BF16),
        pair_recv=vmem((2, 6, HALF, 128), BF16),
        flat_f=vmem((F_BASE + F_ROWS + 64, 128), F32),
        flat_a=vmem((A_BASE + A_ROWS + 32, 128), F32),
        vec=[vmem((6, V_EARLY, 128), F32), vmem((6, SLOTS - V_EARLY, 128), F32)],
        vec_recv=[vmem((5, V_EARLY, 128), F32), vmem((5, SLOTS - V_EARLY, 128), F32)],
        ids=vmem((32, 8, 128), I32),
        down_send=vmem((2, 2, 192, WIDE), BF16),
        up_send=vmem((2, 8, 48, WIDE), BF16),
        out_send=vmem((4, 96, WIDE), BF16),
        qkv_send=vmem((2, 12, 32, WIDE), BF16),
        local=[
            [vmem((2, 192, WIDE), BF16)] * 4,
            [vmem((8, 48, WIDE), BF16)] * 4,
            [vmem((4, 96, WIDE), BF16)],
            [vmem((12, 32, WIDE), BF16)] * 3,
        ],
        landing={
            key: [vmem((count, rows, WIDE), BF16) for count in Part.landing_blocks(order, fixed)]
            for key, (order, fixed, rows) in plans.items()
        },
        sems={key: dma((2, 4)) for key in plans},
        load_sem=dma((21,)),
        core_sem=dma((2, 12)),
        pair_sem=dma((2, 2, 6)),
        vec_sem=[dma((2, 5)), dma((2, 5))],
        ids_sem=dma((2, 5)),
        edge_sem=dma((2, 4)),
        result_sem=dma((2, 3)),
    )


STAGES = (CORE, X, Y, Z0, Z1)


def backward_kernel(*refs):
    (
        x_in, a1t_in, q_in, k_in, v_in, ot_in, lse_in, e_in, cot_in, qkv_in, out_in, up_in, down_in,
        len_tile, gain1, out_bias, gain2, bias2, up_bias, down_bias, gene_ids, lens,
    ) = refs[:22]
    output_o, rows_o, attn_o, ffn_o, counts_o = refs[22:27]
    s = jax.tree.unflatten(jax.tree.structure(backward_scratch()), refs[27:])
    place = Place()
    core, y_bit = place.core, place.y
    mate = place.partner[CORE]
    greeted = greet(place, range(8))

    own_half = pl.ds(pl.multiple_of(core * HALF, HALF), HALF)
    far_half = pl.ds(pl.multiple_of((1 - core) * HALF, HALF), HALF)
    load_sem = s.load_sem

    def load(n, src, dst):
        copy = pltpu.make_async_copy(src, dst, load_sem.at[n])
        copy.start()
        return copy

    load_out = [load(0, ot_in, s.ot), load(1, out_in, s.out), load(2, x_in, s.h)]
    load_e = [pltpu.make_async_copy(ref, s.e, load_sem.at[3]) for ref in (cot_in, e_in)]
    pl.when(place.stays)(load_e[0].start)
    pl.when(place.moves)(load_e[1].start)
    load_up, load_down = [], []
    for j in range(4):
        cols = pl.ds(WIDE * j, WIDE)
        load_up.append(load(4 + 2 * j, up_in.at[:, cols], s.up.at[:, cols]))
        load_down.append(load(5 + 2 * j, down_in.at[cols], s.down.at[cols]))

    def put_vec(slot, row):
        late = int(slot >= V_EARLY)
        slot -= late * V_EARLY
        for t in range(row.shape[1] // 128):
            s.vec[late][0, slot + t : slot + t + 1] = row[:, 128 * t : 128 * t + 128]

    def flat_store(ref, base, stride, value, skip=0):
        for t in range(WIDE // 128):
            at = pl.ds(base + t + t // 2 * skip, value.shape[0], stride=stride)
            ref[at, :] = value[:, 128 * t : 128 * t + 128]

    parts = {}
    for key, (order, fixed, rows) in part_plans().items():
        kind, n = key
        if kind == DOWN:
            local = s.local[DOWN][n]
            finish = functools.partial(flat_store, s.flat_f, F_BASE, 6)
        elif kind == UP:
            local = s.local[UP][n]
            finish = functools.partial(flat_store, s.flat_f, F_BASE + 6 * n, 24)
        elif kind == OUT:
            local = s.local[OUT][0]
            finish = functools.partial(flat_store, s.flat_a, A_BASE, 6)
        else:
            whole = s.local[LOW][n]
            local = whole.at[pl.ds(0, 8)] if kind == LOW else whole.at[pl.ds(8, 4)]
            finish = functools.partial(flat_store, s.flat_a, A_BASE + 2 * n, 18, skip=4)
        landing = s.landing[key]
        parts[key] = Part(place, order, fixed, rows, local, landing, s.sems[key], finish)

    vec_copies = [[], []]

    def vec_launch(late):
        n = len(vec_copies[late])
        copy = remote(
            s.vec[late].at[n], s.vec_recv[late].at[n],
            s.vec_sem[late].at[0, n], s.vec_sem[late].at[1, n],
            place.partner[STAGES[n]],
        )
        copy.start()
        vec_copies[late].append(copy)

    def vec_tick(late):
        n = len(vec_copies[late])
        vec_copies[late][-1].wait_recv()
        s.vec[late][n] = s.vec[late][n - 1] + s.vec_recv[late][n - 1]
        if n < 5:
            vec_launch(late)

    edges = []

    def edge_launch(ref, base, rows):
        end = base + rows
        for src, dst, size, to in ((end - 24, base - 24, 24, NEXT), (base, end, 32, PREV)):
            n = len(edges)
            copy = remote(
                ref.at[pl.ds(src, size)], ref.at[pl.ds(dst, size)],
                s.edge_sem.at[0, n], s.edge_sem.at[1, n], place.partner[to],
            )
            copy.start()
            edges.append(copy)

    def count(n, total):
        high_row = lax.broadcasted_iota(I32, (288, 128), 0)
        low_row = lax.broadcasted_iota(I32, (128, 128), 0)
        tile = s.ids[n]
        for r in range(0, 4, 2):
            high = [(high_row == (tile[r + i : r + i + 1] >> 7)).astype(F32).astype(BF16) for i in range(2)]
            low = [(low_row == (tile[r + i : r + i + 1] & 127)).astype(F32).astype(BF16) for i in range(2)]
            total = total + mm(jnp.concatenate(high, axis=1), jnp.concatenate(low, axis=1), NT)
        return total

    def count_all():
        counts_o[...] = lax.fori_loop(0, 32, count, jnp.zeros((288, 128), F32)).astype(I32)

    special = {
        IDS: lambda: ids_tick(),
        VEC: lambda: vec_tick(0),
        LATE: lambda: vec_tick(1),
        COUNT: count_all,
        EDGE: lambda: edge_launch(s.flat_f, F_BASE, F_ROWS),
    }

    def pause(hook):
        for entry in SCHEDULE.get(hook, ()):
            if isinstance(entry, tuple):
                parts[entry].tick()
            else:
                special[entry]()

    core_copies = []

    def core_send(src, dst):
        n = len(core_copies)
        copy = remote(src, dst, s.core_sem.at[0, n], s.core_sem.at[1, n], mate)
        copy.start()
        core_copies.append(copy)
        return copy

    def put_blocks(ref, key, value):
        order, fixed, rows = part_plans()[key]
        free = [name for name in order if name not in fixed]
        natural = [name for name in (Z1, Z0, X, Y) if name not in fixed]
        for m in range(2 ** len(free)):
            bits = {name: (m >> (len(natural) - 1 - i)) & 1 for i, name in enumerate(natural)}
            at = sum(bits[name] << (len(free) - 1 - i) for i, name in enumerate(free))
            ref[at] = value[m * rows : m * rows + rows]

    for copy in load_out:
        copy.wait()
    gain2_row, bias2_row = gain2[...].reshape(1, WIDE), bias2[...].reshape(1, WIDE)
    h, y, mid, dh, e = s.h, s.y, s.mid, s.dh, s.e
    h[...] = h[...] + mm(s.ot[...].T, s.out[...]) + out_bias[...].reshape(1, WIDE)
    for r in range(4):
        at = pl.ds(128 * r, 128)
        normed, _ = hat_of(h[at])
        s.a2[at] = (normed * gain2_row + bias2_row).astype(BF16)
        y[at] = h[at] + down_bias[...].reshape(1, WIDE)
    flipped = s.a2[...].T
    for c in range(2):
        for m in range(4):
            s.a2t[c, 96 * m : 96 * m + 96] = flipped[192 * m + 96 * c : 192 * m + 96 * c + 96]

    own_len = jnp.full((1, 128), lens[0], I32)
    slots = lax.broadcasted_iota(I32, (1, 128), 1) + y_bit * HALF
    ids = s.ids
    here = sum(place.bit[name] * 2**stage for stage, name in enumerate(STAGES))
    tile = [
        jnp.where(slots + 128 * r < own_len, gene_ids[0:1, 128 * r : 128 * r + 128], -1) for r in range(4)
    ]
    ids[pl.ds(here, 1)] = jnp.concatenate(tile + [jnp.full((4, 128), -1, I32)], axis=0)[None]
    ids_copies = []

    def ids_launch(stage):
        size = 2**stage
        at = pl.ds((here // size) * size, size)
        copy = remote(
            ids.at[at], ids.at[at], s.ids_sem.at[0, stage], s.ids_sem.at[1, stage],
            place.partner[STAGES[stage]],
        )
        copy.start()
        ids_copies.append(copy)

    def ids_tick():
        ids_copies[-1].wait_recv()
        if len(ids_copies) < 5:
            ids_launch(len(ids_copies))

    greeted()
    ids_launch(0)

    load_e[0].wait()
    put_vec(V_DOWN, jnp.sum(e[...].astype(F32), axis=0, keepdims=True))
    half_rows = WIDE // 2
    theirs = pl.ds(pl.multiple_of((1 - core) * half_rows, half_rows), half_rows)
    ours = pl.ds(pl.multiple_of(core * half_rows, half_rows), half_rows)

    def settle(j, grad, down_copy, up_copy):
        own = mm(s.ft[j % 2, ours], e[...]).reshape(2, 192, WIDE)
        down_copy.wait_recv()
        local = s.local[DOWN][j]
        local[...] = (own + local[...].astype(F32)).astype(BF16)
        parts[DOWN, j].launch()
        own = mm(s.a2t[core], grad)
        up_copy.wait_recv()
        add_blocks(s.local[UP][j], (UP, j), own)
        parts[UP, j].launch()

    waiting = None
    for j in range(4):
        cols = pl.ds(WIDE * j, WIDE)
        load_up[j].wait()
        load_down[j].wait()
        if j == 0:
            load_att = [
                load(12, q_in, s.q),
                load(13, k_in.at[own_half], s.k.at[pl.ds(0, HALF)]),
                load(14, k_in.at[far_half], s.k.at[pl.ds(HALF, HALF)]),
                load(15, v_in.at[own_half], s.v.at[pl.ds(0, HALF)]),
                load(16, v_in.at[far_half], s.v.at[pl.ds(HALF, HALF)]),
                load(17, lse_in, s.lse),
            ]
            load_qkv = [load(18, a1t_in, s.a1t), load(19, qkv_in, s.qkv)]
        inner = mm(s.a2[...], s.up[:, cols]) + up_bias[WIDE * j : WIDE * j + WIDE].reshape(1, WIDE)
        phi = 0.5 * (1.0 + lax.erf(inner * 0.7071067811865476))
        slope = phi + inner * jnp.exp2(inner * inner * (-0.5 * LOG2E)) * 0.3989422804014327
        active = (inner * phi).astype(BF16)
        s.ft[j % 2] = active.T
        if j:
            settle(j - 1, *waiting)
        if j >= 2:
            core_copies[2 * j - 4].wait_send()
            core_copies[2 * j - 3].wait_send()
        sent = s.down_send.at[j % 2]
        sent[...] = mm(s.ft[j % 2, theirs], e[...]).astype(BF16).reshape(2, 192, WIDE)
        down_copy = core_send(sent, s.local[DOWN][j])
        pause(4 * j)
        grad = (mm(e[...], s.down[cols], NT) * slope).astype(BF16)
        sent = s.up_send.at[j % 2]
        put_blocks(sent, (UP, j), mm(s.a2t[1 - core], grad).astype(BF16))
        up_copy = core_send(sent, s.local[UP][j])
        pause(4 * j + 1)
        put_vec(V_UP + 6 * j, jnp.sum(grad.astype(F32), axis=0, keepdims=True))
        back = mm(grad, s.up[:, cols], NT)
        mid[...] = back if j == 0 else mid[...] + back
        y[...] = y[...] + mm(active, s.down[cols])
        pause(4 * j + 2)
        waiting = (grad, down_copy, up_copy)
    down = s.down
    grad_h, grad_o, grad_rows, *grads = [down.at[pl.ds(HALF * n, HALF)] for n in range(6)]
    output = s.a2
    sums = [jnp.zeros((1, WIDE), F32) for _ in range(3)]
    for r in range(4):
        at = pl.ds(128 * r, 128)
        output[at] = y[at].astype(BF16)
        normed, inv_std = hat_of(h[at])
        grad = mid[at]
        sums[0] += jnp.sum(grad * normed, axis=0, keepdims=True)
        sums[1] += jnp.sum(grad, axis=0, keepdims=True)
        total = e[at].astype(F32) + norm_pull(grad, normed, inv_std, gain2_row)
        dh[at] = total
        low = total.astype(BF16)
        grad_h[at] = low
        sums[2] += jnp.sum(low.astype(F32), axis=0, keepdims=True)
    put_vec(V_GAIN2, sums[0])
    put_vec(V_BIAS2, sums[1])
    put_vec(V_OUT, sums[2])

    result_copies = []

    def give_back(n, src, dst):
        keep = pltpu.make_async_copy(src, dst, s.result_sem.at[n, 2])
        swap = remote(
            src, dst, s.result_sem.at[n, 0], s.result_sem.at[n, 1], place.partner[DIAG]
        )
        pl.when(place.stays)(keep.start)
        pl.when(place.moves)(swap.start)
        result_copies.append((keep, swap))

    settle(3, *waiting)
    vec_launch(0)
    give_back(0, output, output_o)
    pause(NORM2)

    def out_rows(c):
        return jnp.concatenate(
            [s.ot[pl.ds(pl.multiple_of(384 * x + 192 * c, 192), 192)] for x in range(2)], axis=0
        )

    put_blocks(s.out_send, (OUT, 0), mm(out_rows(1 - core), grad_h[...]).astype(BF16))
    out_copy = core_send(s.out_send, s.local[OUT][0])
    grad_o[...] = mm(grad_h[...], s.out[...], NT).astype(BF16)
    up = s.up
    grad_ot, grad_qt, qt = [up.at[:, pl.ds(HALF * n, HALF)] for n in range(3)]
    grad_ot[...] = grad_o[...].T
    for copy in load_att:
        copy.wait()
    load_x = pltpu.make_async_copy(x_in, y, load_sem.at[20])
    load_x.start()
    qt[...] = s.q[...].T
    own = mm(out_rows(core), grad_h[...])
    out_copy.wait_recv()
    add_blocks(s.local[OUT][0], (OUT, 0), own)
    parts[OUT, 0].launch()
    pause(PROJECT)

    length = len_tile[0:1, 0:1]
    live_own = column(length, core * HALF, HALF)
    live_far = column(length, (1 - core) * HALF, HALF)
    live = jnp.concatenate([live_own, live_far], axis=0)
    lane = lax.broadcasted_iota(I32, (1, 128), 1)
    dk, dv = h, mid
    pair_copies, qkv_copies = [], []

    def far_qkv(g):
        grad = grads[g]
        grad[:, :256] = grad_qt[256 * g : 256 * g + 256].T
        for i in range(2):
            j = 2 * g + i
            for n, mine in enumerate((dk, dv)):
                pair_copies[2 * j + n].wait_recv()
                total = mine[:, 128 * j : 128 * j + 128] + s.pair_recv[n, j].astype(F32)
                start = 256 * (n + 1) + 128 * i
                grad[:, start : start + 128] = jnp.where(live_own, total, 0.0).astype(BF16)
        sent = s.qkv_send.at[g % 2]
        if g == 2:
            qkv_copies[0].wait_send()
        value = mm(s.a1t[1 - core], grad[...]).astype(BF16)
        put_blocks(sent.at[pl.ds(0, 8)], (LOW, g), value[:256])
        put_blocks(sent.at[pl.ds(8, 4)], (HIGH, g), value[256:])
        qkv_copies.append(core_send(sent, s.local[LOW][g]))

    def settle_qkv(g):
        own = mm(s.a1t[core], grads[g][...])
        qkv_copies[g].wait_recv()
        local = s.local[LOW][g]
        add_blocks(local.at[pl.ds(0, 8)], (LOW, g), own[:256])
        add_blocks(local.at[pl.ds(8, 4)], (HIGH, g), own[256:])
        parts[LOW, g].launch()
        parts[HIGH, g].launch()

    def pull_qkv(g):
        grad, at = grads[g], lambda p: slice(WIDE * p + 256 * g, WIDE * p + 256 * g + 256)
        total = mm(grad[:, :256], s.qkv[:, at(0)], NT)
        total = total + mm(grad[:, 256:512], s.qkv[:, at(1)], NT)
        return total + mm(grad[:, 512:], s.qkv[:, at(2)], NT)

    for j in range(WIDE // 128):
        at = slice(128 * j, 128 * j + 128)
        keys, values = s.k[:, at], s.v[:, at]
        keys_t = jnp.where(live, keys, jnp.zeros_like(keys)).T
        grad_keys = grad_values = None
        for i in range(2):
            head = 2 * j + i
            rows = slice(HDIM * head, HDIM * head + HDIM)
            mine = lane // HDIM == i
            scores = mm(keys, padded_head(qt[rows], i))
            probs = jnp.exp2(scores - s.lse[head : head + 1])
            grad_ot_head = grad_ot[rows]
            grad_probs = mm(values, padded_head(grad_ot_head, i))
            delta = jnp.sum(
                grad_ot_head.astype(F32) * s.ot[rows].astype(F32), axis=0, keepdims=True
            )
            grad_scores = (probs * (grad_probs - delta)).astype(BF16)
            queries = jnp.where(mine, s.q[:, at], jnp.zeros((), BF16))
            grad_out = jnp.where(mine, grad_o[:, at], jnp.zeros((), BF16))
            more = mm(probs.astype(BF16), grad_out)
            grad_values = more if i == 0 else grad_values + more
            more = mm(grad_scores, queries)
            grad_keys = more if i == 0 else grad_keys + more
            grad_qt[rows] = (mm(keys_t[HDIM * i : HDIM * i + HDIM], grad_scores) * HDIM**-0.5).astype(BF16)
        grad_keys = grad_keys * LN2
        dk[:, at] = grad_keys[:HALF]
        dv[:, at] = grad_values[:HALF]
        for n, value in enumerate((grad_keys, grad_values)):
            s.pair_send[n, j] = value[HALF:].astype(BF16)
            copy = remote(
                s.pair_send.at[n, j], s.pair_recv.at[n, j],
                s.pair_sem.at[0, n, j], s.pair_sem.at[1, n, j], mate,
            )
            copy.start()
            pair_copies.append(copy)
        if j == 0:
            for copy in load_qkv:
                copy.wait()
        elif j % 2 == 0:
            far_qkv(j // 2 - 1)
        elif j > 1:
            settle_qkv(j // 2 - 1)
        pause(PAIRS + j)
    back = pull_qkv(0) + pull_qkv(1)
    far_qkv(2)
    pause(QKV)

    mid[...] = back + pull_qkv(2)
    load_x.wait()
    gain1_row = gain1[...].reshape(1, WIDE)
    sums = [jnp.zeros((1, WIDE), F32) for _ in range(2)]
    for r in range(4):
        at = pl.ds(128 * r, 128)
        normed, inv_std = hat_of(y[at])
        grad = mid[at]
        sums[0] += jnp.sum(grad * normed, axis=0, keepdims=True)
        sums[1] += jnp.sum(grad, axis=0, keepdims=True)
        grad_rows[at] = (dh[at] + norm_pull(grad, normed, inv_std, gain1_row)).astype(BF16)
    put_vec(V_GAIN1, sums[0])
    put_vec(V_BIAS1, sums[1])
    give_back(1, grad_rows, rows_o)
    for p, slot in enumerate((V_QUERY, None, V_VALUE)):
        if p != 1:
            total = [jnp.sum(grad[:, 256 * p : 256 * p + 256].astype(F32), axis=0, keepdims=True) for grad in grads]
            put_vec(slot, jnp.concatenate(total, axis=1))
    vec_launch(1)
    settle_qkv(2)
    pause(NORM1)

    pause(END)
    while any(not part.done for part in parts.values()):
        for part in parts.values():
            if not part.done:
                part.tick()
    edge_launch(s.flat_a, A_BASE, A_ROWS)
    for copy in edges:
        copy.wait()
    total = jnp.concatenate([s.vec[0][5], s.vec[1][5]], axis=0)
    flat_f, flat_a = s.flat_f, s.flat_a
    me = place.index
    f_end, a_end = F_BASE + F_ROWS, A_BASE + A_ROWS

    @pl.when(me == 0)
    def _():
        flat_f[F_BASE - 12 : F_BASE] = total[V_GAIN2 : V_GAIN2 + 12]
        flat_a[A_BASE - 12 : A_BASE] = total[V_GAIN1 : V_GAIN1 + 12]

    @pl.when(me == 15)
    def _():
        flat_f[f_end : f_end + 24] = total[V_UP : V_UP + 24]

    @pl.when(me == 16)
    def _():
        flat_f[F_BASE - 24 : F_BASE] = total[V_UP : V_UP + 24]

    @pl.when(me == 23)
    def _():
        flat_a[a_end : a_end + 12] = total[V_QUERY : V_QUERY + 12]

    @pl.when(me == 31)
    def _():
        flat_f[f_end : f_end + 6] = total[V_DOWN : V_DOWN + 6]
        flat_f[f_end + 6 : f_end + 32] = jnp.zeros((26, 128), F32)
        flat_a[a_end : a_end + 6] = total[V_OUT : V_OUT + 6]
        flat_a[a_end + 6 : a_end + 32] = jnp.zeros((26, 128), F32)

    f_start = jnp.where(me < 16, F_BASE - 12 + 2 * me, F_BASE - 4 + 2 * (me - 16))
    a_start = jnp.where(me < 24, A_BASE - 12 + me, A_BASE + me - 24)
    ffn_o[...] = flat_f[pl.ds(f_start, ffn_o.shape[0]), :]
    attn_o[...] = flat_a[pl.ds(a_start, attn_o.shape[0]), :]

    for part in parts.values():
        part.drain()
    core_copies[4].wait_send()
    for n in (5, 6, 7, 8, 10, 11):
        core_copies[n].wait_send()
    for copy in pair_copies + ids_copies + vec_copies[0] + vec_copies[1]:
        copy.wait_send()
    for keep, swap in result_copies:
        pl.when(place.stays)(keep.wait)
        pl.when(place.moves)(swap.wait)


def add_blocks(ref, key, value):
    order, fixed, rows = part_plans()[key]
    free = [name for name in order if name not in fixed]
    natural = [name for name in (Z1, Z0, X, Y) if name not in fixed]
    for m in range(2 ** len(free)):
        bits = {name: (m >> (len(natural) - 1 - i)) & 1 for i, name in enumerate(natural)}
        at = sum(bits[name] << (len(free) - 1 - i) for i, name in enumerate(free))
        ref[at] = (ref[at].astype(F32) + value[m * rows : m * rows + rows]).astype(BF16)


def backward_call(arrays, weights, len_tile, vectors, gene_ids, lengths, attn_units, ffn_units):
    any_spec = pl.BlockSpec(memory_space=pl.ANY)
    vmem = pl.BlockSpec(memory_space=pltpu.VMEM)
    shape = jax.ShapeDtypeStruct
    return pl.pallas_call(
        backward_kernel,
        out_shape=(
            shape((HALF, WIDE), BF16),
            shape((HALF, WIDE), BF16),
            shape((attn_units, 128), F32),
            shape((ffn_units, 128), F32),
            shape((288, 128), I32),
        ),
        in_specs=[any_spec] * 13 + [vmem] * 8 + [pl.BlockSpec(memory_space=pltpu.SMEM)],
        out_specs=(any_spec, any_spec, vmem, vmem, vmem),
        scratch_shapes=jax.tree.leaves(backward_scratch()),
        compiler_params=pltpu.CompilerParams(
            collective_id=1, has_side_effects=True, vmem_limit_bytes=64 * 2**20
        ),
        name="backward",
    )(*arrays, *weights, len_tile, *vectors, gene_ids, lengths)


def hand_over_kernel(output_in, rows_in, attn_in, ffn_in, counts_in, output_o, rows_o, attn_o, ffn_o, counts_o, *scratch):
    *held, load_sem, store_sem = scratch
    pairs = ((output_in, output_o), (rows_in, rows_o), (attn_in, attn_o), (ffn_in, ffn_o))
    loads = [pltpu.make_async_copy(src, ref, load_sem.at[n]) for n, ((src, _), ref) in enumerate(zip(pairs, held))]
    stores = [pltpu.make_async_copy(ref, dst, store_sem.at[n]) for n, ((_, dst), ref) in enumerate(zip(pairs, held))]
    for copy in loads:
        copy.start()
    counts_o[...] = counts_in[...].reshape(-1)[: counts_o.shape[0]]
    for load, store in zip(loads, stores):
        load.wait()
        store.start()
    for store in stores:
        store.wait()


def hand_over_call(results):
    any_spec = pl.BlockSpec(memory_space=pl.ANY)
    vmem = pl.BlockSpec(memory_space=pltpu.VMEM)
    large = results[:4]
    return pl.pallas_call(
        hand_over_kernel,
        out_shape=tuple(jax.ShapeDtypeStruct(r.shape, r.dtype) for r in large)
        + (jax.ShapeDtypeStruct((VOCAB,), I32),),
        in_specs=[any_spec] * 4 + [vmem],
        out_specs=(any_spec,) * 4 + (vmem,),
        scratch_shapes=[pltpu.VMEM(r.shape, r.dtype) for r in large]
        + [pltpu.SemaphoreType.DMA((4,)), pltpu.SemaphoreType.DMA((4,))],
        name="hand_over",
    )(*results)


def on_device(
    row_gene,
    row_value,
    row_promoter,
    row_grn,
    row_coexp,
    row_family,
    lengths,
    gene_ids,
    norm1_gain,
    norm1_bias,
    qkv_weight,
    query_bias,
    value_bias,
    out_weight,
    out_bias,
    norm2_gain,
    norm2_bias,
    up_weight,
    up_bias,
    down_weight,
    down_bias,
    cotangent,
):
    rows = [
        member.reshape(HALF, WIDE)
        for member in (row_gene, row_value, row_promoter, row_grn, row_coexp, row_family)
    ]
    x, a1t, q, k, v, ot, lse, e, len_tile = attend_call(
        rows,
        cotangent.reshape(HALF, WIDE),
        lengths,
        qkv_weight,
        norm1_gain,
        norm1_bias,
        query_bias,
        value_bias,
    )
    devices = lax.axis_size("dp") * lax.axis_size("seq")
    attn_len, ffn_len = gradient_lengths(WIDE, 4 * WIDE, devices)
    results = backward_call(
        (x, a1t, q, k, v, ot, lse, e, cotangent.reshape(HALF, WIDE)),
        (qkv_weight, out_weight, up_weight, down_weight),
        len_tile,
        (norm1_gain, out_bias, norm2_gain, norm2_bias, up_bias, down_bias),
        gene_ids,
        lengths,
        attn_len // devices // 128,
        ffn_len // devices // 128,
    )
    output, grad_rows, attn, ffn, counts = hand_over_call(results)
    return (
        output.reshape(row_gene.shape),
        grad_rows.reshape(row_gene.shape),
        attn.reshape(-1),
        ffn.reshape(-1),
        counts,
    )


def gradient_lengths(width, hidden, devices):
    pad = lambda count: -(-count // (devices * 128)) * devices * 128
    return (
        pad(3 * width * width + width * width + 5 * width),
        pad(2 * width * hidden + 3 * width + hidden),
    )


def layer_norm(values_in, gain_vec, bias_vec):
    center = values_in - jnp.mean(values_in, axis=-1, keepdims=True)
    variance = jnp.mean(center * center, axis=-1, keepdims=True)
    inv_std = lax.rsqrt(variance + EPSILON)
    normed = center * inv_std
    return (normed * gain_vec + bias_vec, normed, inv_std)


def norm_back(grad_normed, normed, inv_std, gain_vec):
    grad_hat = grad_normed * gain_vec
    grad_gain = jnp.sum(grad_normed * normed, axis=0)
    grad_bias = jnp.sum(grad_normed, axis=0)
    grad_input = inv_std * (
        grad_hat
        - jnp.mean(grad_hat, axis=-1, keepdims=True)
        - normed * jnp.mean(grad_hat * normed, axis=-1, keepdims=True)
    )
    return (grad_input, grad_gain, grad_bias)


def gelu_exact(inner):
    return jax.nn.gelu(inner, approximate=False)


def padded_flat(members, multiple):
    flat = jnp.concatenate([member.reshape(-1) for member in members])
    total = -(-flat.shape[0] // multiple) * multiple
    return jnp.pad(flat, (0, total - flat.shape[0]))


def attend(queries, key_rows, value_rows, key_keep):
    cell_count, query_len, local_width = queries.shape
    head_count = local_width // HDIM
    block_rows = min(query_len, 512)
    block_count = query_len // block_rows
    scale = HDIM ** (-0.5)

    def one_cell(inputs):
        cell_query, cell_key, cell_value, cell_keep = inputs
        key_heads = cell_key.reshape(-1, head_count, HDIM)
        value_heads = cell_value.reshape(-1, head_count, HDIM)

        def one_block(query_block):
            scores = (
                jnp.einsum(
                    "qhd,khd->hqk", query_block, key_heads, preferred_element_type=jnp.float32
                )
                * scale
            )
            scores = jnp.where(cell_keep[None, None, :], scores, NEGATIVE)
            row_max = jnp.max(scores, axis=-1, keepdims=True)
            exp_scores = jnp.exp(scores - row_max)
            row_total = jnp.sum(exp_scores, axis=-1, keepdims=True)
            attn_probs = exp_scores / row_total
            context = jnp.einsum(
                "hqk,khd->qhd",
                attn_probs.astype(jnp.bfloat16),
                value_heads,
                preferred_element_type=jnp.float32,
            )
            return (
                context.reshape(block_rows, local_width),
                (row_max + jnp.log(row_total))[..., 0],
            )

        context, log_total = lax.map(
            one_block, cell_query.reshape(block_count, block_rows, head_count, HDIM)
        )
        return (context.reshape(query_len, local_width), log_total)

    return lax.map(one_cell, (queries, key_rows, value_rows, key_keep))


def attend_back(queries, key_rows, value_rows, key_keep, log_total, grad_context):
    cell_count, query_len, local_width = queries.shape
    head_count = local_width // HDIM
    block_rows = min(query_len, 512)
    block_count = query_len // block_rows
    scale = HDIM ** (-0.5)

    def one_cell(inputs):
        cell_query, cell_key, cell_value, cell_keep, cell_lse, cell_grad = inputs
        key_heads = cell_key.reshape(-1, head_count, HDIM)
        value_heads = cell_value.reshape(-1, head_count, HDIM)
        key_len = key_heads.shape[0]

        def one_block(running, block_in):
            query_block, lse_block, grad_block = block_in
            scores = (
                jnp.einsum(
                    "qhd,khd->hqk", query_block, key_heads, preferred_element_type=jnp.float32
                )
                * scale
            )
            scores = jnp.where(cell_keep[None, None, :], scores, NEGATIVE)
            attn_probs = jnp.exp(scores - lse_block[..., None])
            grad_probs = jnp.einsum(
                "qhd,khd->hqk", grad_block, value_heads, preferred_element_type=jnp.float32
            )
            grad_scores = (
                attn_probs * (grad_probs - jnp.sum(attn_probs * grad_probs, axis=-1, keepdims=True))
            ).astype(jnp.bfloat16)
            grad_query = (
                jnp.einsum(
                    "hqk,khd->qhd", grad_scores, key_heads, preferred_element_type=jnp.float32
                )
                * scale
            )
            grad_key = (
                running[0]
                + jnp.einsum(
                    "hqk,qhd->khd", grad_scores, query_block, preferred_element_type=jnp.float32
                )
                * scale
            )
            grad_value = running[1] + jnp.einsum(
                "hqk,qhd->khd",
                attn_probs.astype(jnp.bfloat16),
                grad_block,
                preferred_element_type=jnp.float32,
            )
            return ((grad_key, grad_value), grad_query.reshape(block_rows, local_width))

        zeros_start = jnp.zeros((key_len, head_count, HDIM), jnp.float32)
        (grad_key, grad_value), grad_query = lax.scan(
            one_block,
            (zeros_start, zeros_start),
            (
                cell_query.reshape(block_count, block_rows, head_count, HDIM),
                cell_lse,
                cell_grad.reshape(block_count, block_rows, head_count, HDIM),
            ),
        )
        return (
            grad_query.reshape(query_len, local_width),
            grad_key.reshape(key_len, local_width),
            grad_value.reshape(key_len, local_width),
        )

    return lax.map(one_cell, (queries, key_rows, value_rows, key_keep, log_total, grad_context))


def plain_on_device(
    row_gene,
    row_value,
    row_promoter,
    row_grn,
    row_coexp,
    row_family,
    lengths,
    gene_ids,
    norm1_gain,
    norm1_bias,
    qkv_weight,
    query_bias,
    value_bias,
    out_weight,
    out_bias,
    norm2_gain,
    norm2_bias,
    up_weight,
    up_bias,
    down_weight,
    down_bias,
    cotangent,
):
    cell_count, local_len, model_width = row_gene.shape
    row_count = cell_count * local_len
    seq_size = lax.axis_size("seq")
    multiple = lax.axis_size("dp") * seq_size * 128
    place = lax.axis_index("seq")
    positions = place * local_len + jnp.arange(local_len, dtype=jnp.int32)
    live_local = (positions[None, :] < lengths[:, None]).astype(jnp.int32)
    local_counts = jax.ops.segment_sum(
        live_local.reshape(-1), gene_ids.reshape(-1), num_segments=VOCAB
    )
    gene_counts = lax.psum(local_counts, ("dp", "seq"))
    summed = (
        row_gene.astype(jnp.float32)
        + row_value.astype(jnp.float32)
        + row_promoter.astype(jnp.float32)
        + row_grn.astype(jnp.float32)
        + row_coexp.astype(jnp.float32)
        + row_family.astype(jnp.float32)
    )
    summed = summed.reshape(row_count, model_width)
    normed_one, hat_one, inv_one = layer_norm(summed, norm1_gain, norm1_bias)
    normed_in = normed_one.astype(jnp.bfloat16)
    projected = jnp.dot(normed_in, qkv_weight, preferred_element_type=jnp.float32)
    query_full = projected[:, :model_width] + query_bias
    key_full = projected[:, model_width : 2 * model_width]
    value_full = projected[:, 2 * model_width :] + value_bias
    stacked = jnp.stack([query_full, key_full, value_full], axis=1).astype(jnp.bfloat16)
    stacked = stacked.reshape(cell_count, local_len, 3, model_width)
    full_len = local_len * seq_size
    key_keep = jnp.arange(full_len, dtype=jnp.int32)[None, :] < lengths[:, None]
    heads_in = lax.all_to_all(stacked, "seq", split_axis=3, concat_axis=1, tiled=True)
    query_att = heads_in[:, :, 0]
    key_att = heads_in[:, :, 1]
    value_att = heads_in[:, :, 2]
    context, log_total = attend(query_att, key_att, value_att, key_keep)
    context_local = lax.all_to_all(
        context.astype(jnp.bfloat16), "seq", split_axis=1, concat_axis=2, tiled=True
    )
    context_flat = context_local.reshape(row_count, model_width)
    hidden = (
        summed + jnp.dot(context_flat, out_weight, preferred_element_type=jnp.float32) + out_bias
    )
    normed_two, hat_two, inv_two = layer_norm(hidden, norm2_gain, norm2_bias)
    normed_mid = normed_two.astype(jnp.bfloat16)
    inner = jnp.dot(normed_mid, up_weight, preferred_element_type=jnp.float32) + up_bias
    activated, gelu_pull = jax.vjp(gelu_exact, inner)
    activated_low = activated.astype(jnp.bfloat16)
    result = (
        hidden + jnp.dot(activated_low, down_weight, preferred_element_type=jnp.float32) + down_bias
    )
    output = result.astype(jnp.bfloat16).reshape(cell_count, local_len, model_width)
    grad_out_low = cotangent.reshape(row_count, model_width)
    grad_out = grad_out_low.astype(jnp.float32)
    grad_down = jnp.einsum(
        "nf,nd->fd", activated_low, grad_out_low, preferred_element_type=jnp.float32
    )
    grad_down_bias = jnp.sum(grad_out, axis=0)
    grad_act = jnp.einsum(
        "nd,fd->nf", grad_out_low, down_weight, preferred_element_type=jnp.float32
    )
    grad_inner = gelu_pull(grad_act)[0].astype(jnp.bfloat16)
    grad_up = jnp.einsum("nd,nf->df", normed_mid, grad_inner, preferred_element_type=jnp.float32)
    grad_up_bias = jnp.sum(grad_inner.astype(jnp.float32), axis=0)
    grad_mid = jnp.einsum("nf,df->nd", grad_inner, up_weight, preferred_element_type=jnp.float32)
    grad_hid_norm, grad_gain_two, grad_bias_two = norm_back(grad_mid, hat_two, inv_two, norm2_gain)
    grad_hidden = grad_out + grad_hid_norm
    ffn_flat = padded_flat(
        (grad_gain_two, grad_bias_two, grad_up, grad_up_bias, grad_down, grad_down_bias), multiple
    )
    grad_hidden_low = grad_hidden.astype(jnp.bfloat16)
    grad_out_weight = jnp.einsum(
        "nc,nd->cd", context_flat, grad_hidden_low, preferred_element_type=jnp.float32
    )
    grad_out_bias = jnp.sum(grad_hidden_low.astype(jnp.float32), axis=0)
    grad_context = jnp.einsum(
        "nd,cd->nc", grad_hidden_low, out_weight, preferred_element_type=jnp.float32
    )
    grad_context = grad_context.astype(jnp.bfloat16).reshape(cell_count, local_len, model_width)
    grad_heads = lax.all_to_all(grad_context, "seq", split_axis=2, concat_axis=1, tiled=True)
    grad_query, grad_key, grad_value = attend_back(
        query_att, key_att, value_att, key_keep, log_total, grad_heads
    )
    grad_stack = jnp.stack([grad_query, grad_key, grad_value], axis=2).astype(jnp.bfloat16)
    grad_local = lax.all_to_all(grad_stack, "seq", split_axis=1, concat_axis=3, tiled=True)
    grad_qkv = grad_local.reshape(row_count, 3 * model_width)
    grad_qkv_weight = jnp.einsum(
        "nd,ne->de", normed_in, grad_qkv, preferred_element_type=jnp.float32
    )
    grad_query_bias = jnp.sum(grad_qkv[:, :model_width].astype(jnp.float32), axis=0)
    grad_value_bias = jnp.sum(grad_qkv[:, 2 * model_width :].astype(jnp.float32), axis=0)
    grad_normed_in = jnp.einsum(
        "ne,de->nd", grad_qkv, qkv_weight, preferred_element_type=jnp.float32
    )
    grad_sum_norm, grad_gain_one, grad_bias_one = norm_back(
        grad_normed_in, hat_one, inv_one, norm1_gain
    )
    grad_rows = (
        (grad_hidden + grad_sum_norm)
        .astype(jnp.bfloat16)
        .reshape(cell_count, local_len, model_width)
    )
    attn_flat = padded_flat(
        (
            grad_gain_one,
            grad_bias_one,
            grad_qkv_weight,
            grad_query_bias,
            grad_value_bias,
            grad_out_weight,
            grad_out_bias,
        ),
        multiple,
    )
    attn_share, ffn_share = (
        lax.psum_scatter(attn_flat, ("dp", "seq"), scatter_dimension=0, tiled=True),
        lax.psum_scatter(ffn_flat, ("dp", "seq"), scatter_dimension=0, tiled=True),
    )
    return (output, grad_rows, attn_share, ffn_share, gene_counts)


def fits(mesh):
    return dict(mesh.shape) == {"dp": 16, "seq": 2}


def solution(mesh):
    return jax.shard_map(
        on_device if fits(mesh) else plain_on_device,
        mesh=mesh,
        in_specs=(
            P("dp", "seq", None),
            P("dp", "seq", None),
            P("dp", "seq", None),
            P("dp", "seq", None),
            P("dp", "seq", None),
            P("dp", "seq", None),
            P("dp"),
            P("dp", "seq"),
            P(),
            P(),
            P(),
            P(),
            P(),
            P(),
            P(),
            P(),
            P(),
            P(),
            P(),
            P(),
            P(),
            P("dp", "seq", None),
        ),
        out_specs=(
            P("dp", "seq", None),
            P("dp", "seq", None),
            P(("dp", "seq")),
            P(("dp", "seq")),
            P(),
        ),
        check_vma=False,
    )
```

```python
import functools
import typing

import jax
import jax.numpy as jnp
from jax import lax
from jax.experimental import pallas as pl
from jax.experimental.pallas import tpu as pltpu
from jax.sharding import PartitionSpec as P

HDIM = 64
VOCAB = 36000
EPSILON = 1e-05
NEGATIVE = -1e30

F32, BF16, I32 = jnp.float32, jnp.bfloat16, jnp.int32
MESH = pl.DeviceIdType.MESH
LOG2E = 1.4426950408889634
LN2 = 0.6931471805599453
HALF = 512
WIDE = 768
NT = (((1,), (1,)), ((), ()))
NN = (((1,), (0,)), ((), ()))


def mm(lhs, rhs, dims=NN):
    return lax.dot_general(lhs, rhs, dims, preferred_element_type=F32)


def when(pred, body):
    if pred is None:
        body()
    else:
        pl.when(pred)(body)


def both(one, other):
    if one is None:
        return other
    if other is None:
        return one
    return jnp.logical_and(one, other)


CORE, X, Y, Z0, Z1, DIAG, NEXT, PREV = range(8)


class Place:
    def __init__(self):
        self.dp = lax.axis_index("dp")
        self.y = lax.axis_index("seq")
        self.core = self.dp % 2
        self.bit = [
            self.core,
            (self.dp // 2) % 2,
            self.y,
            (self.dp // 4) % 2,
            (self.dp // 8) % 2,
        ]
        flip = lambda name, step: self.dp + step - 2 * step * self.bit[name]
        self.index = self.dp * 2 + self.y
        count = 32
        after, before = (self.index + 1) % count, (self.index + count - 1) % count
        self.partner = [
            (flip(CORE, 1), self.y),
            (flip(X, 2), self.y),
            (self.dp, 1 - self.y),
            (flip(Z0, 4), self.y),
            (flip(Z1, 8), self.y),
            (flip(CORE, 1), 1 - self.y),
            (after // 2, after % 2),
            (before // 2, before % 2),
        ]
        self.moves = self.core != self.y
        self.stays = self.core == self.y


def greet(place, names):
    barrier = pltpu.get_barrier_semaphore()
    for name in names:
        pl.semaphore_signal(barrier, inc=1, device_id=place.partner[name], device_id_type=MESH)
    return lambda: pl.semaphore_wait(barrier, len(names))


def remote(src, dst, send_sem, recv_sem, partner):
    return pltpu.make_async_remote_copy(
        src_ref=src,
        dst_ref=dst,
        send_sem=send_sem,
        recv_sem=recv_sem,
        device_id=partner,
        device_id_type=MESH,
    )


def column(length, start, rows):
    return lax.broadcasted_iota(I32, (rows, 1), 0) + start < length


def hat_of(values):
    center = values - jnp.mean(values, axis=-1, keepdims=True)
    inv_std = lax.rsqrt(jnp.mean(center * center, axis=-1, keepdims=True) + EPSILON)
    return center * inv_std, inv_std


def norm_pull(grad, normed, inv_std, gain):
    grad_hat = grad * gain
    return inv_std * (
        grad_hat
        - jnp.mean(grad_hat, axis=-1, keepdims=True)
        - normed * jnp.mean(grad_hat * normed, axis=-1, keepdims=True)
    )


def padded_head(block, odd):
    zero = jnp.zeros((HDIM, block.shape[1]), block.dtype)
    if odd:
        return jnp.concatenate([zero, block], axis=0)
    return jnp.concatenate([block, zero], axis=0)


ROW_CHUNKS = 4
CHUNK = HALF // ROW_CHUNKS


SLOTS = 72
V_EARLY = 48
V_UP, V_DOWN, V_GAIN2, V_BIAS2, V_OUT, V_GAIN1, V_BIAS1, V_QUERY, V_VALUE = (
    0, 24, 30, 36, 42, 48, 54, 60, 66,
)
F_BASE, F_ROWS = 64, 1152
A_BASE, A_ROWS = 32, 576


class Part:
    def __init__(self, place, order, fixed, rows, local, landing, sems, finish):
        self.place, self.order, self.fixed, self.rows = place, order, fixed, rows
        self.local, self.landing, self.sems, self.finish = local, landing, sems, finish
        self.first, self.count = 0, 2 ** sum(name not in fixed for name in order)
        self.active, self.step, self.sent = None, 0, []

    @staticmethod
    def landing_blocks(order, fixed):
        count, sizes = 2 ** sum(name not in fixed for name in order), []
        for name in order:
            count = count if name in fixed else count // 2
            sizes.append(count)
        return sizes

    def copy(self, step, start, count):
        return remote(
            self.local.at[pl.ds(start, count)],
            self.landing[step],
            self.sems.at[0, step],
            self.sems.at[1, step],
            self.place.partner[self.order[step]],
        )

    def plan(self):
        name = self.order[self.step]
        mine = self.place.bit[name]
        if name in self.fixed:
            away = both(self.active, mine != self.fixed[name])
            home = both(self.active, mine == self.fixed[name])
            return self.copy(self.step, self.first, self.count), away, home
        half = self.count // 2
        return self.copy(self.step, self.first + (1 - mine) * half, half), self.active, self.active

    def launch(self):
        copy, sends, _ = self.plan()
        when(sends, copy.start)
        self.sent.append((copy, sends))

    def tick(self):
        copy, _, takes = self.plan()
        name = self.order[self.step]
        if name not in self.fixed:
            self.count //= 2
            self.first = self.first + self.place.bit[name] * self.count
        last = self.step == len(self.order) - 1
        kept = self.local.at[pl.ds(self.first, self.count)]
        landed = self.landing[self.step]
        self.active = takes
        self.step += 1
        following = None if last else self.plan()

        def body():
            copy.wait_recv()
            if last:
                self.finish(kept[0].astype(F32) + landed[0].astype(F32))
                return
            kept[...] = kept[...] + landed[...]
            when(
                None
                if following[1] is self.active
                else self.place.bit[self.order[self.step]] != self.fixed[self.order[self.step]],
                following[0].start,
            )

        when(takes, body)
        if not last:
            self.sent.append(following[:2])

    @property
    def done(self):
        return self.step == len(self.order)

    def drain(self):
        for copy, sends in self.sent:
            when(sends, copy.wait_send)


DOWN, UP, OUT, LOW, HIGH = range(5)

ORDERS = {
    (DOWN, 0): (Y, Z0, X, Z1),
    (DOWN, 1): (Z0, X, Y, Z1),
    (DOWN, 2): (Z0, X, Y, Z1),
    (DOWN, 3): (X, Y, Z0, Z1),
    (UP, 0): (X, Z0, Y, Z1),
    (UP, 1): (X, Z0, Z1, Y),
    (UP, 2): (Y, Z0, X, Z1),
    (UP, 3): (Z0, X, Y, Z1),
    (OUT, 0): (X, Y, Z1, Z0),
    (LOW, 0): (Y, Z1, Z0, X),
    (LOW, 1): (Y, X, Z0, Z1),
    (LOW, 2): (X, Z0, Y, Z1),
    (HIGH, 0): (X, Z1, Y, Z0),
    (HIGH, 1): (Z0, Y, X, Z1),
    (HIGH, 2): (X, Z1, Y, Z0),
}


def part_plans():
    plans = {}
    for j in range(4):
        plans[DOWN, j] = (ORDERS[DOWN, j], {Z1: 1, Z0: j // 2, X: j % 2}, 192)
        plans[UP, j] = (ORDERS[UP, j], {Z1: 0}, 48)
    plans[OUT, 0] = (ORDERS[OUT, 0], {Z1: 1, Z0: 1}, 96)
    for p in range(3):
        plans[LOW, p] = (ORDERS[LOW, p], {Z1: 0}, 32)
        plans[HIGH, p] = (ORDERS[HIGH, p], {Z1: 1, Z0: 0}, 32)
    return plans


NORM2, PROJECT, PAIRS, QKV, NORM1, END = 16, 17, 18, 24, 25, 26
IDS, VEC, LATE, COUNT, EDGE = range(5)

SCHEDULE = {
    0: (IDS,),
    4: (IDS,),
    13: (IDS,),
    14: ((DOWN, 0),),
    18: (IDS,),
    19: (VEC, (DOWN, 3), (DOWN, 1), (DOWN, 2),),
    20: ((DOWN, 0), (UP, 0), IDS, (OUT, 0), (UP, 2), VEC,),
    22: ((OUT, 0), (UP, 1), VEC,),
    25: (VEC,),
    26: ((HIGH, 0), (DOWN, 3), (LOW, 0), (DOWN, 2), COUNT, (UP, 2), (LOW, 1), (HIGH, 2), (DOWN, 2), (DOWN, 3), (DOWN, 1), LATE, (UP, 3), (HIGH, 0), (UP, 1), (HIGH, 1), (LOW, 0), (UP, 2), (UP, 3), (HIGH, 2), (LOW, 1), (HIGH, 1), (UP, 0), (LOW, 2), LATE, (UP, 3), (DOWN, 1), (UP, 1), (LOW, 0), (DOWN, 0), (HIGH, 1), (HIGH, 0), (UP, 2), (OUT, 0), (LOW, 2), (UP, 0), LATE, (DOWN, 2), (UP, 1), (UP, 0), (DOWN, 3), (HIGH, 0), (LOW, 2), (HIGH, 2), (DOWN, 1), (LOW, 1), LATE, (DOWN, 0), (LOW, 2), (OUT, 0), (UP, 3), (HIGH, 2), EDGE, VEC, (LOW, 0), (LOW, 1), LATE, (HIGH, 1),),
}


class Scratch(typing.NamedTuple):
    x_recv: typing.Any
    lengths: typing.Any
    row_sem: typing.Any
    x_sem: typing.Any
    kv_sem: typing.Any
    len_sem: typing.Any
    cot_sem: typing.Any
    qkv: typing.Any
    out: typing.Any
    up: typing.Any
    down: typing.Any
    e: typing.Any
    a2: typing.Any
    q: typing.Any
    k: typing.Any
    v: typing.Any
    ot: typing.Any
    ft: typing.Any
    a1t: typing.Any
    a2t: typing.Any
    h: typing.Any
    y: typing.Any
    mid: typing.Any
    dh: typing.Any
    lse: typing.Any
    pair_send: typing.Any
    pair_recv: typing.Any
    flat_f: typing.Any
    flat_a: typing.Any
    vec: typing.Any
    vec_recv: typing.Any
    ids: typing.Any
    down_send: typing.Any
    up_send: typing.Any
    out_send: typing.Any
    qkv_send: typing.Any
    local: typing.Any
    landing: typing.Any
    sems: typing.Any
    load_sem: typing.Any
    core_sem: typing.Any
    pair_sem: typing.Any
    vec_sem: typing.Any
    ids_sem: typing.Any
    edge_sem: typing.Any
    result_sem: typing.Any


def backward_scratch():
    vmem, dma = pltpu.VMEM, pltpu.SemaphoreType.DMA
    low, low_t, full = vmem((HALF, WIDE), BF16), vmem((WIDE, HALF), BF16), vmem((HALF, WIDE), F32)
    plans = part_plans()
    return Scratch(
        x_recv=low,
        lengths=vmem((2, 8, 128), I32),
        row_sem=dma((ROW_CHUNKS, 6)),
        x_sem=dma((2, ROW_CHUNKS)),
        kv_sem=dma((2, 2, ROW_CHUNKS)),
        len_sem=dma((2,)),
        cot_sem=dma((2,)),
        qkv=vmem((WIDE, 3 * WIDE), BF16),
        out=vmem((WIDE, WIDE), BF16),
        up=vmem((WIDE, 4 * WIDE), BF16),
        down=vmem((4 * WIDE, WIDE), BF16),
        e=low,
        a2=low,
        q=low,
        k=vmem((2 * HALF, WIDE), BF16),
        v=vmem((2 * HALF, WIDE), BF16),
        ot=low_t,
        ft=vmem((2, WIDE, HALF), BF16),
        a1t=vmem((2, WIDE // 2, HALF), BF16),
        a2t=vmem((2, WIDE // 2, HALF), BF16),
        h=full,
        y=full,
        mid=full,
        dh=full,
        lse=vmem((16, HALF), F32),
        pair_send=vmem((2, 6, HALF, 128), BF16),
        pair_recv=vmem((2, 6, HALF, 128), BF16),
        flat_f=vmem((F_BASE + F_ROWS + 64, 128), F32),
        flat_a=vmem((A_BASE + A_ROWS + 32, 128), F32),
        vec=[vmem((6, V_EARLY, 128), F32), vmem((6, SLOTS - V_EARLY, 128), F32)],
        vec_recv=[vmem((5, V_EARLY, 128), F32), vmem((5, SLOTS - V_EARLY, 128), F32)],
        ids=vmem((32, 8, 128), I32),
        down_send=vmem((2, 2, 192, WIDE), BF16),
        up_send=vmem((2, 8, 48, WIDE), BF16),
        out_send=vmem((4, 96, WIDE), BF16),
        qkv_send=vmem((2, 12, 32, WIDE), BF16),
        local=[
            [vmem((2, 192, WIDE), BF16)] * 4,
            [vmem((8, 48, WIDE), BF16)] * 4,
            [vmem((4, 96, WIDE), BF16)],
            [vmem((12, 32, WIDE), BF16)] * 3,
        ],
        landing={
            key: [vmem((count, rows, WIDE), BF16) for count in Part.landing_blocks(order, fixed)]
            for key, (order, fixed, rows) in plans.items()
        },
        sems={key: dma((2, 4)) for key in plans},
        load_sem=dma((24,)),
        core_sem=dma((2, 12)),
        pair_sem=dma((2, 2, 6)),
        vec_sem=[dma((2, 5)), dma((2, 5))],
        ids_sem=dma((2, 5)),
        edge_sem=dma((2, 4)),
        result_sem=dma((2, 3)),
    )


STAGES = (CORE, X, Y, Z0, Z1)


def layer_kernel(*refs):
    rows_in = refs[:6]
    (
        cot_in, qkv_in, out_in, up_in, down_in, gain1, bias1, query_bias, value_bias, out_bias,
        gain2, bias2, up_bias, down_bias, gene_ids, lens,
    ) = refs[6:22]
    output_o, rows_o, attn_o, ffn_o, counts_o, x_o = refs[22:28]
    s = jax.tree.unflatten(jax.tree.structure(backward_scratch()), refs[28:])
    place = Place()
    core, y_bit = place.core, place.y
    mate, across = place.partner[CORE], place.partner[DIAG]
    greeted = greet(place, range(8))
    load_sem = s.load_sem

    def load(n, src, dst):
        copy = pltpu.make_async_copy(src, dst, load_sem.at[n])
        copy.start()
        return copy

    def load_up(j):
        cols = pl.ds(WIDE * j, WIDE)
        return load(4 + 2 * j, up_in.at[:, cols], s.up.at[:, cols])

    def load_down(j):
        cols = pl.ds(WIDE * j, WIDE)
        return load(5 + 2 * j, down_in.at[cols], s.down.at[cols])

    def rows_at(chunk):
        return pl.ds(chunk * CHUNK, CHUNK)

    held = [s.down.at[pl.ds(HALF * i, HALF)] for i in range(6)]
    loads = [
        [
            pltpu.make_async_copy(
                rows_in[i].at[rows_at(r)], held[i].at[rows_at(r)], s.row_sem.at[r, i]
            )
            for i in range(6)
        ]
        for r in range(ROW_CHUNKS)
    ]
    for group in loads:
        for copy in group:
            copy.start()
    load_qkv = load(21, qkv_in, s.qkv)
    load_out = load(0, out_in, s.out)
    weights_up = {j: load_up(j) for j in (2, 3)}

    s.lengths[0] = jnp.full((8, 128), lens[0], I32)
    greeted()
    send_len = remote(s.lengths.at[0], s.lengths.at[1], s.len_sem.at[0], s.len_sem.at[1], mate)
    send_len.start()

    h, y, mid, dh, e = s.h, s.y, s.mid, s.dh, s.e
    x_send = s.up.at[pl.ds(0, HALF), pl.ds(0, WIDE)]
    swaps = [
        remote(
            x_send.at[rows_at(r)], s.x_recv.at[rows_at(r)], s.x_sem.at[0, r], s.x_sem.at[1, r], across
        )
        for r in range(ROW_CHUNKS)
    ]
    for r in range(ROW_CHUNKS):
        for copy in loads[r]:
            copy.wait()
        total = held[0][rows_at(r)].astype(F32)
        for i in range(1, 6):
            total = total + held[i][rows_at(r)].astype(F32)
        h[rows_at(r)] = total

        @pl.when(place.moves)
        def _():
            x_send[rows_at(r)] = h[rows_at(r)].astype(BF16)
            swaps[r].start()

    weights_down = {j: load_down(j) for j in range(4)}
    load_qkv.wait()
    send_len.wait()
    length = jnp.where(place.stays, s.lengths[0], s.lengths[1])[0:1, 0:1]
    live_own = column(length, core * HALF, HALF)
    live_far = column(length, (1 - core) * HALF, HALF)

    key_first = None
    sends = []
    for r in range(ROW_CHUNKS):

        @pl.when(place.moves)
        def _():
            swaps[r].wait_recv()
            h[rows_at(r)] = s.x_recv[rows_at(r)].astype(F32)

        normed, _ = hat_of(h[rows_at(r)])
        low = (normed * gain1[...].reshape(1, WIDE) + bias1[...].reshape(1, WIDE)).astype(BF16)
        s.a2[rows_at(r)] = low
        projected = mm(low, s.qkv[...])
        scaled = (projected[:, :WIDE] + query_bias[...].reshape(1, WIDE)) * (LOG2E * HDIM**-0.5)
        s.q[rows_at(r)] = scaled.astype(BF16)
        keys = projected[:, WIDE : 2 * WIDE]
        values = projected[:, 2 * WIDE :] + value_bias[...].reshape(1, WIDE)
        if r == 0:
            key_first = keys[0:1]
        live = column(length, core * HALF + r * CHUNK, CHUNK)
        s.k[rows_at(r)] = jnp.where(live, keys, key_first).astype(BF16)
        s.v[rows_at(r)] = jnp.where(live, values, 0.0).astype(BF16)
        for which, ref in enumerate((s.k, s.v)):
            copy = remote(
                ref.at[rows_at(r)], ref.at[pl.ds(HALF + r * CHUNK, CHUNK)],
                s.kv_sem.at[0, which, r], s.kv_sem.at[1, which, r], mate,
            )
            copy.start()
            sends.append(copy)

    load_e = pltpu.make_async_copy(cot_in, e, load_sem.at[1])
    swap_cot = remote(cot_in, e, s.cot_sem.at[0], s.cot_sem.at[1], across)
    pl.when(place.stays)(load_e.start)
    pl.when(place.moves)(swap_cot.start)
    keep_x = pltpu.make_async_copy(h, x_o, load_sem.at[22])
    keep_x.start()

    qt_first = s.ft.at[0]
    qt_first[...] = s.q[...].T
    flipped = s.a2[...].T
    for c in range(2):
        for m in range(6):
            s.a1t[c, 64 * m : 64 * m + 64] = flipped[128 * m + 64 * c : 128 * m + 64 * c + 64]
    for copy in sends:
        copy.wait_recv()

    @pl.when(place.moves)
    def _():
        for swap in swaps:
            swap.wait_send()

    values_t = s.up.at[:, pl.ds(0, 2 * HALF)]
    values_t[...] = s.v[...].T
    slot = lax.broadcasted_iota(I32, (16, 2 * HALF), 1)
    slot = jnp.where(slot < HALF, slot + core * HALF, slot - core * HALF)
    live_row = (slot < length).astype(F32).astype(BF16)
    heads = WIDE // HDIM

    def score(head):
        return mm(
            s.k[:, 128 * (head // 2) : 128 * (head // 2) + 128],
            padded_head(qt_first[HDIM * head : HDIM * head + HDIM], head % 2),
        )

    scores = score(0)
    for head in range(heads):
        rows = slice(HDIM * head, HDIM * head + HDIM)
        later = score(head + 1) if head + 1 < heads else None
        top = jnp.max(scores, axis=0, keepdims=True)
        probs = jnp.exp2(scores - top).astype(BF16)
        context = mm(jnp.concatenate([values_t[rows], live_row], axis=0), probs)
        mass = context[HDIM : HDIM + 1]
        s.ot[rows] = (context[:HDIM] / mass).astype(BF16)
        s.lse[head : head + 1] = top + jnp.log2(mass)
        scores = later
    for j in (0, 1):
        weights_up[j] = load_up(j)

    def put_vec(slot, row):
        late = int(slot >= V_EARLY)
        slot -= late * V_EARLY
        for t in range(row.shape[1] // 128):
            s.vec[late][0, slot + t : slot + t + 1] = row[:, 128 * t : 128 * t + 128]

    def flat_store(ref, base, stride, value, skip=0):
        for t in range(WIDE // 128):
            at = pl.ds(base + t + t // 2 * skip, value.shape[0], stride=stride)
            ref[at, :] = value[:, 128 * t : 128 * t + 128]

    parts = {}
    for key, (order, fixed, rows) in part_plans().items():
        kind, n = key
        if kind == DOWN:
            local = s.local[DOWN][n]
            finish = functools.partial(flat_store, s.flat_f, F_BASE, 6)
        elif kind == UP:
            local = s.local[UP][n]
            finish = functools.partial(flat_store, s.flat_f, F_BASE + 6 * n, 24)
        elif kind == OUT:
            local = s.local[OUT][0]
            finish = functools.partial(flat_store, s.flat_a, A_BASE, 6)
        else:
            whole = s.local[LOW][n]
            local = whole.at[pl.ds(0, 8)] if kind == LOW else whole.at[pl.ds(8, 4)]
            finish = functools.partial(flat_store, s.flat_a, A_BASE + 2 * n, 18, skip=4)
        landing = s.landing[key]
        parts[key] = Part(place, order, fixed, rows, local, landing, s.sems[key], finish)

    vec_copies = [[], []]

    def vec_launch(late):
        n = len(vec_copies[late])
        copy = remote(
            s.vec[late].at[n], s.vec_recv[late].at[n],
            s.vec_sem[late].at[0, n], s.vec_sem[late].at[1, n],
            place.partner[STAGES[n]],
        )
        copy.start()
        vec_copies[late].append(copy)

    def vec_tick(late):
        n = len(vec_copies[late])
        vec_copies[late][-1].wait_recv()
        s.vec[late][n] = s.vec[late][n - 1] + s.vec_recv[late][n - 1]
        if n < 5:
            vec_launch(late)

    edges = []

    def edge_launch(ref, base, rows):
        end = base + rows
        for src, dst, size, to in ((end - 24, base - 24, 24, NEXT), (base, end, 32, PREV)):
            n = len(edges)
            copy = remote(
                ref.at[pl.ds(src, size)], ref.at[pl.ds(dst, size)],
                s.edge_sem.at[0, n], s.edge_sem.at[1, n], place.partner[to],
            )
            copy.start()
            edges.append(copy)

    def count(n, total):
        high_row = lax.broadcasted_iota(I32, (288, 128), 0)
        low_row = lax.broadcasted_iota(I32, (128, 128), 0)
        tile = s.ids[n]
        for r in range(0, 4, 2):
            high = [(high_row == (tile[r + i : r + i + 1] >> 7)).astype(F32).astype(BF16) for i in range(2)]
            low = [(low_row == (tile[r + i : r + i + 1] & 127)).astype(F32).astype(BF16) for i in range(2)]
            total = total + mm(jnp.concatenate(high, axis=1), jnp.concatenate(low, axis=1), NT)
        return total

    def count_all():
        counts_o[...] = lax.fori_loop(0, 32, count, jnp.zeros((288, 128), F32)).astype(I32)

    special = {
        IDS: lambda: ids_tick(),
        VEC: lambda: vec_tick(0),
        LATE: lambda: vec_tick(1),
        COUNT: count_all,
        EDGE: lambda: edge_launch(s.flat_f, F_BASE, F_ROWS),
    }

    def pause(hook):
        for entry in SCHEDULE.get(hook, ()):
            if isinstance(entry, tuple):
                parts[entry].tick()
            else:
                special[entry]()

    core_copies = []

    def core_send(src, dst):
        n = len(core_copies)
        copy = remote(src, dst, s.core_sem.at[0, n], s.core_sem.at[1, n], mate)
        copy.start()
        core_copies.append(copy)
        return copy

    def put_blocks(ref, key, value):
        order, fixed, rows = part_plans()[key]
        free = [name for name in order if name not in fixed]
        natural = [name for name in (Z1, Z0, X, Y) if name not in fixed]
        for m in range(2 ** len(free)):
            bits = {name: (m >> (len(natural) - 1 - i)) & 1 for i, name in enumerate(natural)}
            at = sum(bits[name] << (len(free) - 1 - i) for i, name in enumerate(free))
            ref[at] = value[m * rows : m * rows + rows]

    load_out.wait()
    keep_x.wait()
    gain2_row, bias2_row = gain2[...].reshape(1, WIDE), bias2[...].reshape(1, WIDE)
    h[...] = h[...] + mm(s.ot[...].T, s.out[...]) + out_bias[...].reshape(1, WIDE)
    for r in range(4):
        at = pl.ds(128 * r, 128)
        normed, _ = hat_of(h[at])
        s.a2[at] = (normed * gain2_row + bias2_row).astype(BF16)
        y[at] = h[at] + down_bias[...].reshape(1, WIDE)
    flipped = s.a2[...].T
    for c in range(2):
        for m in range(4):
            s.a2t[c, 96 * m : 96 * m + 96] = flipped[192 * m + 96 * c : 192 * m + 96 * c + 96]

    own_len = jnp.full((1, 128), lens[0], I32)
    slots = lax.broadcasted_iota(I32, (1, 128), 1) + y_bit * HALF
    ids = s.ids
    here = sum(place.bit[name] * 2**stage for stage, name in enumerate(STAGES))
    tile = [
        jnp.where(slots + 128 * r < own_len, gene_ids[0:1, 128 * r : 128 * r + 128], -1) for r in range(4)
    ]
    ids[pl.ds(here, 1)] = jnp.concatenate(tile + [jnp.full((4, 128), -1, I32)], axis=0)[None]
    ids_copies = []

    def ids_launch(stage):
        size = 2**stage
        at = pl.ds((here // size) * size, size)
        copy = remote(
            ids.at[at], ids.at[at], s.ids_sem.at[0, stage], s.ids_sem.at[1, stage],
            place.partner[STAGES[stage]],
        )
        copy.start()
        ids_copies.append(copy)

    def ids_tick():
        ids_copies[-1].wait_recv()
        if len(ids_copies) < 5:
            ids_launch(len(ids_copies))

    ids_launch(0)

    pl.when(place.stays)(load_e.wait)
    pl.when(place.moves)(swap_cot.wait_recv)
    put_vec(V_DOWN, jnp.sum(e[...].astype(F32), axis=0, keepdims=True))
    half_rows = WIDE // 2
    theirs = pl.ds(pl.multiple_of((1 - core) * half_rows, half_rows), half_rows)
    ours = pl.ds(pl.multiple_of(core * half_rows, half_rows), half_rows)

    def settle(j, grad, down_copy, up_copy):
        own = mm(s.ft[j % 2, ours], e[...]).reshape(2, 192, WIDE)
        down_copy.wait_recv()
        local = s.local[DOWN][j]
        local[...] = (own + local[...].astype(F32)).astype(BF16)
        parts[DOWN, j].launch()
        own = mm(s.a2t[core], grad)
        up_copy.wait_recv()
        add_blocks(s.local[UP][j], (UP, j), own)
        parts[UP, j].launch()

    waiting = None
    for j in range(4):
        cols = pl.ds(WIDE * j, WIDE)
        weights_up[j].wait()
        weights_down[j].wait()
        inner = mm(s.a2[...], s.up[:, cols]) + up_bias[WIDE * j : WIDE * j + WIDE].reshape(1, WIDE)
        phi = 0.5 * (1.0 + lax.erf(inner * 0.7071067811865476))
        slope = phi + inner * jnp.exp2(inner * inner * (-0.5 * LOG2E)) * 0.3989422804014327
        active = (inner * phi).astype(BF16)
        s.ft[j % 2] = active.T
        if j:
            settle(j - 1, *waiting)
        if j >= 2:
            core_copies[2 * j - 4].wait_send()
            core_copies[2 * j - 3].wait_send()
        sent = s.down_send.at[j % 2]
        sent[...] = mm(s.ft[j % 2, theirs], e[...]).astype(BF16).reshape(2, 192, WIDE)
        down_copy = core_send(sent, s.local[DOWN][j])
        pause(4 * j)
        grad = (mm(e[...], s.down[cols], NT) * slope).astype(BF16)
        sent = s.up_send.at[j % 2]
        put_blocks(sent, (UP, j), mm(s.a2t[1 - core], grad).astype(BF16))
        up_copy = core_send(sent, s.local[UP][j])
        pause(4 * j + 1)
        put_vec(V_UP + 6 * j, jnp.sum(grad.astype(F32), axis=0, keepdims=True))
        back = mm(grad, s.up[:, cols], NT)
        mid[...] = back if j == 0 else mid[...] + back
        y[...] = y[...] + mm(active, s.down[cols])
        pause(4 * j + 2)
        waiting = (grad, down_copy, up_copy)
    down = s.down
    grad_h, grad_o, grad_rows, *grads = [down.at[pl.ds(HALF * n, HALF)] for n in range(6)]
    output = s.a2
    sums = [jnp.zeros((1, WIDE), F32) for _ in range(3)]
    for r in range(4):
        at = pl.ds(128 * r, 128)
        output[at] = y[at].astype(BF16)
        normed, inv_std = hat_of(h[at])
        grad = mid[at]
        sums[0] += jnp.sum(grad * normed, axis=0, keepdims=True)
        sums[1] += jnp.sum(grad, axis=0, keepdims=True)
        total = e[at].astype(F32) + norm_pull(grad, normed, inv_std, gain2_row)
        dh[at] = total
        low = total.astype(BF16)
        grad_h[at] = low
        sums[2] += jnp.sum(low.astype(F32), axis=0, keepdims=True)
    put_vec(V_GAIN2, sums[0])
    put_vec(V_BIAS2, sums[1])
    put_vec(V_OUT, sums[2])

    result_copies = []

    def give_back(n, src, dst):
        keep = pltpu.make_async_copy(src, dst, s.result_sem.at[n, 2])
        swap = remote(
            src, dst, s.result_sem.at[n, 0], s.result_sem.at[n, 1], place.partner[DIAG]
        )
        pl.when(place.stays)(keep.start)
        pl.when(place.moves)(swap.start)
        result_copies.append((keep, swap))

    settle(3, *waiting)
    vec_launch(0)
    give_back(0, output, output_o)
    pause(NORM2)

    def out_rows(c):
        return jnp.concatenate(
            [s.ot[pl.ds(pl.multiple_of(384 * x + 192 * c, 192), 192)] for x in range(2)], axis=0
        )

    put_blocks(s.out_send, (OUT, 0), mm(out_rows(1 - core), grad_h[...]).astype(BF16))
    out_copy = core_send(s.out_send, s.local[OUT][0])
    grad_o[...] = mm(grad_h[...], s.out[...], NT).astype(BF16)
    up = s.up
    grad_ot, grad_qt, qt = [up.at[:, pl.ds(HALF * n, HALF)] for n in range(3)]
    grad_ot[...] = grad_o[...].T
    load_x = pltpu.make_async_copy(x_o, y, load_sem.at[20])
    load_x.start()
    qt[...] = s.q[...].T
    own = mm(out_rows(core), grad_h[...])
    out_copy.wait_recv()
    add_blocks(s.local[OUT][0], (OUT, 0), own)
    parts[OUT, 0].launch()
    pause(PROJECT)

    live = jnp.concatenate([live_own, live_far], axis=0)
    lane = lax.broadcasted_iota(I32, (1, 128), 1)
    dk, dv = h, mid
    pair_copies, qkv_copies = [], []

    def far_qkv(g):
        grad = grads[g]
        grad[:, :256] = grad_qt[256 * g : 256 * g + 256].T
        for i in range(2):
            j = 2 * g + i
            for n, mine in enumerate((dk, dv)):
                pair_copies[2 * j + n].wait_recv()
                total = mine[:, 128 * j : 128 * j + 128] + s.pair_recv[n, j].astype(F32)
                start = 256 * (n + 1) + 128 * i
                grad[:, start : start + 128] = jnp.where(live_own, total, 0.0).astype(BF16)
        sent = s.qkv_send.at[g % 2]
        if g == 2:
            qkv_copies[0].wait_send()
        value = mm(s.a1t[1 - core], grad[...]).astype(BF16)
        put_blocks(sent.at[pl.ds(0, 8)], (LOW, g), value[:256])
        put_blocks(sent.at[pl.ds(8, 4)], (HIGH, g), value[256:])
        qkv_copies.append(core_send(sent, s.local[LOW][g]))

    def settle_qkv(g):
        own = mm(s.a1t[core], grads[g][...])
        qkv_copies[g].wait_recv()
        local = s.local[LOW][g]
        add_blocks(local.at[pl.ds(0, 8)], (LOW, g), own[:256])
        add_blocks(local.at[pl.ds(8, 4)], (HIGH, g), own[256:])
        parts[LOW, g].launch()
        parts[HIGH, g].launch()

    def pull_qkv(g):
        grad, at = grads[g], lambda p: slice(WIDE * p + 256 * g, WIDE * p + 256 * g + 256)
        total = mm(grad[:, :256], s.qkv[:, at(0)], NT)
        total = total + mm(grad[:, 256:512], s.qkv[:, at(1)], NT)
        return total + mm(grad[:, 512:], s.qkv[:, at(2)], NT)

    for j in range(WIDE // 128):
        at = slice(128 * j, 128 * j + 128)
        keys, values = s.k[:, at], s.v[:, at]
        keys_t = jnp.where(live, keys, jnp.zeros_like(keys)).T
        grad_keys = grad_values = None
        for i in range(2):
            head = 2 * j + i
            rows = slice(HDIM * head, HDIM * head + HDIM)
            mine = lane // HDIM == i
            scores = mm(keys, padded_head(qt[rows], i))
            probs = jnp.exp2(scores - s.lse[head : head + 1])
            grad_ot_head = grad_ot[rows]
            grad_probs = mm(values, padded_head(grad_ot_head, i))
            delta = jnp.sum(
                grad_ot_head.astype(F32) * s.ot[rows].astype(F32), axis=0, keepdims=True
            )
            grad_scores = (probs * (grad_probs - delta)).astype(BF16)
            queries = jnp.where(mine, s.q[:, at], jnp.zeros((), BF16))
            grad_out = jnp.where(mine, grad_o[:, at], jnp.zeros((), BF16))
            more = mm(probs.astype(BF16), grad_out)
            grad_values = more if i == 0 else grad_values + more
            more = mm(grad_scores, queries)
            grad_keys = more if i == 0 else grad_keys + more
            grad_qt[rows] = (mm(keys_t[HDIM * i : HDIM * i + HDIM], grad_scores) * HDIM**-0.5).astype(BF16)
        grad_keys = grad_keys * LN2
        dk[:, at] = grad_keys[:HALF]
        dv[:, at] = grad_values[:HALF]
        for n, value in enumerate((grad_keys, grad_values)):
            s.pair_send[n, j] = value[HALF:].astype(BF16)
            copy = remote(
                s.pair_send.at[n, j], s.pair_recv.at[n, j],
                s.pair_sem.at[0, n, j], s.pair_sem.at[1, n, j], mate,
            )
            copy.start()
            pair_copies.append(copy)
        if j and j % 2 == 0:
            far_qkv(j // 2 - 1)
        elif j > 1:
            settle_qkv(j // 2 - 1)
        pause(PAIRS + j)
    back = pull_qkv(0) + pull_qkv(1)
    far_qkv(2)
    pause(QKV)

    mid[...] = back + pull_qkv(2)
    load_x.wait()
    gain1_row = gain1[...].reshape(1, WIDE)
    sums = [jnp.zeros((1, WIDE), F32) for _ in range(2)]
    for r in range(4):
        at = pl.ds(128 * r, 128)
        normed, inv_std = hat_of(y[at])
        grad = mid[at]
        sums[0] += jnp.sum(grad * normed, axis=0, keepdims=True)
        sums[1] += jnp.sum(grad, axis=0, keepdims=True)
        grad_rows[at] = (dh[at] + norm_pull(grad, normed, inv_std, gain1_row)).astype(BF16)
    put_vec(V_GAIN1, sums[0])
    put_vec(V_BIAS1, sums[1])
    give_back(1, grad_rows, rows_o)
    for p, slot in enumerate((V_QUERY, None, V_VALUE)):
        if p != 1:
            total = [jnp.sum(grad[:, 256 * p : 256 * p + 256].astype(F32), axis=0, keepdims=True) for grad in grads]
            put_vec(slot, jnp.concatenate(total, axis=1))
    vec_launch(1)
    settle_qkv(2)
    pause(NORM1)

    pause(END)
    while any(not part.done for part in parts.values()):
        for part in parts.values():
            if not part.done:
                part.tick()
    edge_launch(s.flat_a, A_BASE, A_ROWS)
    for copy in edges:
        copy.wait()
    total = jnp.concatenate([s.vec[0][5], s.vec[1][5]], axis=0)
    flat_f, flat_a = s.flat_f, s.flat_a
    me = place.index
    f_end, a_end = F_BASE + F_ROWS, A_BASE + A_ROWS

    @pl.when(me == 0)
    def _():
        flat_f[F_BASE - 12 : F_BASE] = total[V_GAIN2 : V_GAIN2 + 12]
        flat_a[A_BASE - 12 : A_BASE] = total[V_GAIN1 : V_GAIN1 + 12]

    @pl.when(me == 15)
    def _():
        flat_f[f_end : f_end + 24] = total[V_UP : V_UP + 24]

    @pl.when(me == 16)
    def _():
        flat_f[F_BASE - 24 : F_BASE] = total[V_UP : V_UP + 24]

    @pl.when(me == 23)
    def _():
        flat_a[a_end : a_end + 12] = total[V_QUERY : V_QUERY + 12]

    @pl.when(me == 31)
    def _():
        flat_f[f_end : f_end + 6] = total[V_DOWN : V_DOWN + 6]
        flat_f[f_end + 6 : f_end + 32] = jnp.zeros((26, 128), F32)
        flat_a[a_end : a_end + 6] = total[V_OUT : V_OUT + 6]
        flat_a[a_end + 6 : a_end + 32] = jnp.zeros((26, 128), F32)

    f_start = jnp.where(me < 16, F_BASE - 12 + 2 * me, F_BASE - 4 + 2 * (me - 16))
    a_start = jnp.where(me < 24, A_BASE - 12 + me, A_BASE + me - 24)
    ffn_o[...] = flat_f[pl.ds(f_start, ffn_o.shape[0]), :]
    attn_o[...] = flat_a[pl.ds(a_start, attn_o.shape[0]), :]

    for part in parts.values():
        part.drain()
    core_copies[4].wait_send()
    for n in (5, 6, 7, 8, 10, 11):
        core_copies[n].wait_send()
    for copy in sends + pair_copies + ids_copies + vec_copies[0] + vec_copies[1]:
        copy.wait_send()
    pl.when(place.moves)(swap_cot.wait_send)
    for keep, swap in result_copies:
        pl.when(place.stays)(keep.wait)
        pl.when(place.moves)(swap.wait)


def add_blocks(ref, key, value):
    order, fixed, rows = part_plans()[key]
    free = [name for name in order if name not in fixed]
    natural = [name for name in (Z1, Z0, X, Y) if name not in fixed]
    for m in range(2 ** len(free)):
        bits = {name: (m >> (len(natural) - 1 - i)) & 1 for i, name in enumerate(natural)}
        at = sum(bits[name] << (len(free) - 1 - i) for i, name in enumerate(free))
        ref[at] = (ref[at].astype(F32) + value[m * rows : m * rows + rows]).astype(BF16)


def layer_call(rows, cotangent, weights, vectors, gene_ids, lengths, attn_units, ffn_units):
    any_spec = pl.BlockSpec(memory_space=pl.ANY)
    vmem = pl.BlockSpec(memory_space=pltpu.VMEM)
    shape = jax.ShapeDtypeStruct
    return pl.pallas_call(
        layer_kernel,
        out_shape=(
            shape((HALF, WIDE), BF16),
            shape((HALF, WIDE), BF16),
            shape((attn_units, 128), F32),
            shape((ffn_units, 128), F32),
            shape((288, 128), I32),
            shape((HALF, WIDE), F32),
        ),
        in_specs=[any_spec] * 11 + [vmem] * 10 + [pl.BlockSpec(memory_space=pltpu.SMEM)],
        out_specs=(any_spec, any_spec, vmem, vmem, vmem, any_spec),
        scratch_shapes=jax.tree.leaves(backward_scratch()),
        compiler_params=pltpu.CompilerParams(
            collective_id=0, has_side_effects=True, vmem_limit_bytes=64 * 2**20
        ),
        name="layer",
    )(*rows, cotangent, *weights, *vectors, gene_ids, lengths)


def hand_over_kernel(output_in, rows_in, attn_in, ffn_in, counts_in, output_o, rows_o, attn_o, ffn_o, counts_o, *scratch):
    *held, load_sem, store_sem = scratch
    pairs = ((output_in, output_o), (rows_in, rows_o), (attn_in, attn_o), (ffn_in, ffn_o))
    loads = [pltpu.make_async_copy(src, ref, load_sem.at[n]) for n, ((src, _), ref) in enumerate(zip(pairs, held))]
    stores = [pltpu.make_async_copy(ref, dst, store_sem.at[n]) for n, ((_, dst), ref) in enumerate(zip(pairs, held))]
    for copy in loads:
        copy.start()
    counts_o[...] = counts_in[...].reshape(-1)[: counts_o.shape[0]]
    for load, store in zip(loads, stores):
        load.wait()
        store.start()
    for store in stores:
        store.wait()


def hand_over_call(results):
    any_spec = pl.BlockSpec(memory_space=pl.ANY)
    vmem = pl.BlockSpec(memory_space=pltpu.VMEM)
    large = results[:4]
    return pl.pallas_call(
        hand_over_kernel,
        out_shape=tuple(jax.ShapeDtypeStruct(r.shape, r.dtype) for r in large)
        + (jax.ShapeDtypeStruct((VOCAB,), I32),),
        in_specs=[any_spec] * 4 + [vmem],
        out_specs=(any_spec,) * 4 + (vmem,),
        scratch_shapes=[pltpu.VMEM(r.shape, r.dtype) for r in large]
        + [pltpu.SemaphoreType.DMA((4,)), pltpu.SemaphoreType.DMA((4,))],
        name="hand_over",
    )(*results)


def on_device(
    row_gene,
    row_value,
    row_promoter,
    row_grn,
    row_coexp,
    row_family,
    lengths,
    gene_ids,
    norm1_gain,
    norm1_bias,
    qkv_weight,
    query_bias,
    value_bias,
    out_weight,
    out_bias,
    norm2_gain,
    norm2_bias,
    up_weight,
    up_bias,
    down_weight,
    down_bias,
    cotangent,
):
    rows = [
        member.reshape(HALF, WIDE)
        for member in (row_gene, row_value, row_promoter, row_grn, row_coexp, row_family)
    ]
    devices = lax.axis_size("dp") * lax.axis_size("seq")
    attn_len, ffn_len = gradient_lengths(WIDE, 4 * WIDE, devices)
    results = layer_call(
        rows,
        cotangent.reshape(HALF, WIDE),
        (qkv_weight, out_weight, up_weight, down_weight),
        (
            norm1_gain,
            norm1_bias,
            query_bias,
            value_bias,
            out_bias,
            norm2_gain,
            norm2_bias,
            up_bias,
            down_bias,
        ),
        gene_ids,
        lengths,
        attn_len // devices // 128,
        ffn_len // devices // 128,
    )[:5]
    output, grad_rows, attn, ffn, counts = hand_over_call(results)
    return (
        output.reshape(row_gene.shape),
        grad_rows.reshape(row_gene.shape),
        attn.reshape(-1),
        ffn.reshape(-1),
        counts,
    )


def gradient_lengths(width, hidden, devices):
    pad = lambda count: -(-count // (devices * 128)) * devices * 128
    return (
        pad(3 * width * width + width * width + 5 * width),
        pad(2 * width * hidden + 3 * width + hidden),
    )


def layer_norm(values_in, gain_vec, bias_vec):
    center = values_in - jnp.mean(values_in, axis=-1, keepdims=True)
    variance = jnp.mean(center * center, axis=-1, keepdims=True)
    inv_std = lax.rsqrt(variance + EPSILON)
    normed = center * inv_std
    return (normed * gain_vec + bias_vec, normed, inv_std)


def norm_back(grad_normed, normed, inv_std, gain_vec):
    grad_hat = grad_normed * gain_vec
    grad_gain = jnp.sum(grad_normed * normed, axis=0)
    grad_bias = jnp.sum(grad_normed, axis=0)
    grad_input = inv_std * (
        grad_hat
        - jnp.mean(grad_hat, axis=-1, keepdims=True)
        - normed * jnp.mean(grad_hat * normed, axis=-1, keepdims=True)
    )
    return (grad_input, grad_gain, grad_bias)


def gelu_exact(inner):
    return jax.nn.gelu(inner, approximate=False)


def padded_flat(members, multiple):
    flat = jnp.concatenate([member.reshape(-1) for member in members])
    total = -(-flat.shape[0] // multiple) * multiple
    return jnp.pad(flat, (0, total - flat.shape[0]))


def attend(queries, key_rows, value_rows, key_keep):
    cell_count, query_len, local_width = queries.shape
    head_count = local_width // HDIM
    block_rows = min(query_len, 512)
    block_count = query_len // block_rows
    scale = HDIM ** (-0.5)

    def one_cell(inputs):
        cell_query, cell_key, cell_value, cell_keep = inputs
        key_heads = cell_key.reshape(-1, head_count, HDIM)
        value_heads = cell_value.reshape(-1, head_count, HDIM)

        def one_block(query_block):
            scores = (
                jnp.einsum(
                    "qhd,khd->hqk", query_block, key_heads, preferred_element_type=jnp.float32
                )
                * scale
            )
            scores = jnp.where(cell_keep[None, None, :], scores, NEGATIVE)
            row_max = jnp.max(scores, axis=-1, keepdims=True)
            exp_scores = jnp.exp(scores - row_max)
            row_total = jnp.sum(exp_scores, axis=-1, keepdims=True)
            attn_probs = exp_scores / row_total
            context = jnp.einsum(
                "hqk,khd->qhd",
                attn_probs.astype(jnp.bfloat16),
                value_heads,
                preferred_element_type=jnp.float32,
            )
            return (
                context.reshape(block_rows, local_width),
                (row_max + jnp.log(row_total))[..., 0],
            )

        context, log_total = lax.map(
            one_block, cell_query.reshape(block_count, block_rows, head_count, HDIM)
        )
        return (context.reshape(query_len, local_width), log_total)

    return lax.map(one_cell, (queries, key_rows, value_rows, key_keep))


def attend_back(queries, key_rows, value_rows, key_keep, log_total, grad_context):
    cell_count, query_len, local_width = queries.shape
    head_count = local_width // HDIM
    block_rows = min(query_len, 512)
    block_count = query_len // block_rows
    scale = HDIM ** (-0.5)

    def one_cell(inputs):
        cell_query, cell_key, cell_value, cell_keep, cell_lse, cell_grad = inputs
        key_heads = cell_key.reshape(-1, head_count, HDIM)
        value_heads = cell_value.reshape(-1, head_count, HDIM)
        key_len = key_heads.shape[0]

        def one_block(running, block_in):
            query_block, lse_block, grad_block = block_in
            scores = (
                jnp.einsum(
                    "qhd,khd->hqk", query_block, key_heads, preferred_element_type=jnp.float32
                )
                * scale
            )
            scores = jnp.where(cell_keep[None, None, :], scores, NEGATIVE)
            attn_probs = jnp.exp(scores - lse_block[..., None])
            grad_probs = jnp.einsum(
                "qhd,khd->hqk", grad_block, value_heads, preferred_element_type=jnp.float32
            )
            grad_scores = (
                attn_probs * (grad_probs - jnp.sum(attn_probs * grad_probs, axis=-1, keepdims=True))
            ).astype(jnp.bfloat16)
            grad_query = (
                jnp.einsum(
                    "hqk,khd->qhd", grad_scores, key_heads, preferred_element_type=jnp.float32
                )
                * scale
            )
            grad_key = (
                running[0]
                + jnp.einsum(
                    "hqk,qhd->khd", grad_scores, query_block, preferred_element_type=jnp.float32
                )
                * scale
            )
            grad_value = running[1] + jnp.einsum(
                "hqk,qhd->khd",
                attn_probs.astype(jnp.bfloat16),
                grad_block,
                preferred_element_type=jnp.float32,
            )
            return ((grad_key, grad_value), grad_query.reshape(block_rows, local_width))

        zeros_start = jnp.zeros((key_len, head_count, HDIM), jnp.float32)
        (grad_key, grad_value), grad_query = lax.scan(
            one_block,
            (zeros_start, zeros_start),
            (
                cell_query.reshape(block_count, block_rows, head_count, HDIM),
                cell_lse,
                cell_grad.reshape(block_count, block_rows, head_count, HDIM),
            ),
        )
        return (
            grad_query.reshape(query_len, local_width),
            grad_key.reshape(key_len, local_width),
            grad_value.reshape(key_len, local_width),
        )

    return lax.map(one_cell, (queries, key_rows, value_rows, key_keep, log_total, grad_context))


def plain_on_device(
    row_gene,
    row_value,
    row_promoter,
    row_grn,
    row_coexp,
    row_family,
    lengths,
    gene_ids,
    norm1_gain,
    norm1_bias,
    qkv_weight,
    query_bias,
    value_bias,
    out_weight,
    out_bias,
    norm2_gain,
    norm2_bias,
    up_weight,
    up_bias,
    down_weight,
    down_bias,
    cotangent,
):
    cell_count, local_len, model_width = row_gene.shape
    row_count = cell_count * local_len
    seq_size = lax.axis_size("seq")
    multiple = lax.axis_size("dp") * seq_size * 128
    place = lax.axis_index("seq")
    positions = place * local_len + jnp.arange(local_len, dtype=jnp.int32)
    live_local = (positions[None, :] < lengths[:, None]).astype(jnp.int32)
    local_counts = jax.ops.segment_sum(
        live_local.reshape(-1), gene_ids.reshape(-1), num_segments=VOCAB
    )
    gene_counts = lax.psum(local_counts, ("dp", "seq"))
    summed = (
        row_gene.astype(jnp.float32)
        + row_value.astype(jnp.float32)
        + row_promoter.astype(jnp.float32)
        + row_grn.astype(jnp.float32)
        + row_coexp.astype(jnp.float32)
        + row_family.astype(jnp.float32)
    )
    summed = summed.reshape(row_count, model_width)
    normed_one, hat_one, inv_one = layer_norm(summed, norm1_gain, norm1_bias)
    normed_in = normed_one.astype(jnp.bfloat16)
    projected = jnp.dot(normed_in, qkv_weight, preferred_element_type=jnp.float32)
    query_full = projected[:, :model_width] + query_bias
    key_full = projected[:, model_width : 2 * model_width]
    value_full = projected[:, 2 * model_width :] + value_bias
    stacked = jnp.stack([query_full, key_full, value_full], axis=1).astype(jnp.bfloat16)
    stacked = stacked.reshape(cell_count, local_len, 3, model_width)
    full_len = local_len * seq_size
    key_keep = jnp.arange(full_len, dtype=jnp.int32)[None, :] < lengths[:, None]
    heads_in = lax.all_to_all(stacked, "seq", split_axis=3, concat_axis=1, tiled=True)
    query_att = heads_in[:, :, 0]
    key_att = heads_in[:, :, 1]
    value_att = heads_in[:, :, 2]
    context, log_total = attend(query_att, key_att, value_att, key_keep)
    context_local = lax.all_to_all(
        context.astype(jnp.bfloat16), "seq", split_axis=1, concat_axis=2, tiled=True
    )
    context_flat = context_local.reshape(row_count, model_width)
    hidden = (
        summed + jnp.dot(context_flat, out_weight, preferred_element_type=jnp.float32) + out_bias
    )
    normed_two, hat_two, inv_two = layer_norm(hidden, norm2_gain, norm2_bias)
    normed_mid = normed_two.astype(jnp.bfloat16)
    inner = jnp.dot(normed_mid, up_weight, preferred_element_type=jnp.float32) + up_bias
    activated, gelu_pull = jax.vjp(gelu_exact, inner)
    activated_low = activated.astype(jnp.bfloat16)
    result = (
        hidden + jnp.dot(activated_low, down_weight, preferred_element_type=jnp.float32) + down_bias
    )
    output = result.astype(jnp.bfloat16).reshape(cell_count, local_len, model_width)
    grad_out_low = cotangent.reshape(row_count, model_width)
    grad_out = grad_out_low.astype(jnp.float32)
    grad_down = jnp.einsum(
        "nf,nd->fd", activated_low, grad_out_low, preferred_element_type=jnp.float32
    )
    grad_down_bias = jnp.sum(grad_out, axis=0)
    grad_act = jnp.einsum(
        "nd,fd->nf", grad_out_low, down_weight, preferred_element_type=jnp.float32
    )
    grad_inner = gelu_pull(grad_act)[0].astype(jnp.bfloat16)
    grad_up = jnp.einsum("nd,nf->df", normed_mid, grad_inner, preferred_element_type=jnp.float32)
    grad_up_bias = jnp.sum(grad_inner.astype(jnp.float32), axis=0)
    grad_mid = jnp.einsum("nf,df->nd", grad_inner, up_weight, preferred_element_type=jnp.float32)
    grad_hid_norm, grad_gain_two, grad_bias_two = norm_back(grad_mid, hat_two, inv_two, norm2_gain)
    grad_hidden = grad_out + grad_hid_norm
    ffn_flat = padded_flat(
        (grad_gain_two, grad_bias_two, grad_up, grad_up_bias, grad_down, grad_down_bias), multiple
    )
    grad_hidden_low = grad_hidden.astype(jnp.bfloat16)
    grad_out_weight = jnp.einsum(
        "nc,nd->cd", context_flat, grad_hidden_low, preferred_element_type=jnp.float32
    )
    grad_out_bias = jnp.sum(grad_hidden_low.astype(jnp.float32), axis=0)
    grad_context = jnp.einsum(
        "nd,cd->nc", grad_hidden_low, out_weight, preferred_element_type=jnp.float32
    )
    grad_context = grad_context.astype(jnp.bfloat16).reshape(cell_count, local_len, model_width)
    grad_heads = lax.all_to_all(grad_context, "seq", split_axis=2, concat_axis=1, tiled=True)
    grad_query, grad_key, grad_value = attend_back(
        query_att, key_att, value_att, key_keep, log_total, grad_heads
    )
    grad_stack = jnp.stack([grad_query, grad_key, grad_value], axis=2).astype(jnp.bfloat16)
    grad_local = lax.all_to_all(grad_stack, "seq", split_axis=1, concat_axis=3, tiled=True)
    grad_qkv = grad_local.reshape(row_count, 3 * model_width)
    grad_qkv_weight = jnp.einsum(
        "nd,ne->de", normed_in, grad_qkv, preferred_element_type=jnp.float32
    )
    grad_query_bias = jnp.sum(grad_qkv[:, :model_width].astype(jnp.float32), axis=0)
    grad_value_bias = jnp.sum(grad_qkv[:, 2 * model_width :].astype(jnp.float32), axis=0)
    grad_normed_in = jnp.einsum(
        "ne,de->nd", grad_qkv, qkv_weight, preferred_element_type=jnp.float32
    )
    grad_sum_norm, grad_gain_one, grad_bias_one = norm_back(
        grad_normed_in, hat_one, inv_one, norm1_gain
    )
    grad_rows = (
        (grad_hidden + grad_sum_norm)
        .astype(jnp.bfloat16)
        .reshape(cell_count, local_len, model_width)
    )
    attn_flat = padded_flat(
        (
            grad_gain_one,
            grad_bias_one,
            grad_qkv_weight,
            grad_query_bias,
            grad_value_bias,
            grad_out_weight,
            grad_out_bias,
        ),
        multiple,
    )
    attn_share, ffn_share = (
        lax.psum_scatter(attn_flat, ("dp", "seq"), scatter_dimension=0, tiled=True),
        lax.psum_scatter(ffn_flat, ("dp", "seq"), scatter_dimension=0, tiled=True),
    )
    return (output, grad_rows, attn_share, ffn_share, gene_counts)


def fits(mesh):
    return dict(mesh.shape) == {"dp": 16, "seq": 2}


def solution(mesh):
    return jax.shard_map(
        on_device if fits(mesh) else plain_on_device,
        mesh=mesh,
        in_specs=(
            P("dp", "seq", None),
            P("dp", "seq", None),
            P("dp", "seq", None),
            P("dp", "seq", None),
            P("dp", "seq", None),
            P("dp", "seq", None),
            P("dp"),
            P("dp", "seq"),
            P(),
            P(),
            P(),
            P(),
            P(),
            P(),
            P(),
            P(),
            P(),
            P(),
            P(),
            P(),
            P(),
            P("dp", "seq", None),
        ),
        out_specs=(
            P("dp", "seq", None),
            P("dp", "seq", None),
            P(("dp", "seq")),
            P(("dp", "seq")),
            P(),
        ),
        check_vma=False,
    )
```

```python
import functools
import typing

import jax
import jax.numpy as jnp
from jax import lax
from jax.experimental import pallas as pl
from jax.experimental.pallas import tpu as pltpu
from jax.sharding import PartitionSpec as P

HDIM = 64
VOCAB = 36000
EPSILON = 1e-05
NEGATIVE = -1e30

F32, BF16, I32 = jnp.float32, jnp.bfloat16, jnp.int32
MESH = pl.DeviceIdType.MESH
LOG2E = 1.4426950408889634
LN2 = 0.6931471805599453
HALF = 512
WIDE = 768
NT = (((1,), (1,)), ((), ()))
NN = (((1,), (0,)), ((), ()))


def mm(lhs, rhs, dims=NN):
    return lax.dot_general(lhs, rhs, dims, preferred_element_type=F32)


def when(pred, body):
    if pred is None:
        body()
    else:
        pl.when(pred)(body)


def both(one, other):
    if one is None:
        return other
    if other is None:
        return one
    return jnp.logical_and(one, other)


CORE, X, Y, Z0, Z1, DIAG, NEXT, PREV = range(8)


class Place:
    def __init__(self):
        self.dp = lax.axis_index("dp")
        self.y = lax.axis_index("seq")
        self.core = self.dp % 2
        self.bit = [
            self.core,
            (self.dp // 2) % 2,
            self.y,
            (self.dp // 4) % 2,
            (self.dp // 8) % 2,
        ]
        flip = lambda name, step: self.dp + step - 2 * step * self.bit[name]
        self.index = self.dp * 2 + self.y
        count = 32
        after, before = (self.index + 1) % count, (self.index + count - 1) % count
        self.partner = [
            (flip(CORE, 1), self.y),
            (flip(X, 2), self.y),
            (self.dp, 1 - self.y),
            (flip(Z0, 4), self.y),
            (flip(Z1, 8), self.y),
            (flip(CORE, 1), 1 - self.y),
            (after // 2, after % 2),
            (before // 2, before % 2),
        ]
        self.moves = self.core != self.y
        self.stays = self.core == self.y


def greet(place, names):
    barrier = pltpu.get_barrier_semaphore()
    for name in names:
        pl.semaphore_signal(barrier, inc=1, device_id=place.partner[name], device_id_type=MESH)
    return lambda: pl.semaphore_wait(barrier, len(names))


def remote(src, dst, send_sem, recv_sem, partner):
    return pltpu.make_async_remote_copy(
        src_ref=src,
        dst_ref=dst,
        send_sem=send_sem,
        recv_sem=recv_sem,
        device_id=partner,
        device_id_type=MESH,
    )


def column(length, start, rows):
    return lax.broadcasted_iota(I32, (rows, 1), 0) + start < length


def hat_of(values):
    center = values - jnp.mean(values, axis=-1, keepdims=True)
    inv_std = lax.rsqrt(jnp.mean(center * center, axis=-1, keepdims=True) + EPSILON)
    return center * inv_std, inv_std


def norm_pull(grad, normed, inv_std, gain):
    grad_hat = grad * gain
    return inv_std * (
        grad_hat
        - jnp.mean(grad_hat, axis=-1, keepdims=True)
        - normed * jnp.mean(grad_hat * normed, axis=-1, keepdims=True)
    )


def padded_head(block, odd):
    zero = jnp.zeros((HDIM, block.shape[1]), block.dtype)
    if odd:
        return jnp.concatenate([zero, block], axis=0)
    return jnp.concatenate([block, zero], axis=0)


ROW_CHUNKS = 4
CHUNK = HALF // ROW_CHUNKS


SLOTS = 72
V_EARLY = 48
V_UP, V_DOWN, V_GAIN2, V_BIAS2, V_OUT, V_GAIN1, V_BIAS1, V_QUERY, V_VALUE = (
    0, 24, 30, 36, 42, 48, 54, 60, 66,
)
F_BASE, F_ROWS = 64, 1152
A_BASE, A_ROWS = 32, 576


class Part:
    def __init__(self, place, order, fixed, rows, local, landing, sems, finish):
        self.place, self.order, self.fixed, self.rows = place, order, fixed, rows
        self.local, self.landing, self.sems, self.finish = local, landing, sems, finish
        self.first, self.count = 0, 2 ** sum(name not in fixed for name in order)
        self.active, self.step, self.sent = None, 0, []

    @staticmethod
    def landing_blocks(order, fixed):
        count, sizes = 2 ** sum(name not in fixed for name in order), []
        for name in order:
            count = count if name in fixed else count // 2
            sizes.append(count)
        return sizes

    def copy(self, step, start, count):
        return remote(
            self.local.at[pl.ds(start, count)],
            self.landing[step],
            self.sems.at[0, step],
            self.sems.at[1, step],
            self.place.partner[self.order[step]],
        )

    def plan(self):
        name = self.order[self.step]
        mine = self.place.bit[name]
        if name in self.fixed:
            away = both(self.active, mine != self.fixed[name])
            home = both(self.active, mine == self.fixed[name])
            return self.copy(self.step, self.first, self.count), away, home
        half = self.count // 2
        return self.copy(self.step, self.first + (1 - mine) * half, half), self.active, self.active

    def launch(self):
        copy, sends, _ = self.plan()
        when(sends, copy.start)
        self.sent.append((copy, sends))

    def tick(self):
        copy, _, takes = self.plan()
        name = self.order[self.step]
        if name not in self.fixed:
            self.count //= 2
            self.first = self.first + self.place.bit[name] * self.count
        last = self.step == len(self.order) - 1
        kept = self.local.at[pl.ds(self.first, self.count)]
        landed = self.landing[self.step]
        self.active = takes
        self.step += 1
        following = None if last else self.plan()

        def body():
            copy.wait_recv()
            if last:
                self.finish(kept[0].astype(F32) + landed[0].astype(F32))
                return
            kept[...] = kept[...] + landed[...]
            when(
                None
                if following[1] is self.active
                else self.place.bit[self.order[self.step]] != self.fixed[self.order[self.step]],
                following[0].start,
            )

        when(takes, body)
        if not last:
            self.sent.append(following[:2])

    @property
    def done(self):
        return self.step == len(self.order)

    def drain(self):
        for copy, sends in self.sent:
            when(sends, copy.wait_send)


DOWN, UP, OUT, LOW, HIGH = range(5)

ORDERS = {
    (DOWN, 0): (Y, Z0, X, Z1),
    (DOWN, 1): (Z0, X, Y, Z1),
    (DOWN, 2): (Z0, X, Y, Z1),
    (DOWN, 3): (X, Y, Z0, Z1),
    (UP, 0): (X, Z0, Y, Z1),
    (UP, 1): (X, Z0, Z1, Y),
    (UP, 2): (Y, Z0, X, Z1),
    (UP, 3): (Z0, X, Y, Z1),
    (OUT, 0): (X, Y, Z1, Z0),
    (LOW, 0): (Y, Z1, Z0, X),
    (LOW, 1): (Y, X, Z0, Z1),
    (LOW, 2): (X, Z0, Y, Z1),
    (HIGH, 0): (X, Z1, Y, Z0),
    (HIGH, 1): (Z0, Y, X, Z1),
    (HIGH, 2): (X, Z1, Y, Z0),
}


def part_plans():
    plans = {}
    for j in range(4):
        plans[DOWN, j] = (ORDERS[DOWN, j], {Z1: 1, Z0: j // 2, X: j % 2}, 192)
        plans[UP, j] = (ORDERS[UP, j], {Z1: 0}, 48)
    plans[OUT, 0] = (ORDERS[OUT, 0], {Z1: 1, Z0: 1}, 96)
    for p in range(3):
        plans[LOW, p] = (ORDERS[LOW, p], {Z1: 0}, 32)
        plans[HIGH, p] = (ORDERS[HIGH, p], {Z1: 1, Z0: 0}, 32)
    return plans


NORM2, PROJECT, PAIRS, QKV, NORM1, END = 16, 17, 18, 24, 25, 26
IDS, VEC, LATE, COUNT, EDGE = range(5)

SCHEDULE = {
    0: (IDS,),
    4: (IDS,),
    13: (IDS,),
    18: ((DOWN, 0), IDS,),
    19: (VEC, (DOWN, 3), (DOWN, 1), (DOWN, 2),),
    20: ((DOWN, 0), (UP, 0), IDS, (OUT, 0), (UP, 2), VEC,),
    22: ((OUT, 0), (UP, 1), VEC,),
    25: (VEC,),
    26: ((HIGH, 0), (DOWN, 3), (LOW, 0), (DOWN, 2), COUNT, (UP, 2), (LOW, 1), (HIGH, 2), (DOWN, 2), (DOWN, 3), (DOWN, 1), LATE, (UP, 3), (HIGH, 0), (UP, 1), (HIGH, 1), (LOW, 0), (UP, 2), (UP, 3), (HIGH, 2), (LOW, 1), (HIGH, 1), (UP, 0), (LOW, 2), LATE, (UP, 3), (DOWN, 1), (UP, 1), (LOW, 0), (DOWN, 0), (HIGH, 1), (HIGH, 0), (UP, 2), (OUT, 0), (LOW, 2), (UP, 0), LATE, (DOWN, 2), (UP, 1), (UP, 0), (DOWN, 3), (HIGH, 0), (LOW, 2), (HIGH, 2), (DOWN, 1), (LOW, 1), LATE, (DOWN, 0), (LOW, 2), (OUT, 0), (UP, 3), (HIGH, 2), EDGE, VEC, (LOW, 0), (LOW, 1), LATE, (HIGH, 1),),
}


class Scratch(typing.NamedTuple):
    x_recv: typing.Any
    lengths: typing.Any
    row_sem: typing.Any
    x_sem: typing.Any
    kv_sem: typing.Any
    len_sem: typing.Any
    cot_sem: typing.Any
    qkv: typing.Any
    out: typing.Any
    up: typing.Any
    down: typing.Any
    e: typing.Any
    a2: typing.Any
    q: typing.Any
    k: typing.Any
    v: typing.Any
    ot: typing.Any
    ft: typing.Any
    a1t: typing.Any
    a2t: typing.Any
    h: typing.Any
    y: typing.Any
    mid: typing.Any
    dh: typing.Any
    lse: typing.Any
    pair_send: typing.Any
    pair_recv: typing.Any
    flat_f: typing.Any
    flat_a: typing.Any
    vec: typing.Any
    vec_recv: typing.Any
    ids: typing.Any
    down_send: typing.Any
    up_send: typing.Any
    out_send: typing.Any
    qkv_send: typing.Any
    local: typing.Any
    landing: typing.Any
    sems: typing.Any
    load_sem: typing.Any
    core_sem: typing.Any
    pair_sem: typing.Any
    vec_sem: typing.Any
    ids_sem: typing.Any
    edge_sem: typing.Any
    result_sem: typing.Any


def backward_scratch():
    vmem, dma = pltpu.VMEM, pltpu.SemaphoreType.DMA
    low, low_t, full = vmem((HALF, WIDE), BF16), vmem((WIDE, HALF), BF16), vmem((HALF, WIDE), F32)
    plans = part_plans()
    return Scratch(
        x_recv=low,
        lengths=vmem((2, 8, 128), I32),
        row_sem=dma((ROW_CHUNKS, 6)),
        x_sem=dma((2, ROW_CHUNKS)),
        kv_sem=dma((2, 2, ROW_CHUNKS)),
        len_sem=dma((2,)),
        cot_sem=dma((2,)),
        qkv=vmem((WIDE, 3 * WIDE), BF16),
        out=vmem((WIDE, WIDE), BF16),
        up=vmem((WIDE, 4 * WIDE), BF16),
        down=vmem((4 * WIDE, WIDE), BF16),
        e=low,
        a2=low,
        q=low,
        k=vmem((2 * HALF, WIDE), BF16),
        v=vmem((2 * HALF, WIDE), BF16),
        ot=low_t,
        ft=vmem((2, WIDE, HALF), BF16),
        a1t=vmem((2, WIDE // 2, HALF), BF16),
        a2t=vmem((2, WIDE // 2, HALF), BF16),
        h=full,
        y=full,
        mid=full,
        dh=full,
        lse=vmem((16, HALF), F32),
        pair_send=vmem((2, 6, HALF, 128), BF16),
        pair_recv=vmem((2, 6, HALF, 128), BF16),
        flat_f=vmem((F_BASE + F_ROWS + 64, 128), F32),
        flat_a=vmem((A_BASE + A_ROWS + 32, 128), F32),
        vec=[vmem((6, V_EARLY, 128), F32), vmem((6, SLOTS - V_EARLY, 128), F32)],
        vec_recv=[vmem((5, V_EARLY, 128), F32), vmem((5, SLOTS - V_EARLY, 128), F32)],
        ids=vmem((32, 8, 128), I32),
        down_send=vmem((2, 2, 192, WIDE), BF16),
        up_send=vmem((2, 8, 48, WIDE), BF16),
        out_send=vmem((4, 96, WIDE), BF16),
        qkv_send=vmem((2, 12, 32, WIDE), BF16),
        local=[
            [vmem((2, 192, WIDE), BF16)] * 4,
            [vmem((8, 48, WIDE), BF16)] * 4,
            [vmem((4, 96, WIDE), BF16)],
            [vmem((12, 32, WIDE), BF16)] * 3,
        ],
        landing={
            key: [vmem((count, rows, WIDE), BF16) for count in Part.landing_blocks(order, fixed)]
            for key, (order, fixed, rows) in plans.items()
        },
        sems={key: dma((2, 4)) for key in plans},
        load_sem=dma((24,)),
        core_sem=dma((2, 12)),
        pair_sem=dma((2, 2, 6)),
        vec_sem=[dma((2, 5)), dma((2, 5))],
        ids_sem=dma((2, 5)),
        edge_sem=dma((2, 4)),
        result_sem=dma((2, 3)),
    )


STAGES = (CORE, X, Y, Z0, Z1)


def layer_kernel(*refs):
    rows_in = refs[:6]
    (
        cot_in, qkv_in, out_in, up_in, down_in, gain1, bias1, query_bias, value_bias, out_bias,
        gain2, bias2, up_bias, down_bias, gene_ids, lens,
    ) = refs[6:22]
    output_o, rows_o, attn_o, ffn_o, counts_o, x_o = refs[22:28]
    s = jax.tree.unflatten(jax.tree.structure(backward_scratch()), refs[28:])
    place = Place()
    core, y_bit = place.core, place.y
    mate, across = place.partner[CORE], place.partner[DIAG]
    greeted = greet(place, range(8))
    load_sem = s.load_sem

    def load(n, src, dst):
        copy = pltpu.make_async_copy(src, dst, load_sem.at[n])
        copy.start()
        return copy

    def load_up(j):
        cols = pl.ds(WIDE * j, WIDE)
        return load(4 + 2 * j, up_in.at[:, cols], s.up.at[:, cols])

    def load_down(j):
        cols = pl.ds(WIDE * j, WIDE)
        return load(5 + 2 * j, down_in.at[cols], s.down.at[cols])

    def rows_at(chunk):
        return pl.ds(chunk * CHUNK, CHUNK)

    held = [s.down.at[pl.ds(HALF * i, HALF)] for i in range(6)]
    loads = [
        [
            pltpu.make_async_copy(
                rows_in[i].at[rows_at(r)], held[i].at[rows_at(r)], s.row_sem.at[r, i]
            )
            for i in range(6)
        ]
        for r in range(ROW_CHUNKS)
    ]
    for group in loads:
        for copy in group:
            copy.start()
    load_qkv = load(21, qkv_in, s.qkv)
    load_out = load(0, out_in, s.out)
    weights_up = {j: load_up(j) for j in (2, 3)}

    s.lengths[0] = jnp.full((8, 128), lens[0], I32)
    greeted()
    send_len = remote(s.lengths.at[0], s.lengths.at[1], s.len_sem.at[0], s.len_sem.at[1], mate)
    send_len.start()

    h, y, mid, dh, e = s.h, s.y, s.mid, s.dh, s.e
    x_send = s.up.at[pl.ds(0, HALF), pl.ds(0, WIDE)]
    swaps = [
        remote(
            x_send.at[rows_at(r)], s.x_recv.at[rows_at(r)], s.x_sem.at[0, r], s.x_sem.at[1, r], across
        )
        for r in range(ROW_CHUNKS)
    ]
    for r in range(ROW_CHUNKS):
        for copy in loads[r]:
            copy.wait()
        total = held[0][rows_at(r)].astype(F32)
        for i in range(1, 6):
            total = total + held[i][rows_at(r)].astype(F32)
        h[rows_at(r)] = total

        @pl.when(place.moves)
        def _():
            x_send[rows_at(r)] = h[rows_at(r)].astype(BF16)
            swaps[r].start()

    weights_down = {j: load_down(j) for j in range(4)}
    load_qkv.wait()
    send_len.wait()
    length = jnp.where(place.stays, s.lengths[0], s.lengths[1])[0:1, 0:1]
    live_own = column(length, core * HALF, HALF)
    live_far = column(length, (1 - core) * HALF, HALF)

    key_first = None
    sends = []
    for r in range(ROW_CHUNKS):

        @pl.when(place.moves)
        def _():
            swaps[r].wait_recv()
            h[rows_at(r)] = s.x_recv[rows_at(r)].astype(F32)

        normed, _ = hat_of(h[rows_at(r)])
        low = (normed * gain1[...].reshape(1, WIDE) + bias1[...].reshape(1, WIDE)).astype(BF16)
        s.a2[rows_at(r)] = low
        projected = mm(low, s.qkv[...])
        scaled = (projected[:, :WIDE] + query_bias[...].reshape(1, WIDE)) * (LOG2E * HDIM**-0.5)
        s.q[rows_at(r)] = scaled.astype(BF16)
        keys = projected[:, WIDE : 2 * WIDE]
        values = projected[:, 2 * WIDE :] + value_bias[...].reshape(1, WIDE)
        if r == 0:
            key_first = keys[0:1]
        live = column(length, core * HALF + r * CHUNK, CHUNK)
        s.k[rows_at(r)] = jnp.where(live, keys, key_first).astype(BF16)
        s.v[rows_at(r)] = jnp.where(live, values, 0.0).astype(BF16)
        for which, ref in enumerate((s.k, s.v)):
            copy = remote(
                ref.at[rows_at(r)], ref.at[pl.ds(HALF + r * CHUNK, CHUNK)],
                s.kv_sem.at[0, which, r], s.kv_sem.at[1, which, r], mate,
            )
            copy.start()
            sends.append(copy)

    load_e = pltpu.make_async_copy(cot_in, e, load_sem.at[1])
    swap_cot = remote(cot_in, e, s.cot_sem.at[0], s.cot_sem.at[1], across)
    pl.when(place.stays)(load_e.start)
    pl.when(place.moves)(swap_cot.start)
    keep_x = pltpu.make_async_copy(h, x_o, load_sem.at[22])
    keep_x.start()

    qt_first = s.ft.at[0]
    qt_first[...] = s.q[...].T
    flipped = s.a2[...].T
    for c in range(2):
        for m in range(6):
            s.a1t[c, 64 * m : 64 * m + 64] = flipped[128 * m + 64 * c : 128 * m + 64 * c + 64]
    for copy in sends:
        copy.wait_recv()

    @pl.when(place.moves)
    def _():
        for swap in swaps:
            swap.wait_send()

    values_t = s.up.at[:, pl.ds(0, 2 * HALF)]
    values_t[...] = s.v[...].T
    slot = lax.broadcasted_iota(I32, (16, 2 * HALF), 1)
    slot = jnp.where(slot < HALF, slot + core * HALF, slot - core * HALF)
    live_row = (slot < length).astype(F32).astype(BF16)
    heads = WIDE // HDIM

    def score(head):
        return mm(
            s.k[:, 128 * (head // 2) : 128 * (head // 2) + 128],
            padded_head(qt_first[HDIM * head : HDIM * head + HDIM], head % 2),
        )

    scores = score(0)
    for head in range(heads):
        rows = slice(HDIM * head, HDIM * head + HDIM)
        later = score(head + 1) if head + 1 < heads else None
        top = jnp.max(scores, axis=0, keepdims=True)
        probs = jnp.exp2(scores - top).astype(BF16)
        context = mm(jnp.concatenate([values_t[rows], live_row], axis=0), probs)
        mass = context[HDIM : HDIM + 1]
        s.ot[rows] = (context[:HDIM] / mass).astype(BF16)
        s.lse[head : head + 1] = top + jnp.log2(mass)
        scores = later
    for j in (0, 1):
        weights_up[j] = load_up(j)

    def put_vec(slot, row):
        late = int(slot >= V_EARLY)
        slot -= late * V_EARLY
        for t in range(row.shape[1] // 128):
            s.vec[late][0, slot + t : slot + t + 1] = row[:, 128 * t : 128 * t + 128]

    def flat_store(ref, base, stride, value, skip=0):
        for t in range(WIDE // 128):
            at = pl.ds(base + t + t // 2 * skip, value.shape[0], stride=stride)
            ref[at, :] = value[:, 128 * t : 128 * t + 128]

    parts = {}
    for key, (order, fixed, rows) in part_plans().items():
        kind, n = key
        if kind == DOWN:
            local = s.local[DOWN][n]
            finish = functools.partial(flat_store, s.flat_f, F_BASE, 6)
        elif kind == UP:
            local = s.local[UP][n]
            finish = functools.partial(flat_store, s.flat_f, F_BASE + 6 * n, 24)
        elif kind == OUT:
            local = s.local[OUT][0]
            finish = functools.partial(flat_store, s.flat_a, A_BASE, 6)
        else:
            whole = s.local[LOW][n]
            local = whole.at[pl.ds(0, 8)] if kind == LOW else whole.at[pl.ds(8, 4)]
            finish = functools.partial(flat_store, s.flat_a, A_BASE + 2 * n, 18, skip=4)
        landing = s.landing[key]
        parts[key] = Part(place, order, fixed, rows, local, landing, s.sems[key], finish)

    vec_copies = [[], []]

    def vec_launch(late):
        n = len(vec_copies[late])
        copy = remote(
            s.vec[late].at[n], s.vec_recv[late].at[n],
            s.vec_sem[late].at[0, n], s.vec_sem[late].at[1, n],
            place.partner[STAGES[n]],
        )
        copy.start()
        vec_copies[late].append(copy)

    def vec_tick(late):
        n = len(vec_copies[late])
        vec_copies[late][-1].wait_recv()
        s.vec[late][n] = s.vec[late][n - 1] + s.vec_recv[late][n - 1]
        if n < 5:
            vec_launch(late)

    edges = []

    def edge_launch(ref, base, rows):
        end = base + rows
        for src, dst, size, to in ((end - 24, base - 24, 24, NEXT), (base, end, 32, PREV)):
            n = len(edges)
            copy = remote(
                ref.at[pl.ds(src, size)], ref.at[pl.ds(dst, size)],
                s.edge_sem.at[0, n], s.edge_sem.at[1, n], place.partner[to],
            )
            copy.start()
            edges.append(copy)

    def count(n, total):
        high_row = lax.broadcasted_iota(I32, (288, 128), 0)
        low_row = lax.broadcasted_iota(I32, (128, 128), 0)
        tile = s.ids[n]
        for r in range(0, 4, 2):
            high = [(high_row == (tile[r + i : r + i + 1] >> 7)).astype(F32).astype(BF16) for i in range(2)]
            low = [(low_row == (tile[r + i : r + i + 1] & 127)).astype(F32).astype(BF16) for i in range(2)]
            total = total + mm(jnp.concatenate(high, axis=1), jnp.concatenate(low, axis=1), NT)
        return total

    def count_all():
        counts_o[...] = lax.fori_loop(0, 32, count, jnp.zeros((288, 128), F32)).astype(I32)

    special = {
        IDS: lambda: ids_tick(),
        VEC: lambda: vec_tick(0),
        LATE: lambda: vec_tick(1),
        COUNT: count_all,
        EDGE: lambda: edge_launch(s.flat_f, F_BASE, F_ROWS),
    }

    def pause(hook):
        for entry in SCHEDULE.get(hook, ()):
            if isinstance(entry, tuple):
                parts[entry].tick()
            else:
                special[entry]()

    core_copies = []

    def core_send(src, dst):
        n = len(core_copies)
        copy = remote(src, dst, s.core_sem.at[0, n], s.core_sem.at[1, n], mate)
        copy.start()
        core_copies.append(copy)
        return copy

    def put_blocks(ref, key, value):
        order, fixed, rows = part_plans()[key]
        free = [name for name in order if name not in fixed]
        natural = [name for name in (Z1, Z0, X, Y) if name not in fixed]
        for m in range(2 ** len(free)):
            bits = {name: (m >> (len(natural) - 1 - i)) & 1 for i, name in enumerate(natural)}
            at = sum(bits[name] << (len(free) - 1 - i) for i, name in enumerate(free))
            ref[at] = value[m * rows : m * rows + rows]

    load_out.wait()
    keep_x.wait()
    gain2_row, bias2_row = gain2[...].reshape(1, WIDE), bias2[...].reshape(1, WIDE)
    h[...] = h[...] + mm(s.ot[...].T, s.out[...]) + out_bias[...].reshape(1, WIDE)
    for r in range(4):
        at = pl.ds(128 * r, 128)
        normed, _ = hat_of(h[at])
        s.a2[at] = (normed * gain2_row + bias2_row).astype(BF16)
        y[at] = h[at] + down_bias[...].reshape(1, WIDE)
    flipped = s.a2[...].T
    for c in range(2):
        for m in range(4):
            s.a2t[c, 96 * m : 96 * m + 96] = flipped[192 * m + 96 * c : 192 * m + 96 * c + 96]

    own_len = jnp.full((1, 128), lens[0], I32)
    slots = lax.broadcasted_iota(I32, (1, 128), 1) + y_bit * HALF
    ids = s.ids
    here = sum(place.bit[name] * 2**stage for stage, name in enumerate(STAGES))
    tile = [
        jnp.where(slots + 128 * r < own_len, gene_ids[0:1, 128 * r : 128 * r + 128], -1) for r in range(4)
    ]
    ids[pl.ds(here, 1)] = jnp.concatenate(tile + [jnp.full((4, 128), -1, I32)], axis=0)[None]
    ids_copies = []

    def ids_launch(stage):
        size = 2**stage
        at = pl.ds((here // size) * size, size)
        copy = remote(
            ids.at[at], ids.at[at], s.ids_sem.at[0, stage], s.ids_sem.at[1, stage],
            place.partner[STAGES[stage]],
        )
        copy.start()
        ids_copies.append(copy)

    def ids_tick():
        ids_copies[-1].wait_recv()
        if len(ids_copies) < 5:
            ids_launch(len(ids_copies))

    ids_launch(0)

    pl.when(place.stays)(load_e.wait)
    pl.when(place.moves)(swap_cot.wait_recv)
    put_vec(V_DOWN, jnp.sum(e[...].astype(F32), axis=0, keepdims=True))
    half_rows = WIDE // 2
    theirs = pl.ds(pl.multiple_of((1 - core) * half_rows, half_rows), half_rows)
    ours = pl.ds(pl.multiple_of(core * half_rows, half_rows), half_rows)

    def settle(j, grad, down_copy, up_copy):
        own = mm(s.ft[j % 2, ours], e[...]).reshape(2, 192, WIDE)
        down_copy.wait_recv()
        local = s.local[DOWN][j]
        local[...] = (own + local[...].astype(F32)).astype(BF16)
        parts[DOWN, j].launch()
        own = mm(s.a2t[core], grad)
        up_copy.wait_recv()
        add_blocks(s.local[UP][j], (UP, j), own)
        parts[UP, j].launch()

    waiting = None
    for j in range(4):
        cols = pl.ds(WIDE * j, WIDE)
        weights_up[j].wait()
        weights_down[j].wait()
        inner = mm(s.a2[...], s.up[:, cols]) + up_bias[WIDE * j : WIDE * j + WIDE].reshape(1, WIDE)
        phi = 0.5 * (1.0 + lax.erf(inner * 0.7071067811865476))
        slope = phi + inner * jnp.exp2(inner * inner * (-0.5 * LOG2E)) * 0.3989422804014327
        active = (inner * phi).astype(BF16)
        s.ft[j % 2] = active.T
        if j:
            settle(j - 1, *waiting)
        if j >= 2:
            core_copies[2 * j - 4].wait_send()
            core_copies[2 * j - 3].wait_send()
        sent = s.down_send.at[j % 2]
        sent[...] = mm(s.ft[j % 2, theirs], e[...]).astype(BF16).reshape(2, 192, WIDE)
        down_copy = core_send(sent, s.local[DOWN][j])
        pause(4 * j)
        grad = (mm(e[...], s.down[cols], NT) * slope).astype(BF16)
        sent = s.up_send.at[j % 2]
        put_blocks(sent, (UP, j), mm(s.a2t[1 - core], grad).astype(BF16))
        up_copy = core_send(sent, s.local[UP][j])
        pause(4 * j + 1)
        put_vec(V_UP + 6 * j, jnp.sum(grad.astype(F32), axis=0, keepdims=True))
        back = mm(grad, s.up[:, cols], NT)
        mid[...] = back if j == 0 else mid[...] + back
        y[...] = y[...] + mm(active, s.down[cols])
        pause(4 * j + 2)
        waiting = (grad, down_copy, up_copy)
    down = s.down
    grad_h, grad_o, grad_rows, *grads = [down.at[pl.ds(HALF * n, HALF)] for n in range(6)]
    output = s.a2
    sums = [jnp.zeros((1, WIDE), F32) for _ in range(3)]
    for r in range(4):
        at = pl.ds(128 * r, 128)
        output[at] = y[at].astype(BF16)
        normed, inv_std = hat_of(h[at])
        grad = mid[at]
        sums[0] += jnp.sum(grad * normed, axis=0, keepdims=True)
        sums[1] += jnp.sum(grad, axis=0, keepdims=True)
        total = e[at].astype(F32) + norm_pull(grad, normed, inv_std, gain2_row)
        dh[at] = total
        low = total.astype(BF16)
        grad_h[at] = low
        sums[2] += jnp.sum(low.astype(F32), axis=0, keepdims=True)
    put_vec(V_GAIN2, sums[0])
    put_vec(V_BIAS2, sums[1])
    put_vec(V_OUT, sums[2])

    result_copies = []

    def give_back(n, src, dst):
        keep = pltpu.make_async_copy(src, dst, s.result_sem.at[n, 2])
        swap = remote(
            src, dst, s.result_sem.at[n, 0], s.result_sem.at[n, 1], place.partner[DIAG]
        )
        pl.when(place.stays)(keep.start)
        pl.when(place.moves)(swap.start)
        result_copies.append((keep, swap))

    settle(3, *waiting)
    vec_launch(0)
    give_back(0, output, output_o)
    pause(NORM2)

    def out_rows(c):
        return jnp.concatenate(
            [s.ot[pl.ds(pl.multiple_of(384 * x + 192 * c, 192), 192)] for x in range(2)], axis=0
        )

    put_blocks(s.out_send, (OUT, 0), mm(out_rows(1 - core), grad_h[...]).astype(BF16))
    out_copy = core_send(s.out_send, s.local[OUT][0])
    grad_o[...] = mm(grad_h[...], s.out[...], NT).astype(BF16)
    up = s.up
    grad_ot, grad_qt, qt = [up.at[:, pl.ds(HALF * n, HALF)] for n in range(3)]
    grad_ot[...] = grad_o[...].T
    load_x = pltpu.make_async_copy(x_o, y, load_sem.at[20])
    load_x.start()
    qt[...] = s.q[...].T
    own = mm(out_rows(core), grad_h[...])
    out_copy.wait_recv()
    add_blocks(s.local[OUT][0], (OUT, 0), own)
    parts[OUT, 0].launch()
    pause(PROJECT)

    live = jnp.concatenate([live_own, live_far], axis=0)
    lane = lax.broadcasted_iota(I32, (1, 128), 1)
    dk, dv = h, mid
    pair_copies, qkv_copies = [], []

    def far_qkv(g):
        grad = grads[g]
        grad[:, :256] = grad_qt[256 * g : 256 * g + 256].T
        for i in range(2):
            j = 2 * g + i
            for n, mine in enumerate((dk, dv)):
                pair_copies[2 * j + n].wait_recv()
                total = mine[:, 128 * j : 128 * j + 128] + s.pair_recv[n, j].astype(F32)
                start = 256 * (n + 1) + 128 * i
                grad[:, start : start + 128] = jnp.where(live_own, total, 0.0).astype(BF16)
        sent = s.qkv_send.at[g % 2]
        if g == 2:
            qkv_copies[0].wait_send()
        value = mm(s.a1t[1 - core], grad[...]).astype(BF16)
        put_blocks(sent.at[pl.ds(0, 8)], (LOW, g), value[:256])
        put_blocks(sent.at[pl.ds(8, 4)], (HIGH, g), value[256:])
        qkv_copies.append(core_send(sent, s.local[LOW][g]))

    def settle_qkv(g):
        own = mm(s.a1t[core], grads[g][...])
        qkv_copies[g].wait_recv()
        local = s.local[LOW][g]
        add_blocks(local.at[pl.ds(0, 8)], (LOW, g), own[:256])
        add_blocks(local.at[pl.ds(8, 4)], (HIGH, g), own[256:])
        parts[LOW, g].launch()
        parts[HIGH, g].launch()

    def pull_qkv(g):
        grad, at = grads[g], lambda p: slice(WIDE * p + 256 * g, WIDE * p + 256 * g + 256)
        total = mm(grad[:, :256], s.qkv[:, at(0)], NT)
        total = total + mm(grad[:, 256:512], s.qkv[:, at(1)], NT)
        return total + mm(grad[:, 512:], s.qkv[:, at(2)], NT)

    for j in range(WIDE // 128):
        at = slice(128 * j, 128 * j + 128)
        keys, values = s.k[:, at], s.v[:, at]
        keys_t = jnp.where(live, keys, jnp.zeros_like(keys)).T
        grad_keys = grad_values = None
        for i in range(2):
            head = 2 * j + i
            rows = slice(HDIM * head, HDIM * head + HDIM)
            mine = lane // HDIM == i
            scores = mm(keys, padded_head(qt[rows], i))
            probs = jnp.exp2(scores - s.lse[head : head + 1])
            grad_ot_head = grad_ot[rows]
            grad_probs = mm(values, padded_head(grad_ot_head, i))
            delta = jnp.sum(
                grad_ot_head.astype(F32) * s.ot[rows].astype(F32), axis=0, keepdims=True
            )
            grad_scores = (probs * (grad_probs - delta)).astype(BF16)
            queries = jnp.where(mine, s.q[:, at], jnp.zeros((), BF16))
            grad_out = jnp.where(mine, grad_o[:, at], jnp.zeros((), BF16))
            more = mm(probs.astype(BF16), grad_out)
            grad_values = more if i == 0 else grad_values + more
            more = mm(grad_scores, queries)
            grad_keys = more if i == 0 else grad_keys + more
            grad_qt[rows] = (mm(keys_t[HDIM * i : HDIM * i + HDIM], grad_scores) * HDIM**-0.5).astype(BF16)
        grad_keys = grad_keys * LN2
        dk[:, at] = grad_keys[:HALF]
        dv[:, at] = grad_values[:HALF]
        for n, value in enumerate((grad_keys, grad_values)):
            s.pair_send[n, j] = value[HALF:].astype(BF16)
            copy = remote(
                s.pair_send.at[n, j], s.pair_recv.at[n, j],
                s.pair_sem.at[0, n, j], s.pair_sem.at[1, n, j], mate,
            )
            copy.start()
            pair_copies.append(copy)
        if j and j % 2 == 0:
            far_qkv(j // 2 - 1)
        elif j > 1:
            settle_qkv(j // 2 - 1)
        pause(PAIRS + j)
    back = pull_qkv(0) + pull_qkv(1)
    far_qkv(2)
    pause(QKV)

    mid[...] = back + pull_qkv(2)
    load_x.wait()
    gain1_row = gain1[...].reshape(1, WIDE)
    sums = [jnp.zeros((1, WIDE), F32) for _ in range(2)]
    for r in range(4):
        at = pl.ds(128 * r, 128)
        normed, inv_std = hat_of(y[at])
        grad = mid[at]
        sums[0] += jnp.sum(grad * normed, axis=0, keepdims=True)
        sums[1] += jnp.sum(grad, axis=0, keepdims=True)
        grad_rows[at] = (dh[at] + norm_pull(grad, normed, inv_std, gain1_row)).astype(BF16)
    put_vec(V_GAIN1, sums[0])
    put_vec(V_BIAS1, sums[1])
    give_back(1, grad_rows, rows_o)
    for p, slot in enumerate((V_QUERY, None, V_VALUE)):
        if p != 1:
            total = [jnp.sum(grad[:, 256 * p : 256 * p + 256].astype(F32), axis=0, keepdims=True) for grad in grads]
            put_vec(slot, jnp.concatenate(total, axis=1))
    vec_launch(1)
    settle_qkv(2)
    pause(NORM1)

    pause(END)
    while any(not part.done for part in parts.values()):
        for part in parts.values():
            if not part.done:
                part.tick()
    edge_launch(s.flat_a, A_BASE, A_ROWS)
    for copy in edges:
        copy.wait()
    total = jnp.concatenate([s.vec[0][5], s.vec[1][5]], axis=0)
    flat_f, flat_a = s.flat_f, s.flat_a
    me = place.index
    f_end, a_end = F_BASE + F_ROWS, A_BASE + A_ROWS

    @pl.when(me == 0)
    def _():
        flat_f[F_BASE - 12 : F_BASE] = total[V_GAIN2 : V_GAIN2 + 12]
        flat_a[A_BASE - 12 : A_BASE] = total[V_GAIN1 : V_GAIN1 + 12]

    @pl.when(me == 15)
    def _():
        flat_f[f_end : f_end + 24] = total[V_UP : V_UP + 24]

    @pl.when(me == 16)
    def _():
        flat_f[F_BASE - 24 : F_BASE] = total[V_UP : V_UP + 24]

    @pl.when(me == 23)
    def _():
        flat_a[a_end : a_end + 12] = total[V_QUERY : V_QUERY + 12]

    @pl.when(me == 31)
    def _():
        flat_f[f_end : f_end + 6] = total[V_DOWN : V_DOWN + 6]
        flat_f[f_end + 6 : f_end + 32] = jnp.zeros((26, 128), F32)
        flat_a[a_end : a_end + 6] = total[V_OUT : V_OUT + 6]
        flat_a[a_end + 6 : a_end + 32] = jnp.zeros((26, 128), F32)

    f_start = jnp.where(me < 16, F_BASE - 12 + 2 * me, F_BASE - 4 + 2 * (me - 16))
    a_start = jnp.where(me < 24, A_BASE - 12 + me, A_BASE + me - 24)
    ffn_o[...] = flat_f[pl.ds(f_start, ffn_o.shape[0]), :]
    attn_o[...] = flat_a[pl.ds(a_start, attn_o.shape[0]), :]

    for part in parts.values():
        part.drain()
    core_copies[4].wait_send()
    for n in (5, 6, 7, 8, 10, 11):
        core_copies[n].wait_send()
    for copy in sends + pair_copies + ids_copies + vec_copies[0] + vec_copies[1]:
        copy.wait_send()
    pl.when(place.moves)(swap_cot.wait_send)
    for keep, swap in result_copies:
        pl.when(place.stays)(keep.wait)
        pl.when(place.moves)(swap.wait)


def add_blocks(ref, key, value):
    order, fixed, rows = part_plans()[key]
    free = [name for name in order if name not in fixed]
    natural = [name for name in (Z1, Z0, X, Y) if name not in fixed]
    for m in range(2 ** len(free)):
        bits = {name: (m >> (len(natural) - 1 - i)) & 1 for i, name in enumerate(natural)}
        at = sum(bits[name] << (len(free) - 1 - i) for i, name in enumerate(free))
        ref[at] = (ref[at].astype(F32) + value[m * rows : m * rows + rows]).astype(BF16)


def layer_call(rows, cotangent, weights, vectors, gene_ids, lengths, attn_units, ffn_units):
    any_spec = pl.BlockSpec(memory_space=pl.ANY)
    vmem = pl.BlockSpec(memory_space=pltpu.VMEM)
    shape = jax.ShapeDtypeStruct
    return pl.pallas_call(
        layer_kernel,
        out_shape=(
            shape((HALF, WIDE), BF16),
            shape((HALF, WIDE), BF16),
            shape((attn_units, 128), F32),
            shape((ffn_units, 128), F32),
            shape((288, 128), I32),
            shape((HALF, WIDE), F32),
        ),
        in_specs=[any_spec] * 11 + [vmem] * 10 + [pl.BlockSpec(memory_space=pltpu.SMEM)],
        out_specs=(any_spec, any_spec, vmem, vmem, vmem, any_spec),
        scratch_shapes=jax.tree.leaves(backward_scratch()),
        compiler_params=pltpu.CompilerParams(
            collective_id=0, has_side_effects=True, vmem_limit_bytes=64 * 2**20
        ),
        name="layer",
    )(*rows, cotangent, *weights, *vectors, gene_ids, lengths)


def hand_over_kernel(output_in, rows_in, attn_in, ffn_in, counts_in, output_o, rows_o, attn_o, ffn_o, counts_o, *scratch):
    *held, load_sem, store_sem = scratch
    pairs = ((output_in, output_o), (rows_in, rows_o), (attn_in, attn_o), (ffn_in, ffn_o))
    loads = [pltpu.make_async_copy(src, ref, load_sem.at[n]) for n, ((src, _), ref) in enumerate(zip(pairs, held))]
    stores = [pltpu.make_async_copy(ref, dst, store_sem.at[n]) for n, ((_, dst), ref) in enumerate(zip(pairs, held))]
    for copy in loads:
        copy.start()
    counts_o[...] = counts_in[...].reshape(-1)[: counts_o.shape[0]]
    for load, store in zip(loads, stores):
        load.wait()
        store.start()
    for store in stores:
        store.wait()


def hand_over_call(results):
    any_spec = pl.BlockSpec(memory_space=pl.ANY)
    vmem = pl.BlockSpec(memory_space=pltpu.VMEM)
    large = results[:4]
    return pl.pallas_call(
        hand_over_kernel,
        out_shape=tuple(jax.ShapeDtypeStruct(r.shape, r.dtype) for r in large)
        + (jax.ShapeDtypeStruct((VOCAB,), I32),),
        in_specs=[any_spec] * 4 + [vmem],
        out_specs=(any_spec,) * 4 + (vmem,),
        scratch_shapes=[pltpu.VMEM(r.shape, r.dtype) for r in large]
        + [pltpu.SemaphoreType.DMA((4,)), pltpu.SemaphoreType.DMA((4,))],
        name="hand_over",
    )(*results)


def on_device(
    row_gene,
    row_value,
    row_promoter,
    row_grn,
    row_coexp,
    row_family,
    lengths,
    gene_ids,
    norm1_gain,
    norm1_bias,
    qkv_weight,
    query_bias,
    value_bias,
    out_weight,
    out_bias,
    norm2_gain,
    norm2_bias,
    up_weight,
    up_bias,
    down_weight,
    down_bias,
    cotangent,
):
    rows = [
        member.reshape(HALF, WIDE)
        for member in (row_gene, row_value, row_promoter, row_grn, row_coexp, row_family)
    ]
    devices = lax.axis_size("dp") * lax.axis_size("seq")
    attn_len, ffn_len = gradient_lengths(WIDE, 4 * WIDE, devices)
    results = layer_call(
        rows,
        cotangent.reshape(HALF, WIDE),
        (qkv_weight, out_weight, up_weight, down_weight),
        (
            norm1_gain,
            norm1_bias,
            query_bias,
            value_bias,
            out_bias,
            norm2_gain,
            norm2_bias,
            up_bias,
            down_bias,
        ),
        gene_ids,
        lengths,
        attn_len // devices // 128,
        ffn_len // devices // 128,
    )[:5]
    output, grad_rows, attn, ffn, counts = hand_over_call(results)
    return (
        output.reshape(row_gene.shape),
        grad_rows.reshape(row_gene.shape),
        attn.reshape(-1),
        ffn.reshape(-1),
        counts,
    )


def gradient_lengths(width, hidden, devices):
    pad = lambda count: -(-count // (devices * 128)) * devices * 128
    return (
        pad(3 * width * width + width * width + 5 * width),
        pad(2 * width * hidden + 3 * width + hidden),
    )


def layer_norm(values_in, gain_vec, bias_vec):
    center = values_in - jnp.mean(values_in, axis=-1, keepdims=True)
    variance = jnp.mean(center * center, axis=-1, keepdims=True)
    inv_std = lax.rsqrt(variance + EPSILON)
    normed = center * inv_std
    return (normed * gain_vec + bias_vec, normed, inv_std)


def norm_back(grad_normed, normed, inv_std, gain_vec):
    grad_hat = grad_normed * gain_vec
    grad_gain = jnp.sum(grad_normed * normed, axis=0)
    grad_bias = jnp.sum(grad_normed, axis=0)
    grad_input = inv_std * (
        grad_hat
        - jnp.mean(grad_hat, axis=-1, keepdims=True)
        - normed * jnp.mean(grad_hat * normed, axis=-1, keepdims=True)
    )
    return (grad_input, grad_gain, grad_bias)


def gelu_exact(inner):
    return jax.nn.gelu(inner, approximate=False)


def padded_flat(members, multiple):
    flat = jnp.concatenate([member.reshape(-1) for member in members])
    total = -(-flat.shape[0] // multiple) * multiple
    return jnp.pad(flat, (0, total - flat.shape[0]))


def attend(queries, key_rows, value_rows, key_keep):
    cell_count, query_len, local_width = queries.shape
    head_count = local_width // HDIM
    block_rows = min(query_len, 512)
    block_count = query_len // block_rows
    scale = HDIM ** (-0.5)

    def one_cell(inputs):
        cell_query, cell_key, cell_value, cell_keep = inputs
        key_heads = cell_key.reshape(-1, head_count, HDIM)
        value_heads = cell_value.reshape(-1, head_count, HDIM)

        def one_block(query_block):
            scores = (
                jnp.einsum(
                    "qhd,khd->hqk", query_block, key_heads, preferred_element_type=jnp.float32
                )
                * scale
            )
            scores = jnp.where(cell_keep[None, None, :], scores, NEGATIVE)
            row_max = jnp.max(scores, axis=-1, keepdims=True)
            exp_scores = jnp.exp(scores - row_max)
            row_total = jnp.sum(exp_scores, axis=-1, keepdims=True)
            attn_probs = exp_scores / row_total
            context = jnp.einsum(
                "hqk,khd->qhd",
                attn_probs.astype(jnp.bfloat16),
                value_heads,
                preferred_element_type=jnp.float32,
            )
            return (
                context.reshape(block_rows, local_width),
                (row_max + jnp.log(row_total))[..., 0],
            )

        context, log_total = lax.map(
            one_block, cell_query.reshape(block_count, block_rows, head_count, HDIM)
        )
        return (context.reshape(query_len, local_width), log_total)

    return lax.map(one_cell, (queries, key_rows, value_rows, key_keep))


def attend_back(queries, key_rows, value_rows, key_keep, log_total, grad_context):
    cell_count, query_len, local_width = queries.shape
    head_count = local_width // HDIM
    block_rows = min(query_len, 512)
    block_count = query_len // block_rows
    scale = HDIM ** (-0.5)

    def one_cell(inputs):
        cell_query, cell_key, cell_value, cell_keep, cell_lse, cell_grad = inputs
        key_heads = cell_key.reshape(-1, head_count, HDIM)
        value_heads = cell_value.reshape(-1, head_count, HDIM)
        key_len = key_heads.shape[0]

        def one_block(running, block_in):
            query_block, lse_block, grad_block = block_in
            scores = (
                jnp.einsum(
                    "qhd,khd->hqk", query_block, key_heads, preferred_element_type=jnp.float32
                )
                * scale
            )
            scores = jnp.where(cell_keep[None, None, :], scores, NEGATIVE)
            attn_probs = jnp.exp(scores - lse_block[..., None])
            grad_probs = jnp.einsum(
                "qhd,khd->hqk", grad_block, value_heads, preferred_element_type=jnp.float32
            )
            grad_scores = (
                attn_probs * (grad_probs - jnp.sum(attn_probs * grad_probs, axis=-1, keepdims=True))
            ).astype(jnp.bfloat16)
            grad_query = (
                jnp.einsum(
                    "hqk,khd->qhd", grad_scores, key_heads, preferred_element_type=jnp.float32
                )
                * scale
            )
            grad_key = (
                running[0]
                + jnp.einsum(
                    "hqk,qhd->khd", grad_scores, query_block, preferred_element_type=jnp.float32
                )
                * scale
            )
            grad_value = running[1] + jnp.einsum(
                "hqk,qhd->khd",
                attn_probs.astype(jnp.bfloat16),
                grad_block,
                preferred_element_type=jnp.float32,
            )
            return ((grad_key, grad_value), grad_query.reshape(block_rows, local_width))

        zeros_start = jnp.zeros((key_len, head_count, HDIM), jnp.float32)
        (grad_key, grad_value), grad_query = lax.scan(
            one_block,
            (zeros_start, zeros_start),
            (
                cell_query.reshape(block_count, block_rows, head_count, HDIM),
                cell_lse,
                cell_grad.reshape(block_count, block_rows, head_count, HDIM),
            ),
        )
        return (
            grad_query.reshape(query_len, local_width),
            grad_key.reshape(key_len, local_width),
            grad_value.reshape(key_len, local_width),
        )

    return lax.map(one_cell, (queries, key_rows, value_rows, key_keep, log_total, grad_context))


def plain_on_device(
    row_gene,
    row_value,
    row_promoter,
    row_grn,
    row_coexp,
    row_family,
    lengths,
    gene_ids,
    norm1_gain,
    norm1_bias,
    qkv_weight,
    query_bias,
    value_bias,
    out_weight,
    out_bias,
    norm2_gain,
    norm2_bias,
    up_weight,
    up_bias,
    down_weight,
    down_bias,
    cotangent,
):
    cell_count, local_len, model_width = row_gene.shape
    row_count = cell_count * local_len
    seq_size = lax.axis_size("seq")
    multiple = lax.axis_size("dp") * seq_size * 128
    place = lax.axis_index("seq")
    positions = place * local_len + jnp.arange(local_len, dtype=jnp.int32)
    live_local = (positions[None, :] < lengths[:, None]).astype(jnp.int32)
    local_counts = jax.ops.segment_sum(
        live_local.reshape(-1), gene_ids.reshape(-1), num_segments=VOCAB
    )
    gene_counts = lax.psum(local_counts, ("dp", "seq"))
    summed = (
        row_gene.astype(jnp.float32)
        + row_value.astype(jnp.float32)
        + row_promoter.astype(jnp.float32)
        + row_grn.astype(jnp.float32)
        + row_coexp.astype(jnp.float32)
        + row_family.astype(jnp.float32)
    )
    summed = summed.reshape(row_count, model_width)
    normed_one, hat_one, inv_one = layer_norm(summed, norm1_gain, norm1_bias)
    normed_in = normed_one.astype(jnp.bfloat16)
    projected = jnp.dot(normed_in, qkv_weight, preferred_element_type=jnp.float32)
    query_full = projected[:, :model_width] + query_bias
    key_full = projected[:, model_width : 2 * model_width]
    value_full = projected[:, 2 * model_width :] + value_bias
    stacked = jnp.stack([query_full, key_full, value_full], axis=1).astype(jnp.bfloat16)
    stacked = stacked.reshape(cell_count, local_len, 3, model_width)
    full_len = local_len * seq_size
    key_keep = jnp.arange(full_len, dtype=jnp.int32)[None, :] < lengths[:, None]
    heads_in = lax.all_to_all(stacked, "seq", split_axis=3, concat_axis=1, tiled=True)
    query_att = heads_in[:, :, 0]
    key_att = heads_in[:, :, 1]
    value_att = heads_in[:, :, 2]
    context, log_total = attend(query_att, key_att, value_att, key_keep)
    context_local = lax.all_to_all(
        context.astype(jnp.bfloat16), "seq", split_axis=1, concat_axis=2, tiled=True
    )
    context_flat = context_local.reshape(row_count, model_width)
    hidden = (
        summed + jnp.dot(context_flat, out_weight, preferred_element_type=jnp.float32) + out_bias
    )
    normed_two, hat_two, inv_two = layer_norm(hidden, norm2_gain, norm2_bias)
    normed_mid = normed_two.astype(jnp.bfloat16)
    inner = jnp.dot(normed_mid, up_weight, preferred_element_type=jnp.float32) + up_bias
    activated, gelu_pull = jax.vjp(gelu_exact, inner)
    activated_low = activated.astype(jnp.bfloat16)
    result = (
        hidden + jnp.dot(activated_low, down_weight, preferred_element_type=jnp.float32) + down_bias
    )
    output = result.astype(jnp.bfloat16).reshape(cell_count, local_len, model_width)
    grad_out_low = cotangent.reshape(row_count, model_width)
    grad_out = grad_out_low.astype(jnp.float32)
    grad_down = jnp.einsum(
        "nf,nd->fd", activated_low, grad_out_low, preferred_element_type=jnp.float32
    )
    grad_down_bias = jnp.sum(grad_out, axis=0)
    grad_act = jnp.einsum(
        "nd,fd->nf", grad_out_low, down_weight, preferred_element_type=jnp.float32
    )
    grad_inner = gelu_pull(grad_act)[0].astype(jnp.bfloat16)
    grad_up = jnp.einsum("nd,nf->df", normed_mid, grad_inner, preferred_element_type=jnp.float32)
    grad_up_bias = jnp.sum(grad_inner.astype(jnp.float32), axis=0)
    grad_mid = jnp.einsum("nf,df->nd", grad_inner, up_weight, preferred_element_type=jnp.float32)
    grad_hid_norm, grad_gain_two, grad_bias_two = norm_back(grad_mid, hat_two, inv_two, norm2_gain)
    grad_hidden = grad_out + grad_hid_norm
    ffn_flat = padded_flat(
        (grad_gain_two, grad_bias_two, grad_up, grad_up_bias, grad_down, grad_down_bias), multiple
    )
    grad_hidden_low = grad_hidden.astype(jnp.bfloat16)
    grad_out_weight = jnp.einsum(
        "nc,nd->cd", context_flat, grad_hidden_low, preferred_element_type=jnp.float32
    )
    grad_out_bias = jnp.sum(grad_hidden_low.astype(jnp.float32), axis=0)
    grad_context = jnp.einsum(
        "nd,cd->nc", grad_hidden_low, out_weight, preferred_element_type=jnp.float32
    )
    grad_context = grad_context.astype(jnp.bfloat16).reshape(cell_count, local_len, model_width)
    grad_heads = lax.all_to_all(grad_context, "seq", split_axis=2, concat_axis=1, tiled=True)
    grad_query, grad_key, grad_value = attend_back(
        query_att, key_att, value_att, key_keep, log_total, grad_heads
    )
    grad_stack = jnp.stack([grad_query, grad_key, grad_value], axis=2).astype(jnp.bfloat16)
    grad_local = lax.all_to_all(grad_stack, "seq", split_axis=1, concat_axis=3, tiled=True)
    grad_qkv = grad_local.reshape(row_count, 3 * model_width)
    grad_qkv_weight = jnp.einsum(
        "nd,ne->de", normed_in, grad_qkv, preferred_element_type=jnp.float32
    )
    grad_query_bias = jnp.sum(grad_qkv[:, :model_width].astype(jnp.float32), axis=0)
    grad_value_bias = jnp.sum(grad_qkv[:, 2 * model_width :].astype(jnp.float32), axis=0)
    grad_normed_in = jnp.einsum(
        "ne,de->nd", grad_qkv, qkv_weight, preferred_element_type=jnp.float32
    )
    grad_sum_norm, grad_gain_one, grad_bias_one = norm_back(
        grad_normed_in, hat_one, inv_one, norm1_gain
    )
    grad_rows = (
        (grad_hidden + grad_sum_norm)
        .astype(jnp.bfloat16)
        .reshape(cell_count, local_len, model_width)
    )
    attn_flat = padded_flat(
        (
            grad_gain_one,
            grad_bias_one,
            grad_qkv_weight,
            grad_query_bias,
            grad_value_bias,
            grad_out_weight,
            grad_out_bias,
        ),
        multiple,
    )
    attn_share, ffn_share = (
        lax.psum_scatter(attn_flat, ("dp", "seq"), scatter_dimension=0, tiled=True),
        lax.psum_scatter(ffn_flat, ("dp", "seq"), scatter_dimension=0, tiled=True),
    )
    return (output, grad_rows, attn_share, ffn_share, gene_counts)


def fits(mesh):
    return dict(mesh.shape) == {"dp": 16, "seq": 2}


def solution(mesh):
    return jax.shard_map(
        on_device if fits(mesh) else plain_on_device,
        mesh=mesh,
        in_specs=(
            P("dp", "seq", None),
            P("dp", "seq", None),
            P("dp", "seq", None),
            P("dp", "seq", None),
            P("dp", "seq", None),
            P("dp", "seq", None),
            P("dp"),
            P("dp", "seq"),
            P(),
            P(),
            P(),
            P(),
            P(),
            P(),
            P(),
            P(),
            P(),
            P(),
            P(),
            P(),
            P(),
            P("dp", "seq", None),
        ),
        out_specs=(
            P("dp", "seq", None),
            P("dp", "seq", None),
            P(("dp", "seq")),
            P(("dp", "seq")),
            P(),
        ),
        check_vma=False,
    )
```
